128 devices in a mesh: dp: 32 (over x, z, core), tensor: 4 (over y).
Axes of the slice: x: 4, y: 4, z: 4, core: 2. Of those that a mesh axis runs over, the one named last changes fastest.
Arguments:
- tokens: bfloat16 [16384, 1024], P(('dp', 'tensor')), may hold values from -24 to 24
- segments: int32 [16384], P('dp'), may hold values from 0 to 3, as said below
- query_weight: bfloat16 [1024, 1024], P('dp', 'tensor'), may hold values from -0.1875 to 0.1875
- key_weight: bfloat16 [1024, 512], P('dp', 'tensor'), may hold values from -0.1875 to 0.1875
- value_weight: bfloat16 [1024, 512], P('dp', 'tensor'), may hold values from -0.1875 to 0.1875
- out_weight: bfloat16 [1024, 1024], P('tensor', 'dp'), may hold values from -1.5 to 1.5
- gate_weight: bfloat16 [1024, 4608], P('dp', 'tensor'), may hold values from -0.1875 to 0.1875
- up_weight: bfloat16 [1024, 4608], P('dp', 'tensor'), may hold values from -0.1875 to 0.1875
- down_weight: bfloat16 [4608, 1024], P('tensor', 'dp'), may hold values from -0.125 to 0.125
- attn_gain: float32 [1024], replicated, may hold values from 0.1 to 1.9
- ffn_gain: float32 [1024], replicated, may hold values from 0.1 to 1.9
- query_gain: float32 [64], replicated, may hold values from 1 to 1.6
- key_gain: float32 [64], replicated, may hold values from 1 to 1.6
- cotangent: bfloat16 [16384, 1024], P(('dp', 'tensor')), may hold values from -24 to 24
Outputs:
- result: bfloat16 [16384, 1024], P(('dp', 'tensor'))
- grad_tokens: bfloat16 [16384, 1024], P(('dp', 'tensor'))
- grad_query_weight: float32 [1024, 1024], P('dp', 'tensor')
- grad_key_weight: float32 [1024, 512], P('dp', 'tensor')
- grad_value_weight: float32 [1024, 512], P('dp', 'tensor')
- grad_out_weight: float32 [1024, 1024], P('tensor', 'dp')
- grad_gate_weight: float32 [1024, 4608], P('dp', 'tensor')
- grad_up_weight: float32 [1024, 4608], P('dp', 'tensor')
- grad_down_weight: float32 [4608, 1024], P('tensor', 'dp')
- grad_attn_gain: float32 [1024], replicated
- grad_ffn_gain: float32 [1024], replicated
- grad_query_gain: float32 [64], replicated
- grad_key_gain: float32 [64], replicated
The draws below stay inside these ranges and needn't reach their ends.
Inputs may be any that keep to these rules, and one draw needn't show every extreme that they name: `segments`: within each sequence of 512 tokens the ids start at 0 and never fall; equal ids mark one document.
All inputs are finite; a program needn't handle non-finite values.
Results may differ from the reference program's by a relative error of at most 0.025.
Values may be sent and summed in bfloat16 or wider, within the bound.
No kernel may reach another device: no remote copies, remote signals or barrier semaphores. Data moves between devices by JAX's collectives and lax.ppermute only.
A program may use at most 128 MiB of HBM per device.

```python
import math
import jax
import jax.numpy as jnp
from jax import lax

D = 1024
H = 16
KVH = 8
HD = 64
FF = 4608
LEN = 512
TOKENS = 16384
N_DP = 32


def draw_segments(key, part):
    key = jax.random.fold_in(key, 7)
    first_key, second_key, third_key = jax.random.split(key, 3)
    sequences = TOKENS // LEN
    first_cut = jax.random.randint(first_key, (sequences, 1), 1, LEN // 4)
    second_cut = jax.random.randint(second_key, (sequences, 1), 1, LEN // 4)
    last_cut = jax.random.randint(third_key, (sequences, 1), 3 * LEN // 4 + 1, LEN)
    indices = jnp.arange(LEN, dtype=jnp.int32)[None, :]
    ids = (indices >= first_cut).astype(jnp.int32) + (indices >= second_cut).astype(jnp.int32) + (indices >= last_cut).astype(jnp.int32)
    return ids.reshape(sequences * LEN)


def with_spikes(entries, rng, source, target, parts, factor):
    def block_of(position):
        return (jnp.arange(entries.shape[position]) // (entries.shape[position] // parts)).reshape((-1,) + (1,) * (entries.ndim - 1 - position))

    one_side = jax.random.permutation(rng, parts)[block_of(target)]
    second = (block_of(target) + parts // 2) % parts
    return jnp.where((block_of(source) == one_side) | (block_of(source) == second), factor * entries, entries)


def level_of(own_key, shape, cuts, low, largest):
    factor_of, own = 1.0, jax.random.fold_in(own_key, 6)
    for position, shards_of in cuts:
        steps = jnp.exp(jax.random.uniform(jax.random.fold_in(own, position), (shards_of,), jnp.float32, low / len(cuts), largest / len(cuts)))
        factor_of = factor_of * jnp.repeat(steps, shape[position] // shards_of).reshape([-1 if axis == position else 1 for axis in range(len(shape))])
    return factor_of


def centred(stream_key, extent, deviation, limit, cuts=(), kind=jnp.bfloat16):
    gain = level_of(stream_key, extent, cuts, -0.22, 0.18) if cuts else 1.0
    values = jax.random.normal(stream_key, extent, jnp.float32) * deviation * gain
    return jnp.minimum(jnp.maximum(values, -limit), limit).astype(kind)


def bell_draw_with(key, extent, deviation, most, shards, heavy, held_as=jnp.bfloat16):
    array = deviation * jax.random.normal(key, extent, jnp.float32)
    if shards:
        array = array * level_of(key, extent, shards, -0.22, 0.18)
    return jnp.clip(with_spikes(array, jax.random.fold_in(key, 3), *heavy), -most, most).astype(held_as)


def setup_inputs(seed: int = 0) -> dict:
    seeds = jax.random.split(jax.random.key(seed), 15)
    tokens = bell_draw_with(seeds[0], (TOKENS, D), 1.0, 24.0, ((0, 128),), (0, 1, 128, 5.5))
    segments = draw_segments(jax.random.fold_in(seeds[14], 71), 0)
    query_weight = centred(seeds[2], (D, H * HD), D ** -0.5, 0.1875, ((0, 32), (1, 4)))
    key_weight = centred(seeds[3], (D, KVH * HD), D ** -0.5, 0.1875, ((0, 32), (1, 4)))
    value_weight = centred(seeds[4], (D, KVH * HD), D ** -0.5, 0.1875, ((0, 32), (1, 4)))
    out_weight = centred(seeds[5], (H * HD, D), (H * HD // 64) ** -0.5, 1.5, ((0, 4), (1, 32)))
    gate_weight = centred(seeds[6], (D, FF), D ** -0.5, 0.1875, ((0, 32), (1, 4)))
    up_weight = centred(seeds[7], (D, FF), D ** -0.5, 0.1875, ((0, 32), (1, 4)))
    down_weight = centred(seeds[8], (FF, D), (FF // 2) ** -0.5, 0.125, ((0, 4), (1, 32)))
    attn_gain = jnp.clip(1.0 + 0.18 * jax.random.normal(seeds[9], (D,), jnp.float32), 0.1, 1.9)
    ffn_gain = jnp.clip(1.0 + 0.18 * jax.random.normal(seeds[10], (D,), jnp.float32), 0.1, 1.9)
    query_gain = jnp.clip(jax.random.uniform(seeds[11], (HD,), jnp.float32, 1.0, 1.6), 1.0, 1.6)
    key_gain = jnp.clip(jax.random.uniform(seeds[12], (HD,), jnp.float32, 1.0, 1.6), 1.0, 1.6)
    cotangent = bell_draw_with(seeds[13], (TOKENS, D), 1.0, 24.0, ((0, 128),), (0, 1, 128, 5.5))
    return {"tokens": tokens, "segments": segments, "query_weight": query_weight, "key_weight": key_weight, "value_weight": value_weight, "out_weight": out_weight, "gate_weight": gate_weight, "up_weight": up_weight, "down_weight": down_weight, "attn_gain": attn_gain, "ffn_gain": ffn_gain, "query_gain": query_gain, "key_gain": key_gain, "cotangent": cotangent}


@jax.custom_vjp
def low(v):
    return lax.optimization_barrier(v.astype(jnp.bfloat16)).astype(jnp.float32)

@jax.custom_vjp
def low_back(v):
    return v

def low_keep(v):
    return (low(v), None)

def low_pass(kept, grad):
    return (grad,)

def back_keep(v):
    return (v, None)

def back_low(kept, grad):
    return (low(grad),)
low.defvjp(low_keep, low_pass)
low_back.defvjp(back_keep, back_low)
epsilon = 1e-05
rope_base = 1000000.0
masked_score = -1e+30

def matmul_high(left, right):
    return jnp.dot(left, right, precision=lax.Precision.HIGHEST, preferred_element_type=jnp.float32)

def rms_norm(value, norm_gain):
    return value * lax.rsqrt(lax.optimization_barrier(jnp.mean(value * value, axis=-1, keepdims=True)) + epsilon) * norm_gain

def doc_positions(segment_ids):
    length = segment_ids.shape[0]
    indices = jnp.arange(length, dtype=jnp.int32)
    begins = jnp.concatenate([jnp.ones((1,), dtype=jnp.bool_), segment_ids[1:] != segment_ids[:-1]])
    starts = lax.cummax(jnp.where(begins, indices, jnp.zeros_like(indices)), axis=0)
    return indices - starts

def rope_tables(positions):
    half_dim = HD // 2
    exponents = jnp.arange(half_dim, dtype=jnp.float32) * (2.0 / HD)
    frequency = jnp.exp(-math.log(rope_base) * exponents)
    angles = positions.astype(jnp.float32)[:, None] * frequency[None, :]
    return (jnp.cos(angles)[:, None, :], jnp.sin(angles)[:, None, :])

def rotate(value, cosine, sine_table):
    half_dim = value.shape[-1] // 2
    first_half = value[..., :half_dim]
    second_half = value[..., half_dim:]
    return jnp.concatenate([first_half * cosine - second_half * sine_table, second_half * cosine + first_half * sine_table], axis=-1)

def block_forward(tokens_in, weights, cosine, sine_table, allowed):
    query_weight, key_weight, value_weight, out_weight, gate_weight, up_weight, down_weight, attn_gain, ffn_gain, query_gain, key_gain = weights
    length = tokens_in.shape[0]
    normed = low(rms_norm(tokens_in, attn_gain))
    query_proj = low_back(matmul_high(normed, query_weight)).reshape(length, H, HD)
    key_proj = low_back(matmul_high(normed, key_weight)).reshape(length, KVH, HD)
    value_proj = low(low_back(matmul_high(normed, value_weight))).reshape(length, KVH, HD)
    query_rot = low(rotate(rms_norm(query_proj, query_gain), cosine, sine_table))
    key_rot = low(rotate(rms_norm(key_proj, key_gain), cosine, sine_table))
    key_wide = jnp.repeat(key_rot, H // KVH, axis=1)
    value_wide = jnp.repeat(value_proj, H // KVH, axis=1)
    raw_scores = jnp.einsum('qhd,khd->hqk', query_rot, key_wide, precision=lax.Precision.HIGHEST)
    scores = low_back(raw_scores * (1.0 / math.sqrt(HD)))
    scores = jnp.where(allowed[None], scores, masked_score)
    row_max = lax.optimization_barrier(jnp.max(scores, axis=-1, keepdims=True))
    exponent = jnp.exp(scores - row_max)
    softmax = exponent / lax.optimization_barrier(jnp.sum(exponent, axis=-1, keepdims=True))
    mixed = jnp.einsum('hqk,khd->qhd', low(softmax), value_wide, precision=lax.Precision.HIGHEST).reshape(length, H * HD)
    mixed = low(low_back(mixed))
    middle = tokens_in + low_back(matmul_high(mixed, out_weight))
    ffn_in = low(rms_norm(middle, ffn_gain))
    gate_value = low_back(matmul_high(ffn_in, gate_weight))
    up_value = low_back(matmul_high(ffn_in, up_weight))
    hidden = low(jax.nn.silu(gate_value) * up_value)
    return middle + low_back(matmul_high(hidden, down_weight))

def reference(tokens, segments, query_weight, key_weight, value_weight, out_weight, gate_weight, up_weight, down_weight, attn_gain, ffn_gain, query_gain, key_gain, cotangent):
    params = (query_weight.astype(jnp.float32), key_weight.astype(jnp.float32), value_weight.astype(jnp.float32), out_weight.astype(jnp.float32), gate_weight.astype(jnp.float32), up_weight.astype(jnp.float32), down_weight.astype(jnp.float32), attn_gain.astype(jnp.float32), ffn_gain.astype(jnp.float32), query_gain.astype(jnp.float32), key_gain.astype(jnp.float32))

    def one_sequence(totals, pieces):
        seq_tokens, seq_ids, seq_grad = pieces
        cosine, sine_table = rope_tables(doc_positions(seq_ids))
        indices = jnp.arange(LEN, dtype=jnp.int32)
        allowed = (indices[:, None] >= indices[None, :]) & (seq_ids[:, None] == seq_ids[None, :])

        def forward(tokens_in, *weights):
            return block_forward(tokens_in, weights, cosine, sine_table, allowed)
        output, pullback = jax.vjp(forward, seq_tokens.astype(jnp.float32), *params)
        gradients = pullback(seq_grad.astype(jnp.float32))
        totals = tuple((carried + added for carried, added in zip(totals, gradients[1:])))
        return (totals, (output.astype(jnp.bfloat16), gradients[0].astype(jnp.bfloat16)))
    starting = tuple((jnp.zeros(param.shape, jnp.float32) for param in params))
    totals, (outputs, input_grads) = lax.scan(one_sequence, starting, (tokens.reshape(N_DP, LEN, D), segments.reshape(N_DP, LEN), cotangent.reshape(N_DP, LEN, D)))
    return (outputs.reshape(TOKENS, D), input_grads.reshape(TOKENS, D), totals[0], totals[1], totals[2], totals[3], totals[4], totals[5], totals[6], totals[7], totals[8], totals[9], totals[10])
```

```python
import math

import jax
import jax.numpy as jnp
from jax import lax
from jax.sharding import Mesh, PartitionSpec as P

HD = 64
FOUR = 4

epsilon = 1e-05
rope_base = 1000000.0
masked_score = -1e30

bf16 = jnp.bfloat16
f32 = jnp.float32


def dot_nn(left, right):
    return lax.dot_general(left, right, (((1,), (0,)), ((), ())), preferred_element_type=f32)


def dot_nt(left, right):
    return lax.dot_general(left, right, (((1,), (1,)), ((), ())), preferred_element_type=f32)


def dot_tn(left, right):
    return lax.dot_general(left, right, (((0,), (0,)), ((), ())), preferred_element_type=f32)


def inverse_rms(value):
    return lax.rsqrt(jnp.mean(value * value, axis=-1, keepdims=True) + epsilon)


def norm_back_value(value, inverse, norm_gain, incoming):
    scaled = incoming * norm_gain
    average = jnp.mean(value * scaled, axis=-1, keepdims=True)
    return inverse * scaled - value * (inverse * inverse * inverse) * average


def doc_positions(segment_ids):
    length = segment_ids.shape[0]
    indices = jnp.arange(length, dtype=jnp.int32)
    begins = jnp.concatenate([jnp.ones((1,), dtype=jnp.bool_), segment_ids[1:] != segment_ids[:-1]])
    starts = lax.cummax(jnp.where(begins, indices, jnp.zeros_like(indices)), axis=0)
    return indices - starts


def rope_tables(positions):
    half_dim = HD // 2
    exponents = jnp.arange(half_dim, dtype=f32) * (2.0 / HD)
    frequency = jnp.exp(-math.log(rope_base) * exponents)
    angles = positions.astype(f32)[:, None] * frequency[None, :]
    return (jnp.cos(angles)[:, None, :], jnp.sin(angles)[:, None, :])


def rotate(value, cosine, sine_table):
    half_dim = value.shape[-1] // 2
    first_half = value[..., :half_dim]
    second_half = value[..., half_dim:]
    return jnp.concatenate(
        [
            first_half * cosine - second_half * sine_table,
            second_half * cosine + first_half * sine_table,
        ],
        axis=-1,
    )


def unrotate(grad, cosine, sine_table):
    return rotate(grad, cosine, -sine_table)


def shift(value, axis, distance, size=FOUR):
    return lax.ppermute(value, axis, [(i, (i + distance) % size) for i in range(size)])


def gather_y(block):
    return [block] + [shift(block, "y", -j) for j in (1, 2, 3)]


def scatter_sum_y(blocks):
    total = blocks[0].astype(f32)
    for arrived in [shift(blocks[j].astype(bf16), "y", j) for j in (1, 2, 3)]:
        total = total + arrived.astype(f32)
    return total


def scatter_sum_axis(pieces, axis):
    me = lax.axis_index(axis)
    arrived = [
        shift(lax.dynamic_index_in_dim(pieces, (me + j) % FOUR, 0, keepdims=False), axis, j)
        for j in (1, 2, 3)
    ]
    total = lax.dynamic_index_in_dim(pieces, me, 0, keepdims=False).astype(f32)
    for part in arrived:
        total = total + part.astype(f32)
    return total


def scatter_sum_dp(grads, cut):
    columns = grads.shape[1]
    me = lax.axis_index("c")
    rows = grads.reshape(16, 2, -1, columns)
    theirs = lax.dynamic_index_in_dim(rows, 1 - me, 1, keepdims=False)
    mine = lax.dynamic_index_in_dim(rows, me, 1, keepdims=False)
    arrived = shift(theirs, "c", 1, 2)
    both = (mine.astype(f32) + arrived.astype(f32)).astype(bf16)
    both = both.reshape(FOUR, FOUR, -1, columns)
    left = both[..., :cut]
    right = jnp.swapaxes(both[..., cut:], 0, 1)
    left = scatter_sum_axis(left, "x").astype(bf16)
    right = scatter_sum_axis(right, "z").astype(bf16)
    left = scatter_sum_axis(left, "z")
    right = scatter_sum_axis(right, "x")
    return left, right


def sum_all(value):
    for axis, size in (("y", 4), ("c", 2), ("x", 4), ("z", 4)):
        total = value
        for arrived in [shift(value, axis, j, size) for j in range(1, size)]:
            total = total + arrived
        value = total
    return value


def roll_blocks(value, amount):
    cut = (FOUR - amount) * (value.shape[0] // FOUR)
    return jnp.concatenate([value[cut:], value[:cut]], axis=0)


def local(
    tokens,
    segments,
    query_weight,
    key_weight,
    value_weight,
    out_weight,
    gate_weight,
    up_weight,
    down_weight,
    attn_gain,
    ffn_gain,
    query_gain,
    key_gain,
    cotangent,
):
    dp = ("x", "z", "c")
    length = segments.shape[0]
    block = length // FOUR
    query_cols = query_weight.shape[1]
    kv_cols = key_weight.shape[1]
    ff_cols = gate_weight.shape[1]
    query_heads = query_cols // HD
    value_heads = kv_cols // HD
    group_size = query_heads // value_heads
    score_scale = 1.0 / math.sqrt(HD)
    y = lax.axis_index("y")

    attn_shard = jnp.concatenate([query_weight, key_weight, value_weight, out_weight.T], axis=1)
    attn_full = lax.all_gather(attn_shard, dp, axis=0, tiled=True)
    ffn_shard = jnp.concatenate([gate_weight, up_weight, down_weight.T], axis=1)
    ffn_full = lax.all_gather(ffn_shard, dp, axis=0, tiled=True)
    qkv_cols = query_cols + 2 * kv_cols
    full_qkv = attn_full[:, :qkv_cols]
    full_out_t = attn_full[:, qkv_cols:]
    full_gate_up = ffn_full[:, : 2 * ff_cols]
    full_down_t = ffn_full[:, 2 * ff_cols :]

    tokens_all = jnp.concatenate(gather_y(tokens), axis=0)
    out_all_t = jnp.concatenate(gather_y(full_out_t), axis=1)
    grad_out_all = jnp.concatenate(gather_y(cotangent), axis=0)

    indices = jnp.roll(jnp.arange(length, dtype=jnp.int32), -block * y)
    ids = jnp.roll(segments, -block * y)
    positions = jnp.roll(doc_positions(segments), -block * y)
    cosine, sine_table = rope_tables(positions)
    allowed = (indices[:, None] >= indices[None, :]) & (ids[:, None] == ids[None, :])

    residual = tokens_all.astype(f32)
    attn_inv = inverse_rms(residual)
    normed = (residual * attn_inv * attn_gain).astype(bf16)
    projected = dot_nn(normed, full_qkv)
    query_proj = projected[:, :query_cols].reshape(length, query_heads, HD)
    key_proj = projected[:, query_cols : query_cols + kv_cols].reshape(length, value_heads, HD)
    value_proj = projected[:, query_cols + kv_cols :].astype(bf16).reshape(length, value_heads, HD)
    query_inv = inverse_rms(query_proj)
    key_inv = inverse_rms(key_proj)
    query_rot = (
        rotate(query_proj * query_inv * query_gain, cosine, sine_table)
        .astype(bf16)
        .reshape(length, value_heads, group_size, HD)
    )
    key_rot = rotate(key_proj * key_inv * key_gain, cosine, sine_table).astype(bf16)
    scores = (
        jnp.einsum("qgjd,kgd->gjqk", query_rot, key_rot, preferred_element_type=f32) * score_scale
    )
    scores = jnp.where(allowed, scores, masked_score)
    row_max = jnp.max(scores, axis=-1, keepdims=True)
    exponent = jnp.exp(scores - row_max)
    row_total = jnp.sum(exponent, axis=-1, keepdims=True)
    softmax_full = exponent / row_total
    softmax_low = softmax_full.astype(bf16)
    mixed = (
        jnp.einsum("gjqk,kgd->qgjd", softmax_low, value_proj, preferred_element_type=f32)
        .reshape(length, query_cols)
        .astype(bf16)
    )
    mixed_all = jnp.concatenate(
        [roll_blocks(part, j) if j else part for j, part in enumerate(gather_y(mixed))], axis=1
    )
    middle_all = residual + dot_nt(mixed_all, out_all_t)
    ffn_inv_all = inverse_rms(middle_all)
    ffn_all = (middle_all * ffn_inv_all * ffn_gain).astype(bf16)
    middle = middle_all[:block]
    ffn_inv = ffn_inv_all[:block]

    gate_value = dot_nn(ffn_all, full_gate_up[:, :ff_cols])
    up_value = dot_nn(ffn_all, full_gate_up[:, ff_cols:])
    grad_hidden = dot_nn(grad_out_all, full_down_t)
    sigmoid_gate = jax.nn.sigmoid(gate_value)
    silu_gate = gate_value * sigmoid_gate
    hidden = (silu_gate * up_value).astype(bf16)
    grad_gate = (
        grad_hidden * up_value * sigmoid_gate * (1.0 + gate_value * (1.0 - sigmoid_gate))
    ).astype(bf16)
    grad_up = (grad_hidden * silu_gate).astype(bf16)
    grad_gate_up = jnp.concatenate([grad_gate, grad_up], axis=1)

    ffn_back = dot_nt(grad_gate_up, full_gate_up).astype(bf16)
    grad_ffn_in = scatter_sum_y([ffn_back[j * block : (j + 1) * block] for j in range(FOUR)])
    ffn_out = dot_nt(hidden, full_down_t).astype(bf16)
    result = (
        middle + scatter_sum_y([ffn_out[j * block : (j + 1) * block] for j in range(FOUR)])
    ).astype(bf16)

    grad_through = norm_back_value(middle, ffn_inv, ffn_gain, grad_ffn_in)
    ffn_gain_part = jnp.sum(grad_ffn_in * middle * ffn_inv, axis=0)
    grad_middle = cotangent.astype(f32) + grad_through
    grad_middle_all = jnp.concatenate(gather_y(grad_middle.astype(bf16)), axis=0)

    gate_up_part = dot_tn(ffn_all, grad_gate_up).astype(bf16)
    down_part = dot_tn(grad_out_all, hidden).astype(bf16)
    ffn_grads = jnp.concatenate([gate_up_part, down_part], axis=1)
    ffn_left, ffn_right = scatter_sum_dp(ffn_grads, (3 * ff_cols // 256) * 128)
    ffn_rows = jnp.concatenate([ffn_left, ffn_right], axis=1)
    grad_gate_weight = ffn_rows[:, :ff_cols]
    grad_up_weight = ffn_rows[:, ff_cols : 2 * ff_cols]
    grad_down_weight = ffn_rows[:, 2 * ff_cols :].T

    out_part = dot_tn(grad_middle_all, mixed).astype(bf16)
    grad_mix = (
        dot_nn(grad_middle_all, full_out_t)
        .astype(bf16)
        .reshape(length, value_heads, group_size, HD)
    )
    grad_probs = jnp.einsum("qgjd,kgd->gjqk", grad_mix, value_proj, preferred_element_type=f32)
    row_delta = jnp.sum(softmax_full * grad_probs, axis=-1, keepdims=True)
    grad_scores = (softmax_full * (grad_probs - row_delta)).astype(bf16)
    grad_query_rot = (
        jnp.einsum("gjqk,kgd->qgjd", grad_scores, key_rot, preferred_element_type=f32)
        * score_scale
    ).reshape(length, query_heads, HD)
    grad_key_rot = (
        jnp.einsum("gjqk,qgjd->kgd", grad_scores, query_rot, preferred_element_type=f32)
        * score_scale
    )
    grad_values = jnp.einsum("gjqk,qgjd->kgd", softmax_low, grad_mix, preferred_element_type=f32)
    grad_query_normed = unrotate(grad_query_rot, cosine, sine_table)
    grad_key_normed = unrotate(grad_key_rot, cosine, sine_table)
    grad_query_proj = norm_back_value(query_proj, query_inv, query_gain, grad_query_normed)
    grad_key_proj = norm_back_value(key_proj, key_inv, key_gain, grad_key_normed)
    query_gain_part = jnp.sum(grad_query_normed * query_proj * query_inv, axis=(0, 1))
    key_gain_part = jnp.sum(grad_key_normed * key_proj * key_inv, axis=(0, 1))
    grad_qkv = jnp.concatenate(
        [
            grad_query_proj.reshape(length, query_cols).astype(bf16),
            grad_key_proj.reshape(length, kv_cols).astype(bf16),
            grad_values.reshape(length, kv_cols).astype(bf16),
        ],
        axis=1,
    )
    attn_back = dot_nt(grad_qkv, full_qkv)
    attn_gain_part = jnp.sum(attn_back * residual * attn_inv, axis=0)
    attn_back = attn_back.astype(bf16)
    grad_normed = scatter_sum_y([attn_back[j * block : (j + 1) * block] for j in range(FOUR)])
    grad_input = norm_back_value(residual[:block], attn_inv[:block], attn_gain, grad_normed)
    grad_tokens = (grad_middle + grad_input).astype(bf16)

    qkv_part = dot_tn(normed, grad_qkv).astype(bf16)
    attn_grads = jnp.concatenate([qkv_part, out_part], axis=1)
    attn_left, attn_right = scatter_sum_dp(attn_grads, 384)
    attn_rows = jnp.concatenate([attn_left, attn_right], axis=1)
    grad_query_weight = attn_rows[:, :query_cols]
    grad_key_weight = attn_rows[:, query_cols : query_cols + kv_cols]
    grad_value_weight = attn_rows[:, query_cols + kv_cols : qkv_cols]
    grad_out_weight = attn_rows[:, qkv_cols:].T

    width = attn_gain.shape[0]
    gains = sum_all(
        jnp.concatenate([attn_gain_part, ffn_gain_part, query_gain_part, key_gain_part]).reshape(
            -1, 128
        )
    ).reshape(-1)
    return (
        result,
        grad_tokens,
        grad_query_weight,
        grad_key_weight,
        grad_value_weight,
        grad_out_weight,
        grad_gate_weight,
        grad_up_weight,
        grad_down_weight,
        gains[:width],
        gains[width : 2 * width],
        gains[2 * width : 2 * width + HD],
        gains[2 * width + HD :],
    )


def solution(mesh):
    axes = Mesh(mesh.devices.reshape(4, 4, 2, 4), ("x", "z", "c", "y"))
    dp = ("x", "z", "c")
    rows = P(("x", "z", "c", "y"), None)
    placed = (
        rows,
        P(dp),
        P(dp, "y"),
        P(dp, "y"),
        P(dp, "y"),
        P("y", dp),
        P(dp, "y"),
        P(dp, "y"),
        P("y", dp),
        P(),
        P(),
        P(),
        P(),
        rows,
    )
    return jax.shard_map(
        local,
        mesh=axes,
        in_specs=placed,
        out_specs=(
            rows,
            rows,
            P(dp, "y"),
            P(dp, "y"),
            P(dp, "y"),
            P("y", dp),
            P(dp, "y"),
            P(dp, "y"),
            P("y", dp),
            P(),
            P(),
            P(),
            P(),
        ),
        check_vma=False,
    )
```

```python
import math

import jax
import jax.numpy as jnp
from jax import lax
from jax.experimental import pallas as pl
from jax.experimental.pallas import tpu as pltpu
from jax.sharding import Mesh, PartitionSpec as P

HD = 64
FOUR = 4

epsilon = 1e-05
rope_base = 1000000.0
masked_score = -1e30

bf16 = jnp.bfloat16
f32 = jnp.float32


def dot_nn(left, right):
    return lax.dot_general(left, right, (((1,), (0,)), ((), ())), preferred_element_type=f32)


def dot_nt(left, right):
    return lax.dot_general(left, right, (((1,), (1,)), ((), ())), preferred_element_type=f32)


def dot_tn(left, right):
    return lax.dot_general(left, right, (((0,), (0,)), ((), ())), preferred_element_type=f32)


def inverse_rms(value):
    return lax.rsqrt(jnp.mean(value * value, axis=-1, keepdims=True) + epsilon)


def norm_back_value(value, inverse, norm_gain, incoming):
    scaled = incoming * norm_gain
    average = jnp.mean(value * scaled, axis=-1, keepdims=True)
    return inverse * scaled - value * (inverse * inverse * inverse) * average


def doc_positions(segment_ids):
    length = segment_ids.shape[0]
    indices = jnp.arange(length, dtype=jnp.int32)
    begins = jnp.concatenate([jnp.ones((1,), dtype=jnp.bool_), segment_ids[1:] != segment_ids[:-1]])
    starts = lax.cummax(jnp.where(begins, indices, jnp.zeros_like(indices)), axis=0)
    return indices - starts


def rope_tables(positions):
    half_dim = HD // 2
    exponents = jnp.arange(half_dim, dtype=f32) * (2.0 / HD)
    frequency = jnp.exp(-math.log(rope_base) * exponents)
    angles = positions.astype(f32)[:, None] * frequency[None, :]
    return (jnp.cos(angles)[:, None, :], jnp.sin(angles)[:, None, :])


def rotate(value, cosine, sine_table):
    half_dim = value.shape[-1] // 2
    first_half = value[..., :half_dim]
    second_half = value[..., half_dim:]
    return jnp.concatenate(
        [
            first_half * cosine - second_half * sine_table,
            second_half * cosine + first_half * sine_table,
        ],
        axis=-1,
    )


def unrotate(grad, cosine, sine_table):
    return rotate(grad, cosine, -sine_table)


def shift(value, axis, distance, size=FOUR):
    return lax.ppermute(value, axis, [(i, (i + distance) % size) for i in range(size)])


def gather_y(block):
    return [block] + [shift(block, "y", -j) for j in (1, 2, 3)]


def scatter_sum_y(blocks):
    total = blocks[0].astype(f32)
    for arrived in [shift(blocks[j].astype(bf16), "y", j) for j in (1, 2, 3)]:
        total = total + arrived.astype(f32)
    return total


def scatter_sum_axis(pieces, axis):
    me = lax.axis_index(axis)
    arrived = [
        shift(lax.dynamic_index_in_dim(pieces, (me + j) % FOUR, 0, keepdims=False), axis, j)
        for j in (1, 2, 3)
    ]
    total = lax.dynamic_index_in_dim(pieces, me, 0, keepdims=False).astype(f32)
    for part in arrived:
        total = total + part.astype(f32)
    return total


def mod4(value):
    return lax.rem(value + FOUR, FOUR)


def ordered_kernel(place_ref, own_ref, other_ref, out_ref):
    x, z, core = place_ref[0], place_ref[1], place_ref[2]
    for i in range(FOUR):
        for k in range(FOUR):
            from_x, from_z = mod4(i - x), mod4(k - z)
            out_ref[i, k, core] = own_ref[from_z, from_x]
            out_ref[i, k, 1 - core] = other_ref[from_z, from_x]


def gather_dp(shard):
    rows, columns = shard.shape
    along_x = jnp.stack([shard] + [shift(shard, "x", -j) for j in (1, 2, 3)])
    along_z = jnp.stack([along_x] + [shift(along_x, "z", -j) for j in (1, 2, 3)])
    other = shift(along_z, "c", 1, 2)
    place = jnp.stack([lax.axis_index(axis) for axis in ("x", "z", "c")]).astype(jnp.int32)
    whole = pl.pallas_call(
        ordered_kernel,
        out_shape=jax.ShapeDtypeStruct((FOUR, FOUR, 2, rows, columns), shard.dtype),
        in_specs=[
            pl.BlockSpec(memory_space=pltpu.SMEM),
            pl.BlockSpec(memory_space=pltpu.VMEM),
            pl.BlockSpec(memory_space=pltpu.VMEM),
        ],
        out_specs=pl.BlockSpec(memory_space=pltpu.VMEM),
        compiler_params=pltpu.CompilerParams(vmem_limit_bytes=16 * 1024 * 1024),
        name="order_weights",
    )(place, along_z, other)
    return whole.reshape(32 * rows, columns)


def scatter_sum_dp_large(grads):
    columns = grads.shape[1]
    part = lax.psum_scatter(grads, ("x", "c"), scatter_dimension=0, tiled=True)
    return scatter_sum_axis(part.reshape(FOUR, -1, columns), "z")


def scatter_sum_dp_small(grads, gains):
    columns = grads.shape[1]
    count = gains.shape[0]
    extra_rows = 16

    def coded(value):
        high = lax.reduce_precision(value, 8, 7)
        both = jnp.concatenate([high.astype(bf16), (value - high).astype(bf16)])
        return jnp.pad(both, (0, extra_rows * columns - 2 * count)).reshape(extra_rows, columns)

    def decoded(rows):
        flat = rows.reshape(-1)
        return flat[:count].astype(f32) + flat[count : 2 * count].astype(f32)

    def exchange(pieces, own, axis, size, gains):
        extra = coded(gains)
        total = own.astype(f32)
        rows = own.shape[0]
        arrived = [
            shift(jnp.concatenate([piece, extra], axis=0), axis, j + 1, size)
            for j, piece in enumerate(pieces)
        ]
        for part in arrived:
            total = total + part[:rows].astype(f32)
            gains = gains + decoded(part[rows:])
        return total, gains

    me = lax.axis_index("c")
    rows = grads.reshape(16, 2, -1, columns)
    take = lambda i: lax.dynamic_index_in_dim(rows, i, 1, keepdims=False).reshape(-1, columns)
    total, gains = exchange([take(1 - me)], take(me), "c", 2, gains)
    for axis in ("x", "z"):
        me = lax.axis_index(axis)
        pieces = total.astype(bf16).reshape(FOUR, -1, columns)
        take = lambda i: lax.dynamic_index_in_dim(pieces, i, 0, keepdims=False)
        total, gains = exchange(
            [take((me + j) % FOUR) for j in (1, 2, 3)], take(me), axis, FOUR, gains
        )
    return total, gains


def roll_blocks(value, amount):
    cut = (FOUR - amount) * (value.shape[0] // FOUR)
    return jnp.concatenate([value[cut:], value[:cut]], axis=0)


def local(
    tokens,
    segments,
    query_weight,
    key_weight,
    value_weight,
    out_weight,
    gate_weight,
    up_weight,
    down_weight,
    attn_gain,
    ffn_gain,
    query_gain,
    key_gain,
    cotangent,
):
    dp = ("x", "z", "c")
    length = segments.shape[0]
    block = length // FOUR
    query_cols = query_weight.shape[1]
    kv_cols = key_weight.shape[1]
    ff_cols = gate_weight.shape[1]
    query_heads = query_cols // HD
    value_heads = kv_cols // HD
    group_size = query_heads // value_heads
    score_scale = 1.0 / math.sqrt(HD)
    y = lax.axis_index("y")

    full_qkv = gather_dp(jnp.concatenate([query_weight, key_weight, value_weight], axis=1))
    qkv_cols = query_cols + 2 * kv_cols
    out_shards = gather_y(out_weight.T)
    large_shard = jnp.concatenate([gate_weight, up_weight, down_weight.T] + out_shards, axis=1)
    large_full = lax.all_gather(large_shard, dp, axis=0, tiled=True)
    full_gate_up = large_full[:, : 2 * ff_cols]
    full_down_t = large_full[:, 2 * ff_cols : 3 * ff_cols]
    out_all_t = large_full[:, 3 * ff_cols :]
    full_out_t = out_all_t[:, :query_cols]

    tokens_all = jnp.concatenate(gather_y(tokens), axis=0)
    grad_out_all = jnp.concatenate(gather_y(cotangent), axis=0)

    indices = jnp.roll(jnp.arange(length, dtype=jnp.int32), -block * y)
    ids = jnp.roll(segments, -block * y)
    positions = jnp.roll(doc_positions(segments), -block * y)
    cosine, sine_table = rope_tables(positions)
    allowed = (indices[:, None] >= indices[None, :]) & (ids[:, None] == ids[None, :])

    residual = tokens_all.astype(f32)
    attn_inv = inverse_rms(residual)
    normed = (residual * attn_inv * attn_gain).astype(bf16)
    projected = dot_nn(normed, full_qkv)
    query_proj = projected[:, :query_cols].reshape(length, query_heads, HD)
    key_proj = projected[:, query_cols : query_cols + kv_cols].reshape(length, value_heads, HD)
    value_proj = projected[:, query_cols + kv_cols :].astype(bf16).reshape(length, value_heads, HD)
    query_inv = inverse_rms(query_proj)
    key_inv = inverse_rms(key_proj)
    query_rot = (
        rotate(query_proj * query_inv * query_gain, cosine, sine_table)
        .astype(bf16)
        .reshape(length, value_heads, group_size, HD)
    )
    key_rot = rotate(key_proj * key_inv * key_gain, cosine, sine_table).astype(bf16)
    scores = (
        jnp.einsum("qgjd,kgd->gjqk", query_rot, key_rot, preferred_element_type=f32) * score_scale
    )
    scores = jnp.where(allowed, scores, masked_score)
    row_max = jnp.max(scores, axis=-1, keepdims=True)
    exponent = jnp.exp(scores - row_max)
    row_total = jnp.sum(exponent, axis=-1, keepdims=True)
    softmax_full = exponent / row_total
    softmax_low = softmax_full.astype(bf16)
    mixed = (
        jnp.einsum("gjqk,kgd->qgjd", softmax_low, value_proj, preferred_element_type=f32)
        .reshape(length, query_cols)
        .astype(bf16)
    )
    mixed_all = jnp.concatenate(
        [roll_blocks(part, j) if j else part for j, part in enumerate(gather_y(mixed))], axis=1
    )
    middle_all = residual + dot_nt(mixed_all, out_all_t)
    ffn_inv_all = inverse_rms(middle_all)
    ffn_all = (middle_all * ffn_inv_all * ffn_gain).astype(bf16)
    middle = middle_all[:block]
    ffn_inv = ffn_inv_all[:block]

    gate_value = dot_nn(ffn_all, full_gate_up[:, :ff_cols])
    up_value = dot_nn(ffn_all, full_gate_up[:, ff_cols:])
    grad_hidden = dot_nn(grad_out_all, full_down_t)
    sigmoid_gate = jax.nn.sigmoid(gate_value)
    silu_gate = gate_value * sigmoid_gate
    hidden = (silu_gate * up_value).astype(bf16)
    grad_gate = (
        grad_hidden * up_value * sigmoid_gate * (1.0 + gate_value * (1.0 - sigmoid_gate))
    ).astype(bf16)
    grad_up = (grad_hidden * silu_gate).astype(bf16)
    grad_gate_up = jnp.concatenate([grad_gate, grad_up], axis=1)

    ffn_back = dot_nt(grad_gate_up, full_gate_up).astype(bf16)
    grad_ffn_in = scatter_sum_y([ffn_back[j * block : (j + 1) * block] for j in range(FOUR)])
    ffn_out = dot_nt(hidden, full_down_t).astype(bf16)
    result = (
        middle + scatter_sum_y([ffn_out[j * block : (j + 1) * block] for j in range(FOUR)])
    ).astype(bf16)

    grad_through = norm_back_value(middle, ffn_inv, ffn_gain, grad_ffn_in)
    ffn_gain_part = jnp.sum(grad_ffn_in * middle * ffn_inv, axis=0)
    grad_middle = cotangent.astype(f32) + grad_through
    grad_middle_all = jnp.concatenate(gather_y(grad_middle.astype(bf16)), axis=0)

    def core_first(value):
        return jnp.swapaxes(value.reshape(length, 4, 4, 2, -1), 2, 3).reshape(length, -1)

    gate_up_part = dot_tn(core_first(ffn_all), grad_gate_up).astype(bf16)
    down_part = dot_tn(core_first(grad_out_all), hidden).astype(bf16)
    ffn_rows = scatter_sum_dp_large(jnp.concatenate([gate_up_part, down_part], axis=1))
    grad_gate_weight = ffn_rows[:, :ff_cols]
    grad_up_weight = ffn_rows[:, ff_cols : 2 * ff_cols]
    grad_down_weight = ffn_rows[:, 2 * ff_cols :].T

    out_part = dot_tn(grad_middle_all, mixed).astype(bf16)
    grad_mix = (
        dot_nn(grad_middle_all, full_out_t)
        .astype(bf16)
        .reshape(length, value_heads, group_size, HD)
    )
    grad_probs = jnp.einsum("qgjd,kgd->gjqk", grad_mix, value_proj, preferred_element_type=f32)
    row_delta = jnp.sum(softmax_full * grad_probs, axis=-1, keepdims=True)
    grad_scores = (softmax_full * (grad_probs - row_delta)).astype(bf16)
    grad_query_rot = (
        jnp.einsum("gjqk,kgd->qgjd", grad_scores, key_rot, preferred_element_type=f32)
        * score_scale
    ).reshape(length, query_heads, HD)
    grad_key_rot = (
        jnp.einsum("gjqk,qgjd->kgd", grad_scores, query_rot, preferred_element_type=f32)
        * score_scale
    )
    grad_values = jnp.einsum("gjqk,qgjd->kgd", softmax_low, grad_mix, preferred_element_type=f32)
    grad_query_normed = unrotate(grad_query_rot, cosine, sine_table)
    grad_key_normed = unrotate(grad_key_rot, cosine, sine_table)
    grad_query_proj = norm_back_value(query_proj, query_inv, query_gain, grad_query_normed)
    grad_key_proj = norm_back_value(key_proj, key_inv, key_gain, grad_key_normed)
    query_gain_part = jnp.sum(grad_query_normed * query_proj * query_inv, axis=(0, 1))
    key_gain_part = jnp.sum(grad_key_normed * key_proj * key_inv, axis=(0, 1))
    grad_qkv = jnp.concatenate(
        [
            grad_query_proj.reshape(length, query_cols).astype(bf16),
            grad_key_proj.reshape(length, kv_cols).astype(bf16),
            grad_values.reshape(length, kv_cols).astype(bf16),
        ],
        axis=1,
    )
    attn_back = dot_nt(grad_qkv, full_qkv)
    attn_gain_part = jnp.sum(attn_back * residual * attn_inv, axis=0)
    attn_back = attn_back.astype(bf16)
    grad_normed = scatter_sum_y([attn_back[j * block : (j + 1) * block] for j in range(FOUR)])
    grad_input = norm_back_value(residual[:block], attn_inv[:block], attn_gain, grad_normed)
    grad_tokens = (grad_middle + grad_input).astype(bf16)

    qkv_part = dot_tn(normed, grad_qkv).astype(bf16)
    attn_grads = jnp.concatenate([qkv_part, out_part], axis=1)
    gains = jnp.concatenate([attn_gain_part, ffn_gain_part, query_gain_part, key_gain_part])
    gains = sum(gather_y(gains.reshape(-1, 128))).reshape(-1)
    attn_rows, gains = scatter_sum_dp_small(attn_grads, gains)
    grad_query_weight = attn_rows[:, :query_cols]
    grad_key_weight = attn_rows[:, query_cols : query_cols + kv_cols]
    grad_value_weight = attn_rows[:, query_cols + kv_cols : qkv_cols]
    grad_out_weight = attn_rows[:, qkv_cols:].T
    width = attn_gain.shape[0]
    return (
        result,
        grad_tokens,
        grad_query_weight,
        grad_key_weight,
        grad_value_weight,
        grad_out_weight,
        grad_gate_weight,
        grad_up_weight,
        grad_down_weight,
        gains[:width],
        gains[width : 2 * width],
        gains[2 * width : 2 * width + HD],
        gains[2 * width + HD :],
    )


def solution(mesh):
    axes = Mesh(mesh.devices.reshape(4, 4, 2, 4), ("x", "z", "c", "y"))
    dp = ("x", "z", "c")
    rows = P(("x", "z", "c", "y"), None)
    placed = (
        rows,
        P(dp),
        P(dp, "y"),
        P(dp, "y"),
        P(dp, "y"),
        P("y", dp),
        P(dp, "y"),
        P(dp, "y"),
        P("y", dp),
        P(),
        P(),
        P(),
        P(),
        rows,
    )
    return jax.shard_map(
        local,
        mesh=axes,
        in_specs=placed,
        out_specs=(
            rows,
            rows,
            P(dp, "y"),
            P(dp, "y"),
            P(dp, "y"),
            P("y", dp),
            P(dp, "y"),
            P(dp, "y"),
            P("y", dp),
            P(),
            P(),
            P(),
            P(),
        ),
        check_vma=False,
    )
```

```python
import math

import jax
import jax.numpy as jnp
from jax import lax
from jax.experimental import pallas as pl
from jax.experimental.pallas import tpu as pltpu
from jax.sharding import Mesh, PartitionSpec as P

HD = 64
FOUR = 4

epsilon = 1e-05
rope_base = 1000000.0
masked_score = -1e30

bf16 = jnp.bfloat16
f32 = jnp.float32


def dot_nn(left, right):
    return lax.dot_general(left, right, (((1,), (0,)), ((), ())), preferred_element_type=f32)


def dot_nt(left, right):
    return lax.dot_general(left, right, (((1,), (1,)), ((), ())), preferred_element_type=f32)


def dot_tn(left, right):
    return lax.dot_general(left, right, (((0,), (0,)), ((), ())), preferred_element_type=f32)


def inverse_rms(value):
    return lax.rsqrt(jnp.mean(value * value, axis=-1, keepdims=True) + epsilon)


def norm_back_value(value, inverse, norm_gain, incoming):
    scaled = incoming * norm_gain
    average = jnp.mean(value * scaled, axis=-1, keepdims=True)
    return inverse * scaled - value * (inverse * inverse * inverse) * average


def doc_positions(segment_ids):
    length = segment_ids.shape[0]
    indices = jnp.arange(length, dtype=jnp.int32)
    begins = jnp.concatenate([jnp.ones((1,), dtype=jnp.bool_), segment_ids[1:] != segment_ids[:-1]])
    starts = lax.cummax(jnp.where(begins, indices, jnp.zeros_like(indices)), axis=0)
    return indices - starts


def rope_tables(positions):
    half_dim = HD // 2
    exponents = jnp.arange(half_dim, dtype=f32) * (2.0 / HD)
    frequency = jnp.exp(-math.log(rope_base) * exponents)
    angles = positions.astype(f32)[:, None] * frequency[None, :]
    return (jnp.cos(angles)[:, None, :], jnp.sin(angles)[:, None, :])


def rotate(value, cosine, sine_table):
    half_dim = value.shape[-1] // 2
    first_half = value[..., :half_dim]
    second_half = value[..., half_dim:]
    return jnp.concatenate(
        [
            first_half * cosine - second_half * sine_table,
            second_half * cosine + first_half * sine_table,
        ],
        axis=-1,
    )


def unrotate(grad, cosine, sine_table):
    return rotate(grad, cosine, -sine_table)


def shift(value, axis, distance, size=FOUR):
    return lax.ppermute(value, axis, [(i, (i + distance) % size) for i in range(size)])


def gather_y(block):
    return [block] + [shift(block, "y", -j) for j in (1, 2, 3)]


def scatter_sum_y(blocks):
    total = blocks[0].astype(f32)
    for arrived in [shift(blocks[j].astype(bf16), "y", j) for j in (1, 2, 3)]:
        total = total + arrived.astype(f32)
    return total


def scatter_sum_axis(pieces, axis):
    me = lax.axis_index(axis)
    arrived = [
        shift(lax.dynamic_index_in_dim(pieces, (me + j) % FOUR, 0, keepdims=False), axis, j)
        for j in (1, 2, 3)
    ]
    total = lax.dynamic_index_in_dim(pieces, me, 0, keepdims=False).astype(f32)
    for part in arrived:
        total = total + part.astype(f32)
    return total


def mod4(value):
    return lax.rem(value + FOUR, FOUR)


def ordered_kernel(place_ref, own_ref, other_ref, out_ref):
    x, z, core = place_ref[0], place_ref[1], place_ref[2]
    for i in range(FOUR):
        for k in range(FOUR):
            from_x, from_z = mod4(i - x), mod4(k - z)
            out_ref[i, k, core] = own_ref[from_z, from_x]
            out_ref[i, k, 1 - core] = other_ref[from_z, from_x]


def gather_dp(shard):
    rows, columns = shard.shape
    along_x = jnp.stack([shard] + [shift(shard, "x", -j) for j in (1, 2, 3)])
    along_z = jnp.stack([along_x] + [shift(along_x, "z", -j) for j in (1, 2, 3)])
    other = shift(along_z, "c", 1, 2)
    place = jnp.stack([lax.axis_index(axis) for axis in ("x", "z", "c")]).astype(jnp.int32)
    whole = pl.pallas_call(
        ordered_kernel,
        out_shape=jax.ShapeDtypeStruct((FOUR, FOUR, 2, rows, columns), shard.dtype),
        in_specs=[
            pl.BlockSpec(memory_space=pltpu.SMEM),
            pl.BlockSpec(memory_space=pltpu.VMEM),
            pl.BlockSpec(memory_space=pltpu.VMEM),
        ],
        out_specs=pl.BlockSpec(memory_space=pltpu.VMEM),
        compiler_params=pltpu.CompilerParams(vmem_limit_bytes=16 * 1024 * 1024),
        name="order_weights",
    )(place, along_z, other)
    return whole.reshape(32 * rows, columns)


def scatter_sum_dp_large(grads):
    part = lax.psum_scatter(grads, ("x", "c"), scatter_dimension=0, tiled=True)
    return lax.psum_scatter(part, "z", scatter_dimension=0, tiled=True).astype(f32)


def scatter_sum_dp_small(grads, gains):
    columns = grads.shape[1]
    count = gains.shape[0]
    extra_rows = 16

    def coded(value):
        high = lax.reduce_precision(value, 8, 7)
        both = jnp.concatenate([high.astype(bf16), (value - high).astype(bf16)])
        return jnp.pad(both, (0, extra_rows * columns - 2 * count)).reshape(extra_rows, columns)

    def decoded(rows):
        flat = rows.reshape(-1)
        return flat[:count].astype(f32) + flat[count : 2 * count].astype(f32)

    def exchange(pieces, own, axis, size, gains):
        extra = coded(gains)
        total = own.astype(f32)
        rows = own.shape[0]
        arrived = [
            shift(jnp.concatenate([piece, extra], axis=0), axis, j + 1, size)
            for j, piece in enumerate(pieces)
        ]
        for part in arrived:
            total = total + part[:rows].astype(f32)
            gains = gains + decoded(part[rows:])
        return total, gains

    me = lax.axis_index("c")
    rows = grads.reshape(16, 2, -1, columns)
    take = lambda i: lax.dynamic_index_in_dim(rows, i, 1, keepdims=False).reshape(-1, columns)
    gains = sum(gather_y(gains.reshape(-1, 128))).reshape(-1)
    total = take(me).astype(f32) + shift(take(1 - me), "c", 1, 2).astype(f32)
    for axis in ("x", "z"):
        me = lax.axis_index(axis)
        pieces = total.astype(bf16).reshape(FOUR, -1, columns)
        take = lambda i: lax.dynamic_index_in_dim(pieces, i, 0, keepdims=False)
        total, gains = exchange(
            [take((me + j) % FOUR) for j in (1, 2, 3)], take(me), axis, FOUR, gains
        )
    gains = gains.reshape(-1, 128)
    return total, (gains + shift(gains, "c", 1, 2)).reshape(-1)


def out_ffn_kernel(
    mixed0, mixed1, mixed2, mixed3, tokens_ref, weights_hbm, gain_ref, cot_ref,
    middle_ref, ffn_in_ref, acts_ref, back_ref, out_ref,
    weights, mixed_all, middle_all, sems,
):
    length, width = tokens_ref.shape
    ff = acts_ref.shape[1] // 3
    block = length // FOUR
    tile = 256
    whole_tiles = ff // tile
    rest = ff - whole_tiles * tile

    def part(first, size, sem):
        columns = pl.ds(first, size)
        return pltpu.make_async_copy(
            weights_hbm.at[:, columns], weights.at[:, columns], sems.at[sem]
        )

    def tile_parts(i):
        size = tile if i < whole_tiles else rest
        return [part(k * ff + i * tile, size, 3 * i + k) for k in range(3)]

    tiles = whole_tiles + (1 if rest else 0)
    out_part = part(3 * ff, width, 3 * tiles)
    out_part.start()
    for i in range(tiles):
        for copy in tile_parts(i):
            copy.start()

    for j, ref in enumerate((mixed0, mixed1, mixed2, mixed3)):
        cols = ref.shape[1]
        for r in range(FOUR):
            q = (r - j) % FOUR
            mixed_all[r * block : (r + 1) * block, j * cols : (j + 1) * cols] = ref[
                q * block : (q + 1) * block, :
            ]
    out_part.wait()

    def out_tile(n, carry):
        columns = pl.ds(pl.multiple_of(n * tile, tile), tile)
        w = weights[columns, 3 * ff : 3 * ff + width]
        middle_all[:, columns] = tokens_ref[:, columns].astype(f32) + dot_nt(mixed_all[...], w)
        return carry

    lax.fori_loop(0, width // tile, out_tile, 0)
    middle = middle_all[...]
    inverse = lax.rsqrt(jnp.mean(middle * middle, axis=-1, keepdims=True) + epsilon)
    ffn_in_ref[...] = (middle * inverse * gain_ref[...]).astype(bf16)
    middle_ref[...] = middle_all[:block, :]

    def hidden_tile(first, size):
        def column(k):
            return pl.ds(pl.multiple_of(k * ff + first, 128), size)

        gate = dot_nn(ffn_in_ref[...], weights[:, column(0)])
        up = dot_nn(ffn_in_ref[...], weights[:, column(1)])
        grad_hidden = dot_nn(cot_ref[...], weights[:, column(2)])
        sig = jax.nn.sigmoid(gate)
        silu = gate * sig
        acts_ref[:, column(0)] = (
            grad_hidden * up * sig * (1.0 + gate * (1.0 - sig))
        ).astype(bf16)
        acts_ref[:, column(1)] = (grad_hidden * silu).astype(bf16)
        acts_ref[:, column(2)] = (silu * up).astype(bf16)

    for i in range(tiles):
        for copy in tile_parts(i):
            copy.wait()
        hidden_tile(i * tile, tile if i < whole_tiles else rest)

    def back_tile(n, carry):
        rows = pl.ds(pl.multiple_of(n * tile, tile), tile)
        back_ref[:, rows] = dot_nt(acts_ref[:, : 2 * ff], weights[rows, : 2 * ff]).astype(bf16)
        out_ref[:, rows] = dot_nt(acts_ref[:, 2 * ff :], weights[rows, 2 * ff : 3 * ff]).astype(
            bf16
        )
        return carry

    lax.fori_loop(0, width // tile, back_tile, 0)


def out_ffn(mixed_parts, tokens_all, weights, gain, cot):
    length, width = tokens_all.shape
    ff = (weights.shape[1] - width) // 3
    shape = jax.ShapeDtypeStruct
    vmem = pl.BlockSpec(memory_space=pltpu.VMEM)
    return pl.pallas_call(
        out_ffn_kernel,
        out_shape=(
            shape((length // FOUR, width), f32),
            shape((length, width), bf16),
            shape((length, 3 * ff), bf16),
            shape((length, width), bf16),
            shape((length, width), bf16),
        ),
        in_specs=[vmem] * 5 + [pl.BlockSpec(memory_space=pl.ANY)] + [vmem] * 2,
        out_specs=(vmem,) * 5,
        scratch_shapes=[
            pltpu.VMEM(weights.shape, bf16),
            pltpu.VMEM((length, width), bf16),
            pltpu.VMEM((length, width), f32),
            pltpu.SemaphoreType.DMA((3 * (-(-ff // 256)) + 1,)),
        ],
        compiler_params=pltpu.CompilerParams(vmem_limit_bytes=48 * 1024 * 1024),
        cost_estimate=pl.CostEstimate(
            flops=2 * length * width * (6 * ff + width),
            bytes_accessed=2 * weights.size + 14 * length * width,
            transcendentals=length * ff,
        ),
        name="out_ffn",
    )(*mixed_parts, tokens_all, weights, gain.reshape(1, -1), cot)


def ffn_grads_kernel(ffn_in_ref, cot_ref, acts_ref, grads_ref, in_t, cot_t):
    rows = ffn_in_ref.shape[1]
    ff = acts_ref.shape[1] // 3
    step = 32
    for source, target in ((ffn_in_ref, in_t), (cot_ref, cot_t)):
        turned = source[...].T
        for x in range(rows // (8 * step)):
            for z in range(FOUR):
                for core in range(2):
                    old = ((x * FOUR + z) * 2 + core) * step
                    new = ((x * 2 + core) * FOUR + z) * step
                    target[new : new + step, :] = turned[old : old + step, :]
    tile = 256
    for first in range(0, 3 * ff, tile):
        size = min(tile, 3 * ff - first)
        left = in_t if first < 2 * ff else cot_t
        grads_ref[:, first : first + size] = dot_nn(
            left[...], acts_ref[:, first : first + size]
        ).astype(bf16)


def ffn_grads(ffn_in, cot, acts):
    length, width = ffn_in.shape
    columns = acts.shape[1]
    half = width // 2
    return pl.pallas_call(
        ffn_grads_kernel,
        grid=(2,),
        out_shape=jax.ShapeDtypeStruct((width, columns), bf16),
        in_specs=[
            pl.BlockSpec((length, half), lambda i: (0, i)),
            pl.BlockSpec((length, half), lambda i: (0, i)),
            pl.BlockSpec((length, columns), lambda i: (0, 0)),
        ],
        out_specs=pl.BlockSpec((half, columns), lambda i: (i, 0)),
        scratch_shapes=[pltpu.VMEM((half, length), bf16), pltpu.VMEM((half, length), bf16)],
        compiler_params=pltpu.CompilerParams(vmem_limit_bytes=40 * 1024 * 1024),
        cost_estimate=pl.CostEstimate(
            flops=2 * length * width * columns,
            bytes_accessed=2 * (2 * length * width + length * columns + width * columns),
            transcendentals=0,
        ),
        name="ffn_grads",
    )(ffn_in, cot, acts)


def local(
    tokens,
    segments,
    query_weight,
    key_weight,
    value_weight,
    out_weight,
    gate_weight,
    up_weight,
    down_weight,
    attn_gain,
    ffn_gain,
    query_gain,
    key_gain,
    cotangent,
):
    dp = ("x", "z", "c")
    length = segments.shape[0]
    block = length // FOUR
    query_cols = query_weight.shape[1]
    kv_cols = key_weight.shape[1]
    ff_cols = gate_weight.shape[1]
    query_heads = query_cols // HD
    value_heads = kv_cols // HD
    group_size = query_heads // value_heads
    score_scale = 1.0 / math.sqrt(HD)
    y = lax.axis_index("y")

    full_qkv = gather_dp(jnp.concatenate([query_weight, key_weight, value_weight], axis=1))
    qkv_cols = query_cols + 2 * kv_cols
    out_shards = gather_y(out_weight.T)
    large_shard = jnp.concatenate([gate_weight, up_weight, down_weight.T] + out_shards, axis=1)
    large_full = lax.all_gather(large_shard, dp, axis=0, tiled=True)
    full_gate_up = large_full[:, : 2 * ff_cols]
    full_down_t = large_full[:, 2 * ff_cols : 3 * ff_cols]
    out_all_t = large_full[:, 3 * ff_cols :]
    full_out_t = out_all_t[:, :query_cols]

    tokens_all = jnp.concatenate(gather_y(tokens), axis=0)
    grad_out_all = jnp.concatenate(gather_y(cotangent), axis=0)

    indices = jnp.roll(jnp.arange(length, dtype=jnp.int32), -block * y)
    ids = jnp.roll(segments, -block * y)
    positions = jnp.roll(doc_positions(segments), -block * y)
    cosine, sine_table = rope_tables(positions)
    allowed = (indices[:, None] >= indices[None, :]) & (ids[:, None] == ids[None, :])

    residual = tokens_all.astype(f32)
    attn_inv = inverse_rms(residual)
    normed = (residual * attn_inv * attn_gain).astype(bf16)
    projected = dot_nn(normed, full_qkv)
    query_proj = projected[:, :query_cols].reshape(length, query_heads, HD)
    key_proj = projected[:, query_cols : query_cols + kv_cols].reshape(length, value_heads, HD)
    value_proj = projected[:, query_cols + kv_cols :].astype(bf16).reshape(length, value_heads, HD)
    query_inv = inverse_rms(query_proj)
    key_inv = inverse_rms(key_proj)
    query_rot = (
        rotate(query_proj * query_inv * query_gain, cosine, sine_table)
        .astype(bf16)
        .reshape(length, value_heads, group_size, HD)
    )
    key_rot = rotate(key_proj * key_inv * key_gain, cosine, sine_table).astype(bf16)
    scores = (
        jnp.einsum("qgjd,kgd->gjqk", query_rot, key_rot, preferred_element_type=f32) * score_scale
    )
    scores = jnp.where(allowed, scores, masked_score)
    row_max = jnp.max(scores, axis=-1, keepdims=True)
    exponent = jnp.exp(scores - row_max)
    row_total = jnp.sum(exponent, axis=-1, keepdims=True)
    softmax_full = exponent / row_total
    softmax_low = softmax_full.astype(bf16)
    mixed = (
        jnp.einsum("gjqk,kgd->qgjd", softmax_low, value_proj, preferred_element_type=f32)
        .reshape(length, query_cols)
        .astype(bf16)
    )
    middle, ffn_all, acts, ffn_back, ffn_out = out_ffn(
        gather_y(mixed), tokens_all, large_full, ffn_gain, grad_out_all
    )
    grad_ffn_in = scatter_sum_y([ffn_back[j * block : (j + 1) * block] for j in range(FOUR)])
    ffn_rows = scatter_sum_dp_large(ffn_grads(ffn_all, grad_out_all, acts))
    ffn_inv = inverse_rms(middle)
    grad_through = norm_back_value(middle, ffn_inv, ffn_gain, grad_ffn_in)
    ffn_gain_part = jnp.sum(grad_ffn_in * middle * ffn_inv, axis=0)
    grad_middle = cotangent.astype(f32) + grad_through
    grad_middle_all = jnp.concatenate(gather_y(grad_middle.astype(bf16)), axis=0)

    ffn_out, grad_middle_all = lax.optimization_barrier((ffn_out, grad_middle_all))
    result = (
        middle + scatter_sum_y([ffn_out[j * block : (j + 1) * block] for j in range(FOUR)])
    ).astype(bf16)
    grad_gate_weight = ffn_rows[:, :ff_cols]
    grad_up_weight = ffn_rows[:, ff_cols : 2 * ff_cols]
    grad_down_weight = ffn_rows[:, 2 * ff_cols :].T

    out_part = dot_tn(grad_middle_all, mixed).astype(bf16)
    grad_mix = (
        dot_nn(grad_middle_all, full_out_t)
        .astype(bf16)
        .reshape(length, value_heads, group_size, HD)
    )
    grad_probs = jnp.einsum("qgjd,kgd->gjqk", grad_mix, value_proj, preferred_element_type=f32)
    row_delta = jnp.sum(softmax_full * grad_probs, axis=-1, keepdims=True)
    grad_scores = (softmax_full * (grad_probs - row_delta)).astype(bf16)
    grad_query_rot = (
        jnp.einsum("gjqk,kgd->qgjd", grad_scores, key_rot, preferred_element_type=f32)
        * score_scale
    ).reshape(length, query_heads, HD)
    grad_key_rot = (
        jnp.einsum("gjqk,qgjd->kgd", grad_scores, query_rot, preferred_element_type=f32)
        * score_scale
    )
    grad_values = jnp.einsum("gjqk,qgjd->kgd", softmax_low, grad_mix, preferred_element_type=f32)
    grad_query_normed = unrotate(grad_query_rot, cosine, sine_table)
    grad_key_normed = unrotate(grad_key_rot, cosine, sine_table)
    grad_query_proj = norm_back_value(query_proj, query_inv, query_gain, grad_query_normed)
    grad_key_proj = norm_back_value(key_proj, key_inv, key_gain, grad_key_normed)
    query_gain_part = jnp.sum(grad_query_normed * query_proj * query_inv, axis=(0, 1))
    key_gain_part = jnp.sum(grad_key_normed * key_proj * key_inv, axis=(0, 1))
    grad_qkv = jnp.concatenate(
        [
            grad_query_proj.reshape(length, query_cols).astype(bf16),
            grad_key_proj.reshape(length, kv_cols).astype(bf16),
            grad_values.reshape(length, kv_cols).astype(bf16),
        ],
        axis=1,
    )
    attn_back = dot_nt(grad_qkv, full_qkv)
    attn_gain_part = jnp.sum(attn_back * residual * attn_inv, axis=0)
    attn_back = attn_back.astype(bf16)
    grad_normed = scatter_sum_y([attn_back[j * block : (j + 1) * block] for j in range(FOUR)])
    grad_input = norm_back_value(residual[:block], attn_inv[:block], attn_gain, grad_normed)
    grad_tokens = (grad_middle + grad_input).astype(bf16)

    qkv_part = dot_tn(normed, grad_qkv).astype(bf16)
    attn_grads = jnp.concatenate([qkv_part, out_part], axis=1)
    gains = jnp.concatenate([attn_gain_part, ffn_gain_part, query_gain_part, key_gain_part])
    attn_rows, gains = scatter_sum_dp_small(attn_grads, gains)
    grad_query_weight = attn_rows[:, :query_cols]
    grad_key_weight = attn_rows[:, query_cols : query_cols + kv_cols]
    grad_value_weight = attn_rows[:, query_cols + kv_cols : qkv_cols]
    grad_out_weight = attn_rows[:, qkv_cols:].T
    width = attn_gain.shape[0]
    return (
        result,
        grad_tokens,
        grad_query_weight,
        grad_key_weight,
        grad_value_weight,
        grad_out_weight,
        grad_gate_weight,
        grad_up_weight,
        grad_down_weight,
        gains[:width],
        gains[width : 2 * width],
        gains[2 * width : 2 * width + HD],
        gains[2 * width + HD :],
    )


def solution(mesh):
    axes = Mesh(mesh.devices.reshape(4, 4, 2, 4), ("x", "z", "c", "y"))
    dp = ("x", "z", "c")
    rows = P(("x", "z", "c", "y"), None)
    placed = (
        rows,
        P(dp),
        P(dp, "y"),
        P(dp, "y"),
        P(dp, "y"),
        P("y", dp),
        P(dp, "y"),
        P(dp, "y"),
        P("y", dp),
        P(),
        P(),
        P(),
        P(),
        rows,
    )
    return jax.shard_map(
        local,
        mesh=axes,
        in_specs=placed,
        out_specs=(
            rows,
            rows,
            P(dp, "y"),
            P(dp, "y"),
            P(dp, "y"),
            P("y", dp),
            P(dp, "y"),
            P(dp, "y"),
            P("y", dp),
            P(),
            P(),
            P(),
            P(),
        ),
        check_vma=False,
    )
```

```python
import math

import jax
import jax.numpy as jnp
from jax import lax
from jax.experimental import pallas as pl
from jax.experimental.pallas import tpu as pltpu
from jax.sharding import Mesh, PartitionSpec as P

HD = 64
FOUR = 4

epsilon = 1e-05
rope_base = 1000000.0
masked_score = -1e30

bf16 = jnp.bfloat16
f32 = jnp.float32


def dot_nn(left, right):
    return lax.dot_general(left, right, (((1,), (0,)), ((), ())), preferred_element_type=f32)


def dot_nt(left, right):
    return lax.dot_general(left, right, (((1,), (1,)), ((), ())), preferred_element_type=f32)


def dot_tn(left, right):
    return lax.dot_general(left, right, (((0,), (0,)), ((), ())), preferred_element_type=f32)


def inverse_rms(value):
    return lax.rsqrt(jnp.mean(value * value, axis=-1, keepdims=True) + epsilon)


def norm_back_value(value, inverse, norm_gain, incoming):
    scaled = incoming * norm_gain
    average = jnp.mean(value * scaled, axis=-1, keepdims=True)
    return inverse * scaled - value * (inverse * inverse * inverse) * average


def doc_positions(segment_ids):
    length = segment_ids.shape[0]
    indices = jnp.arange(length, dtype=jnp.int32)
    begins = jnp.concatenate([jnp.ones((1,), dtype=jnp.bool_), segment_ids[1:] != segment_ids[:-1]])
    starts = lax.cummax(jnp.where(begins, indices, jnp.zeros_like(indices)), axis=0)
    return indices - starts


def rope_tables(positions):
    half_dim = HD // 2
    exponents = jnp.arange(half_dim, dtype=f32) * (2.0 / HD)
    frequency = jnp.exp(-math.log(rope_base) * exponents)
    angles = positions.astype(f32)[:, None] * frequency[None, :]
    cosine, sine = jnp.cos(angles), jnp.sin(angles)
    return (
        jnp.concatenate([cosine, cosine], axis=1),
        jnp.concatenate([-sine, sine], axis=1),
    )


def shift(value, axis, distance, size=FOUR):
    return lax.ppermute(value, axis, [(i, (i + distance) % size) for i in range(size)])


def gather_y(block):
    return [block] + [shift(block, "y", -j) for j in (1, 2, 3)]


def scatter_sum_y(blocks):
    total = blocks[0].astype(f32)
    for arrived in [shift(blocks[j].astype(bf16), "y", j) for j in (1, 2, 3)]:
        total = total + arrived.astype(f32)
    return total


def mod4(value):
    return lax.rem(value + FOUR, FOUR)


def gather_dp_blocks(shard):
    along_x = jnp.stack([shard] + [shift(shard, "x", -j) for j in (1, 2, 3)])
    along_z = jnp.stack([along_x] + [shift(along_x, "z", -j) for j in (1, 2, 3)])
    return along_z, shift(along_z, "c", 1, 2)


def pack_kernel(*refs):
    out_ref = refs[-1]
    first = 0
    for ref in refs[:-1]:
        out_ref[:, first : first + ref.shape[1]] = ref[...]
        first += ref.shape[1]


def pack_columns(parts):
    vmem = pl.BlockSpec(memory_space=pltpu.VMEM)
    return pl.pallas_call(
        pack_kernel,
        out_shape=jax.ShapeDtypeStruct(
            (parts[0].shape[0], sum(part.shape[1] for part in parts)), parts[0].dtype
        ),
        in_specs=[vmem] * len(parts),
        out_specs=vmem,
        name="pack_columns",
    )(*parts)


def order_rows_kernel(y_ref, part0, part1, part2, part3, out_ref):
    for j, part in enumerate((part0, part1, part2, part3)):
        out_ref[mod4(y_ref[0] + j)] = part[...]


def order_rows(parts):
    rows, columns = parts[0].shape
    y = lax.axis_index("y").astype(jnp.int32).reshape(1)
    vmem = pl.BlockSpec(memory_space=pltpu.VMEM)
    return pl.pallas_call(
        order_rows_kernel,
        out_shape=jax.ShapeDtypeStruct((FOUR, rows, columns), parts[0].dtype),
        in_specs=[pl.BlockSpec(memory_space=pltpu.SMEM)] + [vmem] * 4,
        out_specs=vmem,
        compiler_params=pltpu.CompilerParams(vmem_limit_bytes=16 * 1024 * 1024),
        name="order_rows",
    )(y, *parts).reshape(FOUR * rows, columns)


VMEM = pl.BlockSpec(memory_space=pltpu.VMEM)
SMEM = pl.BlockSpec(memory_space=pltpu.SMEM)
shape = jax.ShapeDtypeStruct


def head_mean(value):
    width = value.shape[1]
    row = lax.broadcasted_iota(jnp.int32, (width, width), 0) // HD
    column = lax.broadcasted_iota(jnp.int32, (width, width), 1) // HD
    ones = jnp.where(row == column, 1.0 / HD, 0.0)
    return lax.dot_general(
        value,
        ones,
        (((1,), (0,)), ((), ())),
        precision=lax.Precision.HIGHEST,
        preferred_element_type=f32,
    )


def swap_halves(value):
    width = value.shape[1]
    lane = lax.broadcasted_iota(jnp.int32, value.shape, 1)
    ahead = pltpu.roll(value, width - HD // 2, 1)
    behind = pltpu.roll(value, HD // 2, 1)
    return jnp.where(lane % HD < HD // 2, ahead, behind)


def by_core(turned, target):
    step = 32
    for i in range(turned.shape[0] // step):
        first = (i // 2) * step
        target[i % 2, first : first + step, :] = turned[i * step : (i + 1) * step, :]


def attention_kernel(
    place_ref, tok0, tok1, tok2, tok3, own_ref, other_ref, cos_ref, sin_ref, id_col, id_row,
    gain_ref, head_gain_ref,
    tokens_ref, weights_ref, normed_t_ref, proj_ref, rot_ref, value_ref, probs_ref, mixed_ref,
    normed_ref,
):
    x, z, core, y = place_ref[0], place_ref[1], place_ref[2], place_ref[3]
    length, width = tokens_ref.shape
    block = length // FOUR
    for j, part in enumerate((tok0, tok1, tok2, tok3)):
        rows = pl.ds(pl.multiple_of(mod4(y + j) * block, block), block)
        tokens_ref[rows, :] = part[...]
    for i in range(FOUR):
        for k in range(FOUR):
            from_x, from_z = mod4(i - x), mod4(k - z)
            weights_ref[i, k, core] = own_ref[from_z, from_x]
            weights_ref[i, k, 1 - core] = other_ref[from_z, from_x]
    tokens = tokens_ref[...].astype(f32)
    normed_ref[...] = (tokens * inverse_rms(tokens) * gain_ref[...]).astype(bf16)
    by_core(normed_ref[...].T, normed_t_ref)
    columns = weights_ref.shape[-1]
    projected = dot_nn(normed_ref[...], weights_ref[...].reshape(width, columns))
    heads = proj_ref.shape[1]
    both = projected[:, :heads]
    proj_ref[...] = both
    value_ref[...] = projected[:, heads:].astype(bf16)
    normal = both * lax.rsqrt(head_mean(both * both) + epsilon) * head_gain_ref[...]
    rot_ref[...] = (normal * cos_ref[...] + swap_halves(normal) * sin_ref[...]).astype(bf16)
    query_cols = mixed_ref.shape[1]
    groups = value_ref.shape[1] // HD
    per_group = query_cols // HD // groups
    index = lax.broadcasted_iota(jnp.int32, (length, length), 0)
    other = lax.broadcasted_iota(jnp.int32, (length, length), 1)
    allowed = (index >= other) & (id_col[...] == id_row[...])
    for g in range(groups):
        key = rot_ref[:, query_cols + g * HD : query_cols + (g + 1) * HD]
        value = value_ref[:, g * HD : (g + 1) * HD]
        for h in range(g * per_group, (g + 1) * per_group):
            scores = dot_nt(rot_ref[:, h * HD : (h + 1) * HD], key) * (1.0 / math.sqrt(HD))
            scores = jnp.where(allowed, scores, masked_score)
            exponent = jnp.exp(scores - jnp.max(scores, axis=-1, keepdims=True))
            probs = (exponent * (1.0 / jnp.sum(exponent, axis=-1, keepdims=True))).astype(bf16)
            probs_ref[h] = probs
            mixed_ref[:, h * HD : (h + 1) * HD] = dot_nn(probs, value).astype(bf16)


def attention(place, token_parts, own, other, cos, sin, ids, gain, head_gain):
    rows, width = token_parts[0].shape
    length = FOUR * rows
    heads = head_gain.shape[1]
    columns = own.shape[-1]
    values = columns - heads
    queries = heads - values
    return pl.pallas_call(
        attention_kernel,
        out_shape=(
            shape((length, width), bf16),
            shape((FOUR, FOUR, 2, own.shape[2], columns), bf16),
            shape((2, width // 2, length), bf16),
            shape((length, heads), f32),
            shape((length, heads), bf16),
            shape((length, values), bf16),
            shape((queries // HD, length, length), bf16),
            shape((length, queries), bf16),
        ),
        in_specs=[SMEM] + [VMEM] * 12,
        out_specs=(VMEM,) * 8,
        scratch_shapes=[pltpu.VMEM((length, width), bf16)],
        compiler_params=pltpu.CompilerParams(vmem_limit_bytes=60 * 1024 * 1024),
        cost_estimate=pl.CostEstimate(
            flops=2 * length * (width * columns + 2 * length * queries),
            bytes_accessed=8 * 1024 * 1024,
            transcendentals=length * length * queries // HD,
        ),
        name="attention",
    )(place, *token_parts, own, other, cos, sin, ids.reshape(-1, 1), ids.reshape(1, -1), gain, head_gain)


def attention_back_kernel(
    place_ref, gm0, gm1, gm2, gm3, out_t_ref, weights_ref, tokens_ref, proj_ref, rot_ref, value_ref,
    probs_ref, cos_ref, sin_ref, head_gain_ref, ffn_gain_ref, ffn_out_ref, normed_t_ref, mixed_ref,
    theirs_ref, mine_ref, message_ref, gains_ref,
    turned_key, turned_value, grad_rot, gm_ref, grad_ref, gm_t,
):
    y = place_ref[3]
    length, width = tokens_ref.shape
    block = length // FOUR
    heads = proj_ref.shape[1]
    for j, part in enumerate((gm0, gm1, gm2, gm3)):
        rows = pl.ds(pl.multiple_of(mod4(y + j) * block, block), block)
        gm_ref[rows, :] = part[...]
    scale = 1.0 / math.sqrt(HD)
    query_cols = out_t_ref.shape[1]
    groups = value_ref.shape[1] // HD
    per_group = query_cols // HD // groups
    grad_mixed = dot_nn(gm_ref[...], out_t_ref[...]).astype(bf16)
    grad_mixed_t = grad_mixed.T
    query_t = rot_ref[:, :query_cols].T
    for g in range(groups):
        key = rot_ref[:, query_cols + g * HD : query_cols + (g + 1) * HD]
        value = value_ref[:, g * HD : (g + 1) * HD]
        key_sum = jnp.zeros((HD, length), f32)
        value_sum = jnp.zeros((HD, length), f32)
        for h in range(g * per_group, (g + 1) * per_group):
            columns = slice(h * HD, (h + 1) * HD)
            probs = probs_ref[h]
            wide = probs.astype(f32)
            grad_probs = dot_nt(grad_mixed[:, columns], value)
            delta = jnp.sum(wide * grad_probs, axis=-1, keepdims=True)
            grad_scores = (wide * (grad_probs - delta)).astype(bf16)
            grad_rot[:, columns] = dot_nn(grad_scores, key) * scale
            key_sum = key_sum + dot_nn(query_t[columns, :], grad_scores)
            value_sum = value_sum + dot_nn(grad_mixed_t[columns, :], probs)
        turned_key[g * HD : (g + 1) * HD, :] = key_sum * scale
        turned_value[g * HD : (g + 1) * HD, :] = value_sum
    grad_rot[:, query_cols:] = turned_key[...].T
    grad_ref[:, heads:] = turned_value[...].T.astype(bf16)
    incoming = grad_rot[...]
    normal = incoming * cos_ref[...] - swap_halves(incoming) * sin_ref[...]
    both = proj_ref[...]
    inverse = lax.rsqrt(head_mean(both * both) + epsilon)
    scaled = normal * head_gain_ref[...]
    grad = inverse * scaled - both * (inverse * inverse * inverse) * head_mean(both * scaled)
    grad_ref[:, :heads] = grad.astype(bf16)
    head_part = jnp.sum(normal * both * inverse, axis=0, keepdims=True)

    tokens = tokens_ref[...].astype(f32)
    token_inverse = inverse_rms(tokens)
    weights = weights_ref[...].reshape(width, -1)
    tile = 256
    part = []
    for n in range(width // tile):
        columns = slice(n * tile, (n + 1) * tile)
        back = dot_nt(grad_ref[...], weights[columns, :])
        part.append(jnp.sum(back * (tokens[:, columns] * token_inverse), axis=0, keepdims=True))
        back = back.astype(bf16)
        for i in range(FOUR):
            message_ref[mod4(i - y), :block, columns] = back[i * block : (i + 1) * block, :]
    for j in range(FOUR):
        message_ref[j, block:, :] = ffn_out_ref[j]
    flat = jnp.concatenate(part + [ffn_gain_ref[...], head_part], axis=1)
    gains_ref[...] = jnp.zeros_like(gains_ref)
    line = gains_ref.shape[1]
    for row in range(-(-flat.shape[1] // line)):
        size = min(line, flat.shape[1] - row * line)
        gains_ref[row : row + 1, :size] = flat[:, row * line : row * line + size]

    core = place_ref[2]
    by_core(gm_ref[...].T, gm_t)
    columns = grad_ref.shape[1]
    for which, ref in ((1 - core, theirs_ref), (core, mine_ref)):
        ref[:, :columns] = dot_nn(normed_t_ref[which], grad_ref[...]).astype(bf16)
        ref[:, columns:] = dot_nn(gm_t[which], mixed_ref[...]).astype(bf16)


def attention_back(
    place, gm_parts, out_t, weights, tokens, proj, rot, value, probs, cos, sin, head_gain, ffn_gain_part,
    ffn_out, normed_t, mixed,
):
    length, width = tokens.shape
    heads = proj.shape[1]
    values = value.shape[1]
    line = heads + values + mixed.shape[1]
    return pl.pallas_call(
        attention_back_kernel,
        out_shape=(
            shape((width // 2, line), bf16),
            shape((width // 2, line), bf16),
            shape((FOUR, length // 2, width), bf16),
            shape((8, line), f32),
        ),
        in_specs=[SMEM] + [VMEM] * 18,
        out_specs=(VMEM,) * 4,
        scratch_shapes=[
            pltpu.VMEM((values, length), f32),
            pltpu.VMEM((values, length), f32),
            pltpu.VMEM((length, heads), f32),
            pltpu.VMEM((length, width), bf16),
            pltpu.VMEM((length, heads + values), bf16),
            pltpu.VMEM((2, width // 2, length), bf16),
        ],
        compiler_params=pltpu.CompilerParams(vmem_limit_bytes=60 * 1024 * 1024),
        cost_estimate=pl.CostEstimate(
            flops=8 * length * (width * (heads + 3 * values) + 4 * length * out_t.shape[1]),
            bytes_accessed=16 * 1024 * 1024,
            transcendentals=0,
        ),
        name="attention_back",
    )(
        place, *gm_parts, out_t, weights, tokens, proj, rot, value, probs, cos, sin, head_gain,
        ffn_gain_part, ffn_out, normed_t, mixed,
    )


def coded(value):
    high = value.astype(bf16).astype(f32)
    return jnp.concatenate([high, value - high], axis=0).astype(bf16)


def decoded(rows):
    wide = rows.astype(f32)
    return wide[:8] + wide[8:]


def after_core_kernel(
    place_ref, mine_ref, arrived_ref, gains0, gains1, gains2, gains3,
    own_ref, gains_ref, out1, out2, out3,
):
    x = place_ref[0]
    rows = own_ref.shape[0]

    def piece(j):
        at = pl.ds(pl.multiple_of(mod4(x + j) * rows, rows), rows)
        return mine_ref[at, :].astype(f32) + arrived_ref[at, :].astype(f32)

    gains = gains0[...] + gains1[...] + gains2[...] + gains3[...]
    gains_ref[...] = gains
    own_ref[...] = piece(0)
    for j, ref in ((1, out1), (2, out2), (3, out3)):
        ref[:rows, :] = piece(j).astype(bf16)
        ref[rows:, :] = coded(gains)


def after_core(place, mine, arrived, gains):
    rows, columns = mine.shape
    rows = rows // FOUR
    return pl.pallas_call(
        after_core_kernel,
        out_shape=(shape((rows, columns), f32), shape((8, columns), f32))
        + (shape((rows + 16, columns), bf16),) * 3,
        in_specs=[SMEM] + [VMEM] * 6,
        out_specs=(VMEM,) * 5,
        name="after_core",
    )(place, mine, arrived, *gains)


def after_x_kernel(
    place_ref, own_in, gains_in, in1, in2, in3, own_ref, gains_ref, out1, out2, out3, total
):
    z = place_ref[1]
    rows = own_in.shape[0]
    value = own_in[...]
    gains = gains_in[...]
    for ref in (in1, in2, in3):
        value = value + ref[:rows, :].astype(f32)
        gains = gains + decoded(ref[rows:, :])
    total[...] = value
    gains_ref[...] = gains
    few = own_ref.shape[0]

    def piece(j):
        return total[pl.ds(pl.multiple_of(mod4(z + j) * few, few), few), :]

    own_ref[...] = piece(0)
    for j, ref in ((1, out1), (2, out2), (3, out3)):
        ref[:few, :] = piece(j).astype(bf16)
        ref[few:, :] = coded(gains)


def after_x(place, own, gains, arrived):
    rows, columns = own.shape
    few = rows // FOUR
    return pl.pallas_call(
        after_x_kernel,
        out_shape=(shape((few, columns), f32), shape((8, columns), f32))
        + (shape((few + 16, columns), bf16),) * 3,
        in_specs=[SMEM] + [VMEM] * 5,
        out_specs=(VMEM,) * 5,
        scratch_shapes=[pltpu.VMEM((rows, columns), f32)],
        name="after_x",
    )(place, own, gains, *arrived)


def after_z_kernel(own_in, gains_in, in1, in2, in3, query_ref, key_ref, value_ref, out_ref, gains_ref):
    rows = own_in.shape[0]
    value = own_in[...]
    gains = gains_in[...]
    for ref in (in1, in2, in3):
        value = value + ref[:rows, :].astype(f32)
        gains = gains + decoded(ref[rows:, :])
    gains_ref[...] = gains
    first = 0
    for ref in (query_ref, key_ref, value_ref, out_ref):
        ref[...] = value[:, first : first + ref.shape[1]]
        first += ref.shape[1]


def after_z(own, gains, arrived, sizes):
    rows, columns = own.shape
    return pl.pallas_call(
        after_z_kernel,
        out_shape=tuple(shape((rows, size), f32) for size in sizes) + (shape(gains.shape, f32),),
        in_specs=[VMEM] * 5,
        out_specs=(VMEM,) * (len(sizes) + 1),
        name="after_z",
    )(own, gains, *arrived)


def out_ffn_kernel(
    y_ref, mixed0, mixed1, mixed2, mixed3, tokens_ref, weights_hbm, gain_ref, cot_ref,
    middle_ref, ffn_in_ref, acts_ref, back_ref, out_ref,
    weights, mixed_all, middle_all, sems,
):
    length, width = tokens_ref.shape
    ff = acts_ref.shape[1] // 3
    block = length // FOUR
    tile = 256
    whole_tiles = ff // tile
    rest = ff - whole_tiles * tile

    def part(first, size, sem):
        columns = pl.ds(first, size)
        return pltpu.make_async_copy(
            weights_hbm.at[:, columns], weights.at[:, columns], sems.at[sem]
        )

    def tile_parts(i):
        size = tile if i < whole_tiles else rest
        return [part(k * ff + i * tile, size, 3 * i + k) for k in range(3)]

    tiles = whole_tiles + (1 if rest else 0)
    out_part = part(3 * ff, width, 3 * tiles)
    out_part.start()
    for i in range(tiles):
        for copy in tile_parts(i):
            copy.start()

    for j, ref in enumerate((mixed0, mixed1, mixed2, mixed3)):
        cols = ref.shape[1]
        mixed_all[:, j * cols : (j + 1) * cols] = ref[...]
    out_part.wait()

    def out_tile(n, carry):
        columns = pl.ds(pl.multiple_of(n * tile, tile), tile)
        w = weights[columns, 3 * ff : 3 * ff + width]
        middle_all[:, columns] = tokens_ref[:, columns].astype(f32) + dot_nt(mixed_all[...], w)
        return carry

    lax.fori_loop(0, width // tile, out_tile, 0)
    middle = middle_all[...]
    inverse = lax.rsqrt(jnp.mean(middle * middle, axis=-1, keepdims=True) + epsilon)
    ffn_in_ref[...] = (middle * inverse * gain_ref[...]).astype(bf16)
    y = y_ref[0]
    middle_ref[...] = middle_all[pl.ds(pl.multiple_of(y * block, block), block), :]

    def hidden_tile(first, size):
        def column(k):
            return pl.ds(pl.multiple_of(k * ff + first, 128), size)

        gate = dot_nn(ffn_in_ref[...], weights[:, column(0)])
        up = dot_nn(ffn_in_ref[...], weights[:, column(1)])
        grad_hidden = dot_nn(cot_ref[...], weights[:, column(2)])
        sig = jax.nn.sigmoid(gate)
        silu = gate * sig
        acts_ref[:, column(0)] = (
            grad_hidden * up * sig * (1.0 + gate * (1.0 - sig))
        ).astype(bf16)
        acts_ref[:, column(1)] = (grad_hidden * silu).astype(bf16)
        acts_ref[:, column(2)] = (silu * up).astype(bf16)

    for i in range(tiles):
        for copy in tile_parts(i):
            copy.wait()
        hidden_tile(i * tile, tile if i < whole_tiles else rest)

    def back_tile(n, carry):
        rows = pl.ds(pl.multiple_of(n * tile, tile), tile)
        back = dot_nt(acts_ref[:, : 2 * ff], weights[rows, : 2 * ff]).astype(bf16)
        for i in range(FOUR):
            back_ref[mod4(i - y), :, rows] = back[i * block : (i + 1) * block, :]
        out = dot_nt(acts_ref[:, 2 * ff :], weights[rows, 2 * ff : 3 * ff]).astype(bf16)
        for i in range(FOUR):
            out_ref[mod4(i - y), :, rows] = out[i * block : (i + 1) * block, :]
        return carry

    lax.fori_loop(0, width // tile, back_tile, 0)


def out_ffn(mixed_parts, tokens_all, weights, gain, cot):
    length, width = tokens_all.shape
    ff = (weights.shape[1] - width) // 3
    vmem = pl.BlockSpec(memory_space=pltpu.VMEM)
    return pl.pallas_call(
        out_ffn_kernel,
        out_shape=(
            shape((length // FOUR, width), f32),
            shape((length, width), bf16),
            shape((length, 3 * ff), bf16),
            shape((FOUR, length // FOUR, width), bf16),
            shape((FOUR, length // FOUR, width), bf16),
        ),
        in_specs=[pl.BlockSpec(memory_space=pltpu.SMEM)] + [vmem] * 5 + [pl.BlockSpec(memory_space=pl.ANY)] + [vmem] * 2,
        out_specs=(vmem,) * 5,
        scratch_shapes=[
            pltpu.VMEM(weights.shape, bf16),
            pltpu.VMEM((length, width), bf16),
            pltpu.VMEM((length, width), f32),
            pltpu.SemaphoreType.DMA((3 * (-(-ff // 256)) + 1,)),
        ],
        compiler_params=pltpu.CompilerParams(vmem_limit_bytes=60 * 1024 * 1024),
        cost_estimate=pl.CostEstimate(
            flops=2 * length * width * (6 * ff + width),
            bytes_accessed=2 * weights.size + 14 * length * width,
            transcendentals=length * ff,
        ),
        name="out_ffn",
    )(lax.axis_index("y").astype(jnp.int32).reshape(1), *mixed_parts, tokens_all, weights, gain.reshape(1, -1), cot)


def ffn_grads_kernel(ffn_in_ref, cot_ref, acts_ref, grads_ref, in_t, cot_t):
    rows = ffn_in_ref.shape[1]
    ff = acts_ref.shape[1] // 3
    step = 32
    for source, target in ((ffn_in_ref, in_t), (cot_ref, cot_t)):
        turned = source[...].T
        for x in range(rows // (8 * step)):
            for z in range(FOUR):
                for core in range(2):
                    old = ((x * FOUR + z) * 2 + core) * step
                    new = ((x * 2 + core) * FOUR + z) * step
                    target[new : new + step, :] = turned[old : old + step, :]
    tile = 256
    for first in range(0, 3 * ff, tile):
        size = min(tile, 3 * ff - first)
        left = in_t if first < 2 * ff else cot_t
        grads_ref[:, first : first + size] = dot_nn(
            left[...], acts_ref[:, first : first + size]
        ).astype(bf16)


def ffn_grads(ffn_in, cot, acts):
    length, width = ffn_in.shape
    columns = acts.shape[1]
    half = width // 2
    return pl.pallas_call(
        ffn_grads_kernel,
        grid=(2,),
        out_shape=jax.ShapeDtypeStruct((width, columns), bf16),
        in_specs=[
            pl.BlockSpec((length, half), lambda i: (0, i)),
            pl.BlockSpec((length, half), lambda i: (0, i)),
            pl.BlockSpec((length, columns), lambda i: (0, 0)),
        ],
        out_specs=pl.BlockSpec((half, columns), lambda i: (i, 0)),
        scratch_shapes=[pltpu.VMEM((half, length), bf16), pltpu.VMEM((half, length), bf16)],
        compiler_params=pltpu.CompilerParams(vmem_limit_bytes=60 * 1024 * 1024),
        cost_estimate=pl.CostEstimate(
            flops=2 * length * width * columns,
            bytes_accessed=2 * (2 * length * width + length * columns + width * columns),
            transcendentals=0,
        ),
        name="ffn_grads",
    )(ffn_in, cot, acts)


def local(
    tokens,
    segments,
    query_weight,
    key_weight,
    value_weight,
    out_weight,
    gate_weight,
    up_weight,
    down_weight,
    attn_gain,
    ffn_gain,
    query_gain,
    key_gain,
    cotangent,
):
    dp = ("x", "z", "c")
    length = segments.shape[0]
    block = length // FOUR
    query_cols = query_weight.shape[1]
    kv_cols = key_weight.shape[1]
    ff_cols = gate_weight.shape[1]
    qkv_cols = query_cols + 2 * kv_cols
    place = jnp.stack([lax.axis_index(axis) for axis in ("x", "z", "c", "y")]).astype(jnp.int32)

    own, other = gather_dp_blocks(pack_columns([query_weight, key_weight, value_weight]))
    large_shard = pack_columns([gate_weight, up_weight, down_weight.T] + gather_y(out_weight.T))
    large_full = lax.all_gather(large_shard, dp, axis=0, tiled=True)
    full_out_t = large_full[:, 3 * ff_cols : 3 * ff_cols + query_cols]

    token_parts = gather_y(tokens)
    grad_out_all = order_rows(gather_y(cotangent))
    cosine, sine = rope_tables(doc_positions(segments))
    repeats = (query_cols + kv_cols) // HD
    cosine, sine = jnp.tile(cosine, (1, repeats)), jnp.tile(sine, (1, repeats))
    head_gain = jnp.concatenate(
        [query_gain] * (query_cols // HD) + [key_gain] * (kv_cols // HD)
    ).reshape(1, -1)
    tokens_all, full_qkv, normed_t, proj, rot, value, probs, mixed = attention(
        place, token_parts, own, other, cosine, sine, segments, attn_gain.reshape(1, -1), head_gain
    )
    middle, ffn_all, acts, ffn_back, ffn_out = out_ffn(
        gather_y(mixed), tokens_all, large_full, ffn_gain, grad_out_all
    )
    grad_ffn_in = scatter_sum_y([ffn_back[j] for j in range(FOUR)])
    ffn_part = lax.psum_scatter(
        ffn_grads(ffn_all, grad_out_all, acts), ("x", "c"), scatter_dimension=0, tiled=True
    )
    ffn_inv = inverse_rms(middle)
    grad_through = norm_back_value(middle, ffn_inv, ffn_gain, grad_ffn_in)
    ffn_gain_part = jnp.sum(grad_ffn_in * middle * ffn_inv, axis=0)
    grad_middle = cotangent.astype(f32) + grad_through
    gm_parts = gather_y(grad_middle.astype(bf16))
    width = tokens.shape[1]
    theirs, mine, messages, gains = attention_back(
        place, gm_parts, full_out_t, full_qkv, tokens_all, proj, rot, value, probs, cosine, sine,
        head_gain, ffn_gain_part.reshape(1, -1), ffn_out, normed_t, mixed,
    )
    ffn_part, mine = lax.optimization_barrier((ffn_part, mine))
    ffn_rows = lax.psum_scatter(ffn_part, "z", scatter_dimension=0, tiled=True)

    arrived = shift(theirs, "c", 1, 2)
    all_gains = gather_y(gains)
    back_parts = [messages[0]] + [shift(messages[j], "y", j) for j in (1, 2, 3)]
    own_rows, gains, *outgoing = after_core(place, mine, arrived, all_gains)
    arrived = [shift(part, "x", j + 1) for j, part in enumerate(outgoing)]
    ffn_rows, own_rows = lax.optimization_barrier((ffn_rows, own_rows))
    ffn_rows = ffn_rows.astype(f32)
    grad_gate_weight = ffn_rows[:, :ff_cols]
    grad_up_weight = ffn_rows[:, ff_cols : 2 * ff_cols]
    grad_down_weight = ffn_rows[:, 2 * ff_cols :].T
    own_rows, gains, *outgoing = after_x(place, own_rows, gains, arrived)
    arrived = [shift(part, "z", j + 1) for j, part in enumerate(outgoing)]
    grad_query_weight, grad_key_weight, grad_value_weight, grad_out_t, gains = after_z(
        own_rows, gains, arrived, (query_cols, kv_cols, kv_cols, query_cols)
    )
    back_parts, gains = lax.optimization_barrier((back_parts, gains))
    grad_out_weight = grad_out_t.T
    gains = (gains + shift(gains, "c", 1, 2)).reshape(-1)
    query_gains = gains[2 * width : 2 * width + query_cols].reshape(-1, HD)
    key_gains = gains[2 * width + query_cols :][:kv_cols].reshape(-1, HD)

    sums = sum(part.astype(f32) for part in back_parts)
    result = (middle + sums[block:]).astype(bf16)
    own_tokens = tokens.astype(f32)
    grad_input = norm_back_value(own_tokens, inverse_rms(own_tokens), attn_gain, sums[:block])
    grad_tokens = (grad_middle + grad_input).astype(bf16)
    return (
        result,
        grad_tokens,
        grad_query_weight,
        grad_key_weight,
        grad_value_weight,
        grad_out_weight,
        grad_gate_weight,
        grad_up_weight,
        grad_down_weight,
        gains[:width],
        gains[width : 2 * width],
        jnp.sum(query_gains, axis=0),
        jnp.sum(key_gains, axis=0),
    )


def solution(mesh):
    axes = Mesh(mesh.devices.reshape(4, 4, 2, 4), ("x", "z", "c", "y"))
    dp = ("x", "z", "c")
    rows = P(("x", "z", "c", "y"), None)
    placed = (
        rows,
        P(dp),
        P(dp, "y"),
        P(dp, "y"),
        P(dp, "y"),
        P("y", dp),
        P(dp, "y"),
        P(dp, "y"),
        P("y", dp),
        P(),
        P(),
        P(),
        P(),
        rows,
    )
    return jax.shard_map(
        local,
        mesh=axes,
        in_specs=placed,
        out_specs=(
            rows,
            rows,
            P(dp, "y"),
            P(dp, "y"),
            P(dp, "y"),
            P("y", dp),
            P(dp, "y"),
            P(dp, "y"),
            P("y", dp),
            P(),
            P(),
            P(),
            P(),
        ),
        check_vma=False,
    )
```

```python
import math

import jax
import jax.numpy as jnp
from jax import lax
from jax.experimental import pallas as pl
from jax.experimental.pallas import tpu as pltpu
from jax.sharding import Mesh, PartitionSpec as P

HD = 64
FOUR = 4

epsilon = 1e-05
rope_base = 1000000.0
masked_score = -1e30

bf16 = jnp.bfloat16
f32 = jnp.float32


def dot_nn(left, right):
    return lax.dot_general(left, right, (((1,), (0,)), ((), ())), preferred_element_type=f32)


def dot_nt(left, right):
    return lax.dot_general(left, right, (((1,), (1,)), ((), ())), preferred_element_type=f32)


def dot_tn(left, right):
    return lax.dot_general(left, right, (((0,), (0,)), ((), ())), preferred_element_type=f32)


def inverse_rms(value):
    return lax.rsqrt(jnp.mean(value * value, axis=-1, keepdims=True) + epsilon)


def norm_back_value(value, inverse, norm_gain, incoming):
    scaled = incoming * norm_gain
    average = jnp.mean(value * scaled, axis=-1, keepdims=True)
    return inverse * scaled - value * (inverse * inverse * inverse) * average


def doc_positions(segment_ids):
    length = segment_ids.shape[0]
    indices = jnp.arange(length, dtype=jnp.int32)
    begins = jnp.concatenate([jnp.ones((1,), dtype=jnp.bool_), segment_ids[1:] != segment_ids[:-1]])
    starts = lax.cummax(jnp.where(begins, indices, jnp.zeros_like(indices)), axis=0)
    return indices - starts


def rope_tables(positions):
    half_dim = HD // 2
    exponents = jnp.arange(half_dim, dtype=f32) * (2.0 / HD)
    frequency = jnp.exp(-math.log(rope_base) * exponents)
    angles = positions.astype(f32)[:, None] * frequency[None, :]
    cosine, sine = jnp.cos(angles), jnp.sin(angles)
    return (
        jnp.concatenate([cosine, cosine], axis=1),
        jnp.concatenate([-sine, sine], axis=1),
    )


def shift(value, axis, distance, size=FOUR):
    return lax.ppermute(value, axis, [(i, (i + distance) % size) for i in range(size)])


def gather_y(block):
    return [block] + [shift(block, "y", -j) for j in (1, 2, 3)]


def scatter_sum_y(blocks):
    total = blocks[0].astype(f32)
    for arrived in [shift(blocks[j].astype(bf16), "y", j) for j in (1, 2, 3)]:
        total = total + arrived.astype(f32)
    return total


def mod4(value):
    return lax.rem(value + FOUR, FOUR)


def gather_dp_blocks(shard):
    along_x = jnp.stack([shard] + [shift(shard, "x", -j) for j in (1, 2, 3)])
    along_z = jnp.stack([along_x] + [shift(along_x, "z", -j) for j in (1, 2, 3)])
    return along_z, shift(along_z, "c", 1, 2)


def pack_kernel(*refs):
    out_ref = refs[-1]
    first = 0
    for ref in refs[:-1]:
        out_ref[:, first : first + ref.shape[1]] = ref[...]
        first += ref.shape[1]


def pack_columns(parts):
    vmem = pl.BlockSpec(memory_space=pltpu.VMEM)
    return pl.pallas_call(
        pack_kernel,
        out_shape=jax.ShapeDtypeStruct(
            (parts[0].shape[0], sum(part.shape[1] for part in parts)), parts[0].dtype
        ),
        in_specs=[vmem] * len(parts),
        out_specs=vmem,
        name="pack_columns",
    )(*parts)


def order_rows_kernel(y_ref, part0, part1, part2, part3, out_ref):
    for j, part in enumerate((part0, part1, part2, part3)):
        out_ref[mod4(y_ref[0] + j)] = part[part.shape[0] - out_ref.shape[1] :, :]


def order_rows(parts, rows):
    columns = parts[0].shape[1]
    y = lax.axis_index("y").astype(jnp.int32).reshape(1)
    vmem = pl.BlockSpec(memory_space=pltpu.VMEM)
    return pl.pallas_call(
        order_rows_kernel,
        out_shape=jax.ShapeDtypeStruct((FOUR, rows, columns), parts[0].dtype),
        in_specs=[pl.BlockSpec(memory_space=pltpu.SMEM)] + [vmem] * 4,
        out_specs=vmem,
        compiler_params=pltpu.CompilerParams(vmem_limit_bytes=60 * 1024 * 1024),
        name="order_rows",
    )(y, *parts).reshape(FOUR * rows, columns)


VMEM = pl.BlockSpec(memory_space=pltpu.VMEM)
SMEM = pl.BlockSpec(memory_space=pltpu.SMEM)
shape = jax.ShapeDtypeStruct


def head_mean(value):
    width = value.shape[1]
    row = lax.broadcasted_iota(jnp.int32, (width, width), 0) // HD
    column = lax.broadcasted_iota(jnp.int32, (width, width), 1) // HD
    ones = jnp.where(row == column, 1.0 / HD, 0.0)
    return lax.dot_general(
        value,
        ones,
        (((1,), (0,)), ((), ())),
        precision=lax.Precision.HIGHEST,
        preferred_element_type=f32,
    )


def swap_halves(value):
    width = value.shape[1]
    lane = lax.broadcasted_iota(jnp.int32, value.shape, 1)
    ahead = pltpu.roll(value, width - HD // 2, 1)
    behind = pltpu.roll(value, HD // 2, 1)
    return jnp.where(lane % HD < HD // 2, ahead, behind)


def by_core(turned, target):
    step = 32
    for i in range(turned.shape[0] // step):
        first = (i // 2) * step
        target[i % 2, first : first + step, :] = turned[i * step : (i + 1) * step, :]


def attention_kernel(
    place_ref, tok0, tok1, tok2, tok3, own_ref, other_ref, cos_ref, sin_ref, id_col, id_row,
    gain_ref, head_gain_ref,
    tokens_ref, weights_ref, normed_t_ref, proj_ref, rot_ref, value_ref, probs_ref, mixed_ref,
    normed_ref,
):
    x, z, core, y = place_ref[0], place_ref[1], place_ref[2], place_ref[3]
    length, width = tokens_ref.shape
    block = length // FOUR
    for j, part in enumerate((tok0, tok1, tok2, tok3)):
        rows = pl.ds(pl.multiple_of(mod4(y + j) * block, block), block)
        tokens_ref[rows, :] = part[:block, :]
    for i in range(FOUR):
        for k in range(FOUR):
            from_x, from_z = mod4(i - x), mod4(k - z)
            weights_ref[i, k, core] = own_ref[from_z, from_x]
            weights_ref[i, k, 1 - core] = other_ref[from_z, from_x]
    tokens = tokens_ref[...].astype(f32)
    normed_ref[...] = (tokens * inverse_rms(tokens) * gain_ref[...]).astype(bf16)
    by_core(normed_ref[...].T, normed_t_ref)
    columns = weights_ref.shape[-1]
    projected = dot_nn(normed_ref[...], weights_ref[...].reshape(width, columns))
    heads = proj_ref.shape[1]
    both = projected[:, :heads]
    proj_ref[...] = both
    value_ref[...] = projected[:, heads:].astype(bf16)
    normal = both * lax.rsqrt(head_mean(both * both) + epsilon) * head_gain_ref[...]
    rot_ref[...] = (normal * cos_ref[...] + swap_halves(normal) * sin_ref[...]).astype(bf16)
    query_cols = mixed_ref.shape[1]
    groups = value_ref.shape[1] // HD
    per_group = query_cols // HD // groups
    index = lax.broadcasted_iota(jnp.int32, (length, length), 0)
    other = lax.broadcasted_iota(jnp.int32, (length, length), 1)
    allowed = (index >= other) & (id_col[...] == id_row[...])
    for g in range(groups):
        key = rot_ref[:, query_cols + g * HD : query_cols + (g + 1) * HD]
        value = value_ref[:, g * HD : (g + 1) * HD]
        for h in range(g * per_group, (g + 1) * per_group):
            scores = dot_nt(rot_ref[:, h * HD : (h + 1) * HD], key) * (1.0 / math.sqrt(HD))
            scores = jnp.where(allowed, scores, masked_score)
            exponent = jnp.exp(scores - jnp.max(scores, axis=-1, keepdims=True))
            probs = (exponent * (1.0 / jnp.sum(exponent, axis=-1, keepdims=True))).astype(bf16)
            probs_ref[h] = probs
            mixed_ref[:, h * HD : (h + 1) * HD] = dot_nn(probs, value).astype(bf16)


def attention(place, rows, token_parts, own, other, cos, sin, ids, gain, head_gain):
    width = token_parts[0].shape[1]
    length = FOUR * rows
    heads = head_gain.shape[1]
    columns = own.shape[-1]
    values = columns - heads
    queries = heads - values
    return pl.pallas_call(
        attention_kernel,
        out_shape=(
            shape((length, width), bf16),
            shape((FOUR, FOUR, 2, own.shape[2], columns), bf16),
            shape((2, width // 2, length), bf16),
            shape((length, heads), f32),
            shape((length, heads), bf16),
            shape((length, values), bf16),
            shape((queries // HD, length, length), bf16),
            shape((length, queries), bf16),
        ),
        in_specs=[SMEM] + [VMEM] * 12,
        out_specs=(VMEM,) * 8,
        scratch_shapes=[pltpu.VMEM((length, width), bf16)],
        compiler_params=pltpu.CompilerParams(vmem_limit_bytes=60 * 1024 * 1024),
        cost_estimate=pl.CostEstimate(
            flops=2 * length * (width * columns + 2 * length * queries),
            bytes_accessed=8 * 1024 * 1024,
            transcendentals=length * length * queries // HD,
        ),
        name="attention",
    )(place, *token_parts, own, other, cos, sin, ids.reshape(-1, 1), ids.reshape(1, -1), gain, head_gain)


def attention_back_kernel(
    place_ref, gm0, gm1, gm2, gm3, out_t_ref, weights_ref, tokens_ref, proj_ref, rot_ref, value_ref,
    probs_ref, cos_ref, sin_ref, head_gain_ref, ffn_gain_ref, ffn_out_ref, normed_t_ref, mixed_ref,
    theirs_ref, mine_ref, message0, message1, message2, message3, gains_ref,
    turned_key, turned_value, grad_rot, gm_ref, grad_ref, gm_t, back_all,
):
    y = place_ref[3]
    length, width = tokens_ref.shape
    block = length // FOUR
    heads = proj_ref.shape[1]
    for j, part in enumerate((gm0, gm1, gm2, gm3)):
        rows = pl.ds(pl.multiple_of(mod4(y + j) * block, block), block)
        gm_ref[rows, :] = part[...]
    scale = 1.0 / math.sqrt(HD)
    query_cols = out_t_ref.shape[1]
    groups = value_ref.shape[1] // HD
    per_group = query_cols // HD // groups
    grad_mixed = dot_nn(gm_ref[...], out_t_ref[...]).astype(bf16)
    grad_mixed_t = grad_mixed.T
    query_t = rot_ref[:, :query_cols].T
    for g in range(groups):
        key = rot_ref[:, query_cols + g * HD : query_cols + (g + 1) * HD]
        value = value_ref[:, g * HD : (g + 1) * HD]
        key_sum = jnp.zeros((HD, length), f32)
        value_sum = jnp.zeros((HD, length), f32)
        for h in range(g * per_group, (g + 1) * per_group):
            columns = slice(h * HD, (h + 1) * HD)
            probs = probs_ref[h]
            wide = probs.astype(f32)
            grad_probs = dot_nt(grad_mixed[:, columns], value)
            delta = jnp.sum(wide * grad_probs, axis=-1, keepdims=True)
            grad_scores = (wide * (grad_probs - delta)).astype(bf16)
            grad_rot[:, columns] = dot_nn(grad_scores, key) * scale
            key_sum = key_sum + dot_nn(query_t[columns, :], grad_scores)
            value_sum = value_sum + dot_nn(grad_mixed_t[columns, :], probs)
        turned_key[g * HD : (g + 1) * HD, :] = key_sum * scale
        turned_value[g * HD : (g + 1) * HD, :] = value_sum
    grad_rot[:, query_cols:] = turned_key[...].T
    grad_ref[:, heads:] = turned_value[...].T.astype(bf16)
    incoming = grad_rot[...]
    normal = incoming * cos_ref[...] - swap_halves(incoming) * sin_ref[...]
    both = proj_ref[...]
    inverse = lax.rsqrt(head_mean(both * both) + epsilon)
    scaled = normal * head_gain_ref[...]
    grad = inverse * scaled - both * (inverse * inverse * inverse) * head_mean(both * scaled)
    grad_ref[:, :heads] = grad.astype(bf16)
    head_part = jnp.sum(normal * both * inverse, axis=0, keepdims=True)

    tokens = tokens_ref[...].astype(f32)
    token_inverse = inverse_rms(tokens)
    weights = weights_ref[...].reshape(width, -1)
    tile = 256
    part = []
    for n in range(width // tile):
        columns = slice(n * tile, (n + 1) * tile)
        back = dot_nt(grad_ref[...], weights[columns, :])
        part.append(jnp.sum(back * (tokens[:, columns] * token_inverse), axis=0, keepdims=True))
        back = back.astype(bf16)
        for i in range(FOUR):
            back_all[mod4(i - y), :, columns] = back[i * block : (i + 1) * block, :]
    for j, ref in enumerate((message0, message1, message2, message3)):
        ref[:block, :] = back_all[j]
        ref[block:, :] = ffn_out_ref[j]
    flat = jnp.concatenate(part + [ffn_gain_ref[...], head_part], axis=1)
    gains_ref[...] = jnp.zeros_like(gains_ref)
    line = gains_ref.shape[1]
    for row in range(-(-flat.shape[1] // line)):
        size = min(line, flat.shape[1] - row * line)
        gains_ref[row : row + 1, :size] = flat[:, row * line : row * line + size]

    core = place_ref[2]
    by_core(gm_ref[...].T, gm_t)
    columns = grad_ref.shape[1]
    for which, ref in ((1 - core, theirs_ref), (core, mine_ref)):
        rows = mine_ref.shape[0]
        ref[:rows, :columns] = dot_nn(normed_t_ref[which], grad_ref[...]).astype(bf16)
        ref[:rows, columns:] = dot_nn(gm_t[which], mixed_ref[...]).astype(bf16)
    theirs_ref[mine_ref.shape[0] :, :] = coded(gains_ref[...])


def attention_back(
    place, gm_parts, out_t, weights, tokens, proj, rot, value, probs, cos, sin, head_gain, ffn_gain_part,
    ffn_out, normed_t, mixed,
):
    length, width = tokens.shape
    heads = proj.shape[1]
    values = value.shape[1]
    line = heads + values + mixed.shape[1]
    return pl.pallas_call(
        attention_back_kernel,
        out_shape=(
            shape((width // 2 + 16, line), bf16),
            shape((width // 2, line), bf16),
        )
        + (shape((length // 2, width), bf16),) * 4
        + (shape((8, line), f32),),
        in_specs=[SMEM] + [VMEM] * 18,
        out_specs=(VMEM,) * 7,
        scratch_shapes=[
            pltpu.VMEM((values, length), f32),
            pltpu.VMEM((values, length), f32),
            pltpu.VMEM((length, heads), f32),
            pltpu.VMEM((length, width), bf16),
            pltpu.VMEM((length, heads + values), bf16),
            pltpu.VMEM((2, width // 2, length), bf16),
            pltpu.VMEM((FOUR, length // FOUR, width), bf16),
        ],
        compiler_params=pltpu.CompilerParams(vmem_limit_bytes=60 * 1024 * 1024),
        cost_estimate=pl.CostEstimate(
            flops=10**11,
            bytes_accessed=16 * 1024 * 1024,
            transcendentals=0,
        ),
        name="attention_back",
    )(
        place, *gm_parts, out_t, weights, tokens, proj, rot, value, probs, cos, sin, head_gain,
        ffn_gain_part, ffn_out, normed_t, mixed,
    )


def coded(value):
    high = value.astype(bf16).astype(f32)
    return jnp.concatenate([high, value - high], axis=0).astype(bf16)


def decoded(rows):
    wide = rows.astype(f32)
    return wide[:8] + wide[8:]


def after_core_kernel(
    place_ref, mine_ref, arrived_ref, gains_in,
    own_ref, gains_ref, out1, out2, out3,
):
    x = place_ref[0]
    rows = own_ref.shape[0]

    def piece(j):
        at = pl.ds(pl.multiple_of(mod4(x + j) * rows, rows), rows)
        return mine_ref[at, :].astype(f32) + arrived_ref[at, :].astype(f32)

    gains = gains_in[...] + decoded(arrived_ref[FOUR * rows :, :])
    gains_ref[...] = gains
    own_ref[...] = piece(0)
    for j, ref in ((1, out1), (2, out2), (3, out3)):
        ref[:rows, :] = piece(j).astype(bf16)
        ref[rows:, :] = coded(gains)


def after_core(place, mine, arrived, gains):
    rows, columns = mine.shape
    rows = rows // FOUR
    return pl.pallas_call(
        after_core_kernel,
        out_shape=(shape((rows, columns), f32), shape((8, columns), f32))
        + (shape((rows + 16, columns), bf16),) * 3,
        in_specs=[SMEM] + [VMEM] * 3,
        out_specs=(VMEM,) * 5,
        compiler_params=pltpu.CompilerParams(vmem_limit_bytes=60 * 1024 * 1024),
        name="after_core",
    )(place, mine, arrived, gains)


def after_x_kernel(
    place_ref, own_in, gains_in, in1, in2, in3, own_ref, gains_ref, out1, out2, out3, total
):
    z = place_ref[1]
    rows = own_in.shape[0]
    value = own_in[...]
    gains = gains_in[...]
    for ref in (in1, in2, in3):
        value = value + ref[:rows, :].astype(f32)
        gains = gains + decoded(ref[rows:, :])
    total[...] = value
    gains_ref[...] = gains
    few = own_ref.shape[0]

    def piece(j):
        return total[pl.ds(pl.multiple_of(mod4(z + j) * few, few), few), :]

    own_ref[...] = piece(0)
    extra = coded(gains)
    for j, ref in ((1, out1), (2, out2), (3, out3)):
        ref[:few, :] = piece(j).astype(bf16)
        ref[few:, :] = extra


def after_x(place, own, gains, arrived):
    rows, columns = own.shape
    few = rows // FOUR
    return pl.pallas_call(
        after_x_kernel,
        out_shape=(shape((few, columns), f32), shape((8, columns), f32))
        + (shape((few + 16, columns), bf16),) * 3,
        in_specs=[SMEM] + [VMEM] * 5,
        out_specs=(VMEM,) * 5,
        scratch_shapes=[pltpu.VMEM((rows, columns), f32)],
        compiler_params=pltpu.CompilerParams(vmem_limit_bytes=60 * 1024 * 1024),
        name="after_x",
    )(place, own, gains, *arrived)


def split_z_kernel(place_ref, part_ref, *refs):
    rows = refs[0].shape[0]
    for j, ref in enumerate(refs):
        at = pl.multiple_of(mod4(place_ref[1] + j) * rows, rows)
        ref[...] = part_ref[pl.ds(at, rows), :]


def split_z(place, part):
    rows, columns = part.shape
    return pl.pallas_call(
        split_z_kernel,
        out_shape=(shape((rows // FOUR, columns), part.dtype),) * 4,
        in_specs=[SMEM, VMEM],
        out_specs=(VMEM,) * 4,
        compiler_params=pltpu.CompilerParams(vmem_limit_bytes=60 * 1024 * 1024),
        name="split_z",
    )(place, part)


def after_z_kernel(own_in, gains_in, in1, in2, in3, ffn_in, ffn1, ffn2, ffn3, *refs):
    rows = own_in.shape[0]
    count = 4
    value = own_in[...]
    gains = gains_in[...]
    for ref in (in1, in2, in3):
        value = value + ref[:rows, :].astype(f32)
        gains = gains + decoded(ref[rows:, :])
    refs[-1][...] = gains
    first = 0
    for ref in refs[:count]:
        ref[...] = value[:, first : first + ref.shape[1]]
        first += ref.shape[1]
    first = 0
    for ref in refs[count:-1]:
        at = slice(first, first + ref.shape[1])
        total = ffn_in[:, at].astype(f32)
        for part in (ffn1, ffn2, ffn3):
            total = total + part[:, at].astype(f32)
        ref[...] = total
        first += ref.shape[1]


def after_z(own, gains, arrived, ffn_own, ffn_arrived, sizes, ffn_sizes):
    rows, columns = own.shape
    return pl.pallas_call(
        after_z_kernel,
        out_shape=tuple(shape((rows, size), f32) for size in sizes + ffn_sizes)
        + (shape(gains.shape, f32),),
        in_specs=[VMEM] * 9,
        out_specs=(VMEM,) * (len(sizes + ffn_sizes) + 1),
        compiler_params=pltpu.CompilerParams(vmem_limit_bytes=60 * 1024 * 1024),
        name="after_z",
    )(own, gains, *arrived, ffn_own, *ffn_arrived)


def last_gains_kernel(part0, part1, part2, part3, attn_ref, ffn_ref, query_ref, key_ref):
    total = part0[...] + part1[...] + part2[...] + part3[...]
    flat = jnp.concatenate([total[row : row + 1, :] for row in range(4)], axis=1)
    width = attn_ref.shape[1]
    attn_ref[...] = flat[:, :width]
    ffn_ref[...] = flat[:, width : 2 * width]
    first = 2 * width
    for ref, heads in ((query_ref, 4), (key_ref, 2)):
        ref[...] = sum(flat[:, first + h * HD : first + (h + 1) * HD] for h in range(heads))
        first += heads * HD


def last_gains(parts, width):
    return pl.pallas_call(
        last_gains_kernel,
        out_shape=(shape((1, width), f32),) * 2 + (shape((1, HD), f32),) * 2,
        in_specs=[VMEM] * 4,
        out_specs=(VMEM,) * 4,
        name="last_gains",
    )(*parts)


def out_ffn_kernel(
    y_ref, mixed0, mixed1, mixed2, mixed3, tokens_ref, weights_hbm, gain_ref, cot_ref,
    middle_ref, ffn_in_ref, acts_ref, back0, back1, back2, back3, out_ref,
    weights, mixed_all, middle_all, back_all, sems,
):
    length, width = tokens_ref.shape
    ff = acts_ref.shape[1] // 3
    block = length // FOUR
    tile = 256
    whole_tiles = ff // tile
    rest = ff - whole_tiles * tile

    def part(first, size, sem):
        columns = pl.ds(first, size)
        return pltpu.make_async_copy(
            weights_hbm.at[:, columns], weights.at[:, columns], sems.at[sem]
        )

    def tile_parts(i):
        size = tile if i < whole_tiles else rest
        return [part(k * ff + i * tile, size, 3 * i + k) for k in range(3)]

    tiles = whole_tiles + (1 if rest else 0)
    out_part = part(3 * ff, width, 3 * tiles)
    out_part.start()
    for i in range(tiles):
        for copy in tile_parts(i):
            copy.start()

    for j, ref in enumerate((mixed0, mixed1, mixed2, mixed3)):
        cols = ref.shape[1]
        mixed_all[:, j * cols : (j + 1) * cols] = ref[...]
    out_part.wait()

    def out_tile(n, carry):
        columns = pl.ds(pl.multiple_of(n * tile, tile), tile)
        w = weights[columns, 3 * ff : 3 * ff + width]
        middle_all[:, columns] = tokens_ref[:, columns].astype(f32) + dot_nt(mixed_all[...], w)
        return carry

    lax.fori_loop(0, width // tile, out_tile, 0)
    middle = middle_all[...]
    inverse = lax.rsqrt(jnp.mean(middle * middle, axis=-1, keepdims=True) + epsilon)
    ffn_in_ref[...] = (middle * inverse * gain_ref[...]).astype(bf16)
    y = y_ref[0]
    middle_ref[...] = middle_all[pl.ds(pl.multiple_of(y * block, block), block), :]

    def hidden_tile(first, size):
        def column(k):
            return pl.ds(pl.multiple_of(k * ff + first, 128), size)

        gate = dot_nn(ffn_in_ref[...], weights[:, column(0)])
        up = dot_nn(ffn_in_ref[...], weights[:, column(1)])
        grad_hidden = dot_nn(cot_ref[...], weights[:, column(2)])
        sig = jax.nn.sigmoid(gate)
        silu = gate * sig
        acts_ref[:, column(0)] = (
            grad_hidden * up * sig * (1.0 + gate * (1.0 - sig))
        ).astype(bf16)
        acts_ref[:, column(1)] = (grad_hidden * silu).astype(bf16)
        acts_ref[:, column(2)] = (silu * up).astype(bf16)

    for i in range(tiles):
        for copy in tile_parts(i):
            copy.wait()
        hidden_tile(i * tile, tile if i < whole_tiles else rest)

    def back_tile(n, carry):
        rows = pl.ds(pl.multiple_of(n * tile, tile), tile)
        back = dot_nt(acts_ref[:, : 2 * ff], weights[rows, : 2 * ff]).astype(bf16)
        for i in range(FOUR):
            back_all[mod4(i - y), :, rows] = back[i * block : (i + 1) * block, :]
        out = dot_nt(acts_ref[:, 2 * ff :], weights[rows, 2 * ff : 3 * ff]).astype(bf16)
        for i in range(FOUR):
            out_ref[mod4(i - y), :, rows] = out[i * block : (i + 1) * block, :]
        return carry

    lax.fori_loop(0, width // tile, back_tile, 0)
    for j, ref in enumerate((back0, back1, back2, back3)):
        ref[...] = back_all[j]


def out_ffn(mixed_parts, tokens_all, weights, gain, cot):
    length, width = tokens_all.shape
    ff = (weights.shape[1] - width) // 3
    vmem = pl.BlockSpec(memory_space=pltpu.VMEM)
    return pl.pallas_call(
        out_ffn_kernel,
        out_shape=(
            shape((length // FOUR, width), f32),
            shape((length, width), bf16),
            shape((length, 3 * ff), bf16),
        )
        + (shape((length // FOUR, width), bf16),) * 4
        + (shape((FOUR, length // FOUR, width), bf16),),
        in_specs=[pl.BlockSpec(memory_space=pltpu.SMEM)] + [vmem] * 5 + [pl.BlockSpec(memory_space=pl.ANY)] + [vmem] * 2,
        out_specs=(vmem,) * 8,
        scratch_shapes=[
            pltpu.VMEM(weights.shape, bf16),
            pltpu.VMEM((length, width), bf16),
            pltpu.VMEM((length, width), f32),
            pltpu.VMEM((FOUR, length // FOUR, width), bf16),
            pltpu.SemaphoreType.DMA((3 * (-(-ff // 256)) + 1,)),
        ],
        compiler_params=pltpu.CompilerParams(vmem_limit_bytes=60 * 1024 * 1024),
        cost_estimate=pl.CostEstimate(
            flops=2 * length * width * (6 * ff + width),
            bytes_accessed=2 * weights.size + 14 * length * width,
            transcendentals=length * ff,
        ),
        name="out_ffn",
    )(lax.axis_index("y").astype(jnp.int32).reshape(1), *mixed_parts, tokens_all, weights, gain.reshape(1, -1), cot)


def ffn_grads_kernel(ffn_in_ref, cot_ref, acts_ref, grads_ref, in_t, cot_t):
    rows = ffn_in_ref.shape[1]
    ff = acts_ref.shape[1] // 3
    step = 32
    for source, target in ((ffn_in_ref, in_t), (cot_ref, cot_t)):
        turned = source[...].T
        for x in range(rows // (8 * step)):
            for z in range(FOUR):
                for core in range(2):
                    old = ((x * FOUR + z) * 2 + core) * step
                    new = ((x * 2 + core) * FOUR + z) * step
                    target[new : new + step, :] = turned[old : old + step, :]
    tile = 256
    for first in range(0, 3 * ff, tile):
        size = min(tile, 3 * ff - first)
        left = in_t if first < 2 * ff else cot_t
        grads_ref[:, first : first + size] = dot_nn(
            left[...], acts_ref[:, first : first + size]
        ).astype(bf16)


def ffn_grads(ffn_in, cot, acts):
    length, width = ffn_in.shape
    columns = acts.shape[1]
    half = width // 4
    return pl.pallas_call(
        ffn_grads_kernel,
        grid=(4,),
        out_shape=jax.ShapeDtypeStruct((width, columns), bf16),
        in_specs=[
            pl.BlockSpec((length, half), lambda i: (0, i)),
            pl.BlockSpec((length, half), lambda i: (0, i)),
            pl.BlockSpec((length, columns), lambda i: (0, 0)),
        ],
        out_specs=pl.BlockSpec((half, columns), lambda i: (i, 0)),
        scratch_shapes=[pltpu.VMEM((half, length), bf16), pltpu.VMEM((half, length), bf16)],
        compiler_params=pltpu.CompilerParams(vmem_limit_bytes=60 * 1024 * 1024),
        cost_estimate=pl.CostEstimate(
            flops=2 * length * width * columns,
            bytes_accessed=2 * (2 * length * width + length * columns + width * columns),
            transcendentals=0,
        ),
        name="ffn_grads",
    )(ffn_in, cot, acts)


def local(
    tokens,
    segments,
    query_weight,
    key_weight,
    value_weight,
    out_weight,
    gate_weight,
    up_weight,
    down_weight,
    attn_gain,
    ffn_gain,
    query_gain,
    key_gain,
    cotangent,
):
    dp = ("x", "z", "c")
    length = segments.shape[0]
    block = length // FOUR
    query_cols = query_weight.shape[1]
    kv_cols = key_weight.shape[1]
    ff_cols = gate_weight.shape[1]
    qkv_cols = query_cols + 2 * kv_cols
    place = jnp.stack([lax.axis_index(axis) for axis in ("x", "z", "c", "y")]).astype(jnp.int32)

    own, other = gather_dp_blocks(pack_columns([query_weight, key_weight, value_weight]))
    large_shard = pack_columns([gate_weight, up_weight, down_weight.T] + gather_y(out_weight.T))
    large_full = lax.all_gather(large_shard, dp, axis=0, tiled=True)
    full_out_t = large_full[:, 3 * ff_cols : 3 * ff_cols + query_cols]

    token_parts = gather_y(jnp.concatenate([tokens, cotangent], axis=0))
    grad_out_all = order_rows(token_parts, block)
    cosine, sine = rope_tables(doc_positions(segments))
    repeats = (query_cols + kv_cols) // HD
    cosine, sine = jnp.tile(cosine, (1, repeats)), jnp.tile(sine, (1, repeats))
    head_gain = jnp.concatenate(
        [query_gain] * (query_cols // HD) + [key_gain] * (kv_cols // HD)
    ).reshape(1, -1)
    tokens_all, full_qkv, normed_t, proj, rot, value, probs, mixed = attention(
        place, block, token_parts, own, other, cosine, sine, segments, attn_gain.reshape(1, -1), head_gain
    )
    middle, ffn_all, acts, *ffn_back, ffn_out = out_ffn(
        gather_y(mixed), tokens_all, large_full, ffn_gain, grad_out_all
    )
    arrived = [ffn_back[0]] + [shift(ffn_back[j], "y", j) for j in (1, 2, 3)]
    ffn_sums, arrived = lax.optimization_barrier((ffn_grads(ffn_all, grad_out_all, acts), arrived))
    grad_ffn_in = sum(part.astype(f32) for part in arrived)
    ffn_part = lax.psum_scatter(ffn_sums, ("x", "c"), scatter_dimension=0, tiled=True)
    ffn_inv = inverse_rms(middle)
    grad_through = norm_back_value(middle, ffn_inv, ffn_gain, grad_ffn_in)
    ffn_gain_part = jnp.sum(grad_ffn_in * middle * ffn_inv, axis=0)
    grad_middle = cotangent.astype(f32) + grad_through
    gm_parts = gather_y(grad_middle.astype(bf16))
    width = tokens.shape[1]
    theirs, mine, *messages, gains = attention_back(
        place, gm_parts, full_out_t, full_qkv, tokens_all, proj, rot, value, probs, cosine, sine,
        head_gain, ffn_gain_part.reshape(1, -1), ffn_out, normed_t, mixed,
    )
    arrived = shift(theirs, "c", 1, 2)
    back_parts = [messages[0]] + [shift(messages[j], "y", j) for j in (1, 2, 3)]
    own_rows, gains, *outgoing = after_core(place, mine, arrived, gains)
    arrived = [shift(part, "x", j + 1) for j, part in enumerate(outgoing)]
    ffn_own, *ffn_pieces = split_z(place, ffn_part)
    ffn_pieces, own_rows = lax.optimization_barrier((ffn_pieces, own_rows))
    ffn_arrived = [shift(part, "z", j + 1) for j, part in enumerate(ffn_pieces)]
    own_rows, gains, *outgoing = after_x(place, own_rows, gains, arrived)
    arrived = [shift(part, "z", j + 1) for j, part in enumerate(outgoing)]
    back_parts, ffn_arrived, arrived = lax.optimization_barrier((back_parts, ffn_arrived, arrived))
    *weight_grads, gains = after_z(
        own_rows, gains, arrived, ffn_own, ffn_arrived,
        (query_cols, kv_cols, kv_cols, query_cols), (ff_cols,) * 3,
    )
    grad_query_weight, grad_key_weight, grad_value_weight, grad_out_t = weight_grads[:4]
    grad_gate_weight, grad_up_weight, grad_down_t = weight_grads[4:]
    grad_out_weight = grad_out_t.T
    grad_down_weight = grad_down_t.T
    gain_grads = last_gains(gather_y(gains), width)

    sums = sum(part.astype(f32) for part in back_parts)
    result = (middle + sums[block:]).astype(bf16)
    own_tokens = tokens.astype(f32)
    grad_input = norm_back_value(own_tokens, inverse_rms(own_tokens), attn_gain, sums[:block])
    grad_tokens = (grad_middle + grad_input).astype(bf16)
    return (
        result,
        grad_tokens,
        grad_query_weight,
        grad_key_weight,
        grad_value_weight,
        grad_out_weight,
        grad_gate_weight,
        grad_up_weight,
        grad_down_weight,
        *[gain.reshape(-1) for gain in gain_grads],
    )


def solution(mesh):
    axes = Mesh(mesh.devices.reshape(4, 4, 2, 4), ("x", "z", "c", "y"))
    dp = ("x", "z", "c")
    rows = P(("x", "z", "c", "y"), None)
    placed = (
        rows,
        P(dp),
        P(dp, "y"),
        P(dp, "y"),
        P(dp, "y"),
        P("y", dp),
        P(dp, "y"),
        P(dp, "y"),
        P("y", dp),
        P(),
        P(),
        P(),
        P(),
        rows,
    )
    return jax.shard_map(
        local,
        mesh=axes,
        in_specs=placed,
        out_specs=(
            rows,
            rows,
            P(dp, "y"),
            P(dp, "y"),
            P(dp, "y"),
            P("y", dp),
            P(dp, "y"),
            P(dp, "y"),
            P("y", dp),
            P(),
            P(),
            P(),
            P(),
        ),
        check_vma=False,
    )
```

```python
import math

import jax
import jax.numpy as jnp
from jax import lax
from jax.experimental import pallas as pl
from jax.experimental.pallas import tpu as pltpu
from jax.sharding import Mesh, PartitionSpec as P

HD = 64
FOUR = 4

epsilon = 1e-05
rope_base = 1000000.0
masked_score = -1e30

bf16 = jnp.bfloat16
f32 = jnp.float32


def dot_nn(left, right):
    return lax.dot_general(left, right, (((1,), (0,)), ((), ())), preferred_element_type=f32)


def dot_nt(left, right):
    return lax.dot_general(left, right, (((1,), (1,)), ((), ())), preferred_element_type=f32)


def dot_tn(left, right):
    return lax.dot_general(left, right, (((0,), (0,)), ((), ())), preferred_element_type=f32)


def inverse_rms(value):
    return lax.rsqrt(jnp.mean(value * value, axis=-1, keepdims=True) + epsilon)


def norm_back_value(value, inverse, norm_gain, incoming):
    scaled = incoming * norm_gain
    average = jnp.mean(value * scaled, axis=-1, keepdims=True)
    return inverse * scaled - value * (inverse * inverse * inverse) * average


def doc_positions(segment_ids):
    length = segment_ids.shape[0]
    indices = jnp.arange(length, dtype=jnp.int32)
    begins = jnp.concatenate([jnp.ones((1,), dtype=jnp.bool_), segment_ids[1:] != segment_ids[:-1]])
    starts = lax.cummax(jnp.where(begins, indices, jnp.zeros_like(indices)), axis=0)
    return indices - starts


def rope_tables(positions):
    half_dim = HD // 2
    exponents = jnp.arange(half_dim, dtype=f32) * (2.0 / HD)
    frequency = jnp.exp(-math.log(rope_base) * exponents)
    angles = positions.astype(f32)[:, None] * frequency[None, :]
    cosine, sine = jnp.cos(angles), jnp.sin(angles)
    return (
        jnp.concatenate([cosine, cosine], axis=1),
        jnp.concatenate([-sine, sine], axis=1),
    )


def shift(value, axis, distance, size=FOUR):
    return lax.ppermute(value, axis, [(i, (i + distance) % size) for i in range(size)])


def gather_y(block):
    return [block] + [shift(block, "y", -j) for j in (1, 2, 3)]


def scatter_sum_y(blocks):
    total = blocks[0].astype(f32)
    for arrived in [shift(blocks[j].astype(bf16), "y", j) for j in (1, 2, 3)]:
        total = total + arrived.astype(f32)
    return total


def mod4(value):
    return lax.rem(value + FOUR, FOUR)


def gather_dp_blocks(shard):
    along_x = jnp.stack([shard] + [shift(shard, "x", -j) for j in (1, 2, 3)])
    along_z = jnp.stack([along_x] + [shift(along_x, "z", -j) for j in (1, 2, 3)])
    return along_z, shift(along_z, "c", 1, 2)


def pack_kernel(*refs):
    out_ref = refs[-1]
    first = 0
    for ref in refs[:-1]:
        out_ref[:, first : first + ref.shape[1]] = ref[...]
        first += ref.shape[1]


def pack_columns(parts):
    vmem = pl.BlockSpec(memory_space=pltpu.VMEM)
    return pl.pallas_call(
        pack_kernel,
        out_shape=jax.ShapeDtypeStruct(
            (parts[0].shape[0], sum(part.shape[1] for part in parts)), parts[0].dtype
        ),
        in_specs=[vmem] * len(parts),
        out_specs=vmem,
        name="pack_columns",
    )(*parts)


def order_rows_kernel(y_ref, part0, part1, part2, part3, out_ref):
    for j, part in enumerate((part0, part1, part2, part3)):
        out_ref[mod4(y_ref[0] + j)] = part[part.shape[0] - out_ref.shape[1] :, :]


def order_rows(parts, rows):
    columns = parts[0].shape[1]
    y = lax.axis_index("y").astype(jnp.int32).reshape(1)
    vmem = pl.BlockSpec(memory_space=pltpu.VMEM)
    return pl.pallas_call(
        order_rows_kernel,
        out_shape=jax.ShapeDtypeStruct((FOUR, rows, columns), parts[0].dtype),
        in_specs=[pl.BlockSpec(memory_space=pltpu.SMEM)] + [vmem] * 4,
        out_specs=vmem,
        compiler_params=pltpu.CompilerParams(vmem_limit_bytes=60 * 1024 * 1024),
        name="order_rows",
    )(y, *parts).reshape(FOUR * rows, columns)


VMEM = pl.BlockSpec(memory_space=pltpu.VMEM)
ANY = pl.BlockSpec(memory_space=pl.ANY)
SMEM = pl.BlockSpec(memory_space=pltpu.SMEM)
shape = jax.ShapeDtypeStruct


def head_mean(value):
    width = value.shape[1]
    row = lax.broadcasted_iota(jnp.int32, (width, width), 0) // HD
    column = lax.broadcasted_iota(jnp.int32, (width, width), 1) // HD
    ones = jnp.where(row == column, 1.0 / HD, 0.0)
    return lax.dot_general(
        value,
        ones,
        (((1,), (0,)), ((), ())),
        precision=lax.Precision.HIGHEST,
        preferred_element_type=f32,
    )


def swap_halves(value):
    width = value.shape[1]
    lane = lax.broadcasted_iota(jnp.int32, value.shape, 1)
    ahead = pltpu.roll(value, width - HD // 2, 1)
    behind = pltpu.roll(value, HD // 2, 1)
    return jnp.where(lane % HD < HD // 2, ahead, behind)


def by_core(turned, target):
    step = 32
    for i in range(turned.shape[0] // step):
        first = (i // 2) * step
        target[i % 2, first : first + step, :] = turned[i * step : (i + 1) * step, :]


def attention_kernel(
    place_ref, tok0, tok1, tok2, tok3, own_ref, other_ref, cos_ref, sin_ref, id_col, id_row,
    gain_ref, head_gain_ref,
    tokens_ref, weights_ref, normed_t_ref, proj_ref, rot_ref, value_ref, probs_ref, mixed_ref,
    normed_ref,
):
    x, z, core, y = place_ref[0], place_ref[1], place_ref[2], place_ref[3]
    length, width = tokens_ref.shape
    block = length // FOUR
    for j, part in enumerate((tok0, tok1, tok2, tok3)):
        rows = pl.ds(pl.multiple_of(mod4(y + j) * block, block), block)
        tokens_ref[rows, :] = part[:block, :]
    for i in range(FOUR):
        for k in range(FOUR):
            from_x, from_z = mod4(i - x), mod4(k - z)
            weights_ref[i, k, core] = own_ref[from_z, from_x]
            weights_ref[i, k, 1 - core] = other_ref[from_z, from_x]
    tokens = tokens_ref[...].astype(f32)
    normed_ref[...] = (tokens * inverse_rms(tokens) * gain_ref[...]).astype(bf16)
    by_core(normed_ref[...].T, normed_t_ref)
    columns = weights_ref.shape[-1]
    projected = dot_nn(normed_ref[...], weights_ref[...].reshape(width, columns))
    heads = proj_ref.shape[1]
    both = projected[:, :heads]
    proj_ref[...] = both
    value_ref[...] = projected[:, heads:].astype(bf16)
    normal = both * lax.rsqrt(head_mean(both * both) + epsilon) * head_gain_ref[...]
    rot_ref[...] = (normal * cos_ref[...] + swap_halves(normal) * sin_ref[...]).astype(bf16)
    query_cols = mixed_ref.shape[1]
    groups = value_ref.shape[1] // HD
    per_group = query_cols // HD // groups
    index = lax.broadcasted_iota(jnp.int32, (length, length), 0)
    other = lax.broadcasted_iota(jnp.int32, (length, length), 1)
    allowed = (index >= other) & (id_col[...] == id_row[...])
    for g in range(groups):
        key = rot_ref[:, query_cols + g * HD : query_cols + (g + 1) * HD]
        value = value_ref[:, g * HD : (g + 1) * HD]
        for h in range(g * per_group, (g + 1) * per_group):
            scores = dot_nt(rot_ref[:, h * HD : (h + 1) * HD], key) * (1.0 / math.sqrt(HD))
            scores = jnp.where(allowed, scores, masked_score)
            exponent = jnp.exp(scores - jnp.max(scores, axis=-1, keepdims=True))
            probs = (exponent * (1.0 / jnp.sum(exponent, axis=-1, keepdims=True))).astype(bf16)
            probs_ref[h] = probs
            mixed_ref[:, h * HD : (h + 1) * HD] = dot_nn(probs, value).astype(bf16)


def attention(place, rows, token_parts, own, other, cos, sin, ids, gain, head_gain):
    width = token_parts[0].shape[1]
    length = FOUR * rows
    heads = head_gain.shape[1]
    columns = own.shape[-1]
    values = columns - heads
    queries = heads - values
    return pl.pallas_call(
        attention_kernel,
        out_shape=(
            shape((length, width), bf16),
            shape((FOUR, FOUR, 2, own.shape[2], columns), bf16),
            shape((2, width // 2, length), bf16),
            shape((length, heads), f32),
            shape((length, heads), bf16),
            shape((length, values), bf16),
            shape((queries // HD, length, length), bf16),
            shape((length, queries), bf16),
        ),
        in_specs=[SMEM] + [VMEM] * 12,
        out_specs=(VMEM,) * 8,
        scratch_shapes=[pltpu.VMEM((length, width), bf16)],
        compiler_params=pltpu.CompilerParams(vmem_limit_bytes=60 * 1024 * 1024),
        cost_estimate=pl.CostEstimate(
            flops=2 * length * (width * columns + 2 * length * queries),
            bytes_accessed=8 * 1024 * 1024,
            transcendentals=length * length * queries // HD,
        ),
        name="attention",
    )(place, *token_parts, own, other, cos, sin, ids.reshape(-1, 1), ids.reshape(1, -1), gain, head_gain)


def attention_back_kernel(
    place_ref, gm0, gm1, gm2, gm3, out_t_ref, weights_hbm, tokens_hbm, proj_ref, rot_ref, value_ref,
    probs_ref, cos_ref, sin_ref, head_gain_ref, ffn_gain_ref, ffn_out_hbm, normed_t_hbm, mixed_ref,
    theirs_ref, mine_ref, message0, message1, message2, message3, gains_ref,
    turned_key, turned_value, grad_rot, gm_ref, grad_ref, gm_t, back_all,
    weights_ref, tokens_ref, ffn_out_ref, normed_t_ref, sems,
):
    late = [
        pltpu.make_async_copy(source, target, sems.at[i])
        for i, (source, target) in enumerate(
            (
                (weights_hbm, weights_ref),
                (tokens_hbm, tokens_ref),
                (ffn_out_hbm, ffn_out_ref),
                (normed_t_hbm, normed_t_ref),
            )
        )
    ]
    for copy in late:
        copy.start()
    y = place_ref[3]
    length, width = tokens_ref.shape
    block = length // FOUR
    heads = proj_ref.shape[1]
    for j, part in enumerate((gm0, gm1, gm2, gm3)):
        rows = pl.ds(pl.multiple_of(mod4(y + j) * block, block), block)
        gm_ref[rows, :] = part[...]
    scale = 1.0 / math.sqrt(HD)
    query_cols = out_t_ref.shape[1]
    groups = value_ref.shape[1] // HD
    per_group = query_cols // HD // groups
    grad_mixed = dot_nn(gm_ref[...], out_t_ref[...]).astype(bf16)
    grad_mixed_t = grad_mixed.T
    query_t = rot_ref[:, :query_cols].T
    for g in range(groups):
        key = rot_ref[:, query_cols + g * HD : query_cols + (g + 1) * HD]
        value = value_ref[:, g * HD : (g + 1) * HD]
        key_sum = jnp.zeros((HD, length), f32)
        value_sum = jnp.zeros((HD, length), f32)
        for h in range(g * per_group, (g + 1) * per_group):
            columns = slice(h * HD, (h + 1) * HD)
            probs = probs_ref[h]
            wide = probs.astype(f32)
            grad_probs = dot_nt(grad_mixed[:, columns], value)
            delta = jnp.sum(wide * grad_probs, axis=-1, keepdims=True)
            grad_scores = (wide * (grad_probs - delta)).astype(bf16)
            grad_rot[:, columns] = dot_nn(grad_scores, key) * scale
            key_sum = key_sum + dot_nn(query_t[columns, :], grad_scores)
            value_sum = value_sum + dot_nn(grad_mixed_t[columns, :], probs)
        turned_key[g * HD : (g + 1) * HD, :] = key_sum * scale
        turned_value[g * HD : (g + 1) * HD, :] = value_sum
    grad_rot[:, query_cols:] = turned_key[...].T
    grad_ref[:, heads:] = turned_value[...].T.astype(bf16)
    incoming = grad_rot[...]
    normal = incoming * cos_ref[...] - swap_halves(incoming) * sin_ref[...]
    both = proj_ref[...]
    inverse = lax.rsqrt(head_mean(both * both) + epsilon)
    scaled = normal * head_gain_ref[...]
    grad = inverse * scaled - both * (inverse * inverse * inverse) * head_mean(both * scaled)
    grad_ref[:, :heads] = grad.astype(bf16)
    head_part = jnp.sum(normal * both * inverse, axis=0, keepdims=True)

    for copy in late:
        copy.wait()
    tokens = tokens_ref[...].astype(f32)
    token_inverse = inverse_rms(tokens)
    weights = weights_ref[...].reshape(width, -1)
    tile = 256
    part = []
    for n in range(width // tile):
        columns = slice(n * tile, (n + 1) * tile)
        back = dot_nt(grad_ref[...], weights[columns, :])
        part.append(jnp.sum(back * (tokens[:, columns] * token_inverse), axis=0, keepdims=True))
        back = back.astype(bf16)
        for i in range(FOUR):
            back_all[mod4(i - y), :, columns] = back[i * block : (i + 1) * block, :]
    for j, ref in enumerate((message0, message1, message2, message3)):
        ref[:block, :] = back_all[j]
        ref[block:, :] = ffn_out_ref[j]
    flat = jnp.concatenate(part + [ffn_gain_ref[...], head_part], axis=1)
    gains_ref[...] = jnp.zeros_like(gains_ref)
    line = gains_ref.shape[1]
    for row in range(-(-flat.shape[1] // line)):
        size = min(line, flat.shape[1] - row * line)
        gains_ref[row : row + 1, :size] = flat[:, row * line : row * line + size]

    core = place_ref[2]
    by_core(gm_ref[...].T, gm_t)
    columns = grad_ref.shape[1]
    for which, ref in ((1 - core, theirs_ref), (core, mine_ref)):
        rows = mine_ref.shape[0]
        ref[:rows, :columns] = dot_nn(normed_t_ref[which], grad_ref[...]).astype(bf16)
        ref[:rows, columns:] = dot_nn(gm_t[which], mixed_ref[...]).astype(bf16)
    theirs_ref[mine_ref.shape[0] :, :] = coded(gains_ref[...])


def attention_back(
    place, gm_parts, out_t, weights, tokens, proj, rot, value, probs, cos, sin, head_gain, ffn_gain_part,
    ffn_out, normed_t, mixed,
):
    length, width = tokens.shape
    heads = proj.shape[1]
    values = value.shape[1]
    line = heads + values + mixed.shape[1]
    return pl.pallas_call(
        attention_back_kernel,
        out_shape=(
            shape((width // 2 + 16, line), bf16),
            shape((width // 2, line), bf16),
        )
        + (shape((length // 2, width), bf16),) * 4
        + (shape((8, line), f32),),
        in_specs=[SMEM] + [VMEM] * 5 + [ANY] * 2 + [VMEM] * 8 + [ANY] * 2 + [VMEM],
        out_specs=(VMEM,) * 7,
        scratch_shapes=[
            pltpu.VMEM((values, length), f32),
            pltpu.VMEM((values, length), f32),
            pltpu.VMEM((length, heads), f32),
            pltpu.VMEM((length, width), bf16),
            pltpu.VMEM((length, heads + values), bf16),
            pltpu.VMEM((2, width // 2, length), bf16),
            pltpu.VMEM((FOUR, length // FOUR, width), bf16),
            pltpu.VMEM(weights.shape, bf16),
            pltpu.VMEM((length, width), bf16),
            pltpu.VMEM(ffn_out.shape, bf16),
            pltpu.VMEM(normed_t.shape, bf16),
            pltpu.SemaphoreType.DMA((4,)),
        ],
        compiler_params=pltpu.CompilerParams(vmem_limit_bytes=60 * 1024 * 1024),
        cost_estimate=pl.CostEstimate(
            flops=10**11,
            bytes_accessed=16 * 1024 * 1024,
            transcendentals=0,
        ),
        name="attention_back",
    )(
        place, *gm_parts, out_t, weights, tokens, proj, rot, value, probs, cos, sin, head_gain,
        ffn_gain_part, ffn_out, normed_t, mixed,
    )


def coded(value):
    high = value.astype(bf16).astype(f32)
    return jnp.concatenate([high, value - high], axis=0).astype(bf16)


def decoded(rows):
    wide = rows.astype(f32)
    return wide[:8] + wide[8:]


def after_core_kernel(
    place_ref, mine_ref, arrived_ref, gains_in,
    own_ref, gains_ref, out1, out2, out3,
):
    z = place_ref[1]
    rows = own_ref.shape[0]
    few = rows // FOUR

    def piece(j):
        parts = []
        for x in range(FOUR):
            at = pl.ds(pl.multiple_of(x * rows + mod4(z + j) * few, few), few)
            parts.append(mine_ref[at, :].astype(f32) + arrived_ref[at, :].astype(f32))
        return jnp.concatenate(parts, axis=0)

    gains = gains_in[...] + decoded(arrived_ref[FOUR * rows :, :])
    gains_ref[...] = gains
    own_ref[...] = piece(0)
    for j, ref in ((1, out1), (2, out2), (3, out3)):
        ref[:rows, :] = piece(j).astype(bf16)
        ref[rows:, :] = coded(gains)


def after_core(place, mine, arrived, gains):
    rows, columns = mine.shape
    rows = rows // FOUR
    return pl.pallas_call(
        after_core_kernel,
        out_shape=(shape((rows, columns), f32), shape((8, columns), f32))
        + (shape((rows + 16, columns), bf16),) * 3,
        in_specs=[SMEM] + [VMEM] * 3,
        out_specs=(VMEM,) * 5,
        compiler_params=pltpu.CompilerParams(vmem_limit_bytes=60 * 1024 * 1024),
        name="after_core",
    )(place, mine, arrived, gains)


def after_z_kernel(
    place_ref, own_in, gains_in, in1, in2, in3, own_ref, gains_ref, out1, out2, out3, total
):
    x = place_ref[0]
    rows = own_in.shape[0]
    value = own_in[...]
    gains = gains_in[...]
    for ref in (in1, in2, in3):
        value = value + ref[:rows, :].astype(f32)
        gains = gains + decoded(ref[rows:, :])
    total[...] = value
    gains_ref[...] = gains
    few = own_ref.shape[0]

    def piece(j):
        return total[pl.ds(pl.multiple_of(mod4(x + j) * few, few), few), :]

    own_ref[...] = piece(0)
    extra = coded(gains)
    for j, ref in ((1, out1), (2, out2), (3, out3)):
        ref[:few, :] = piece(j).astype(bf16)
        ref[few:, :] = extra


def after_z(place, own, gains, arrived):
    rows, columns = own.shape
    few = rows // FOUR
    return pl.pallas_call(
        after_z_kernel,
        out_shape=(shape((few, columns), f32), shape((8, columns), f32))
        + (shape((few + 16, columns), bf16),) * 3,
        in_specs=[SMEM] + [VMEM] * 5,
        out_specs=(VMEM,) * 5,
        scratch_shapes=[pltpu.VMEM((rows, columns), f32)],
        compiler_params=pltpu.CompilerParams(vmem_limit_bytes=60 * 1024 * 1024),
        name="after_z",
    )(place, own, gains, *arrived)


def split_z_kernel(place_ref, part_ref, *refs):
    rows = refs[0].shape[0]
    for j, ref in enumerate(refs):
        at = pl.multiple_of(mod4(place_ref[1] + j) * rows, rows)
        ref[...] = part_ref[pl.ds(at, rows), :]


def split_z(place, part):
    rows, columns = part.shape
    return pl.pallas_call(
        split_z_kernel,
        out_shape=(shape((rows // FOUR, columns), part.dtype),) * 4,
        in_specs=[SMEM, VMEM],
        out_specs=(VMEM,) * 4,
        compiler_params=pltpu.CompilerParams(vmem_limit_bytes=60 * 1024 * 1024),
        name="split_z",
    )(place, part)


def after_x_kernel(own_in, gains_in, in1, in2, in3, ffn_in, ffn1, ffn2, ffn3, *refs):
    rows = own_in.shape[0]
    count = 4
    value = own_in[...]
    gains = gains_in[...]
    for ref in (in1, in2, in3):
        value = value + ref[:rows, :].astype(f32)
        gains = gains + decoded(ref[rows:, :])
    refs[-1][...] = gains
    first = 0
    for ref in refs[:count]:
        ref[...] = value[:, first : first + ref.shape[1]]
        first += ref.shape[1]
    first = 0
    for ref in refs[count:-1]:
        at = slice(first, first + ref.shape[1])
        total = ffn_in[:, at].astype(f32)
        for part in (ffn1, ffn2, ffn3):
            total = total + part[:, at].astype(f32)
        ref[...] = total
        first += ref.shape[1]


def after_x(own, gains, arrived, ffn_own, ffn_arrived, sizes, ffn_sizes):
    rows, columns = own.shape
    return pl.pallas_call(
        after_x_kernel,
        out_shape=tuple(shape((rows, size), f32) for size in sizes + ffn_sizes)
        + (shape(gains.shape, f32),),
        in_specs=[VMEM] * 9,
        out_specs=(VMEM,) * (len(sizes + ffn_sizes) + 1),
        compiler_params=pltpu.CompilerParams(vmem_limit_bytes=60 * 1024 * 1024),
        name="after_x",
    )(own, gains, *arrived, ffn_own, *ffn_arrived)


def last_gains_kernel(part0, part1, part2, part3, attn_ref, ffn_ref, query_ref, key_ref):
    total = part0[...] + part1[...] + part2[...] + part3[...]
    flat = jnp.concatenate([total[row : row + 1, :] for row in range(4)], axis=1)
    width = attn_ref.shape[1]
    attn_ref[...] = flat[:, :width]
    ffn_ref[...] = flat[:, width : 2 * width]
    first = 2 * width
    for ref, heads in ((query_ref, 4), (key_ref, 2)):
        ref[...] = sum(flat[:, first + h * HD : first + (h + 1) * HD] for h in range(heads))
        first += heads * HD


def last_gains(parts, width):
    return pl.pallas_call(
        last_gains_kernel,
        out_shape=(shape((1, width), f32),) * 2 + (shape((1, HD), f32),) * 2,
        in_specs=[VMEM] * 4,
        out_specs=(VMEM,) * 4,
        name="last_gains",
    )(*parts)


def out_ffn_kernel(
    y_ref, mixed0, mixed1, mixed2, mixed3, tokens_ref, weights_hbm, gain_ref, cot_ref,
    middle_ref, ffn_in_hbm, acts_hbm, back0, back1, back2, back3, out_ref,
    weights, mixed_all, middle_all, back_all, ffn_in_ref, acts_ref, sems, leaving,
):
    length, width = tokens_ref.shape
    ff = acts_ref.shape[1] // 3
    block = length // FOUR
    tile = 256
    whole_tiles = ff // tile
    rest = ff - whole_tiles * tile

    def part(first, size, sem):
        columns = pl.ds(first, size)
        return pltpu.make_async_copy(
            weights_hbm.at[:, columns], weights.at[:, columns], sems.at[sem]
        )

    def tile_parts(i):
        size = tile if i < whole_tiles else rest
        return [part(k * ff + i * tile, size, 3 * i + k) for k in range(3)]

    tiles = whole_tiles + (1 if rest else 0)
    out_part = part(3 * ff, width, 3 * tiles)
    out_part.start()
    for i in range(tiles):
        for copy in tile_parts(i):
            copy.start()

    for j, ref in enumerate((mixed0, mixed1, mixed2, mixed3)):
        cols = ref.shape[1]
        mixed_all[:, j * cols : (j + 1) * cols] = ref[...]
    out_part.wait()

    def out_tile(n, carry):
        columns = pl.ds(pl.multiple_of(n * tile, tile), tile)
        w = weights[columns, 3 * ff : 3 * ff + width]
        middle_all[:, columns] = tokens_ref[:, columns].astype(f32) + dot_nt(mixed_all[...], w)
        return carry

    lax.fori_loop(0, width // tile, out_tile, 0)
    middle = middle_all[...]
    inverse = lax.rsqrt(jnp.mean(middle * middle, axis=-1, keepdims=True) + epsilon)
    ffn_in_ref[...] = (middle * inverse * gain_ref[...]).astype(bf16)
    y = y_ref[0]
    results = [pltpu.make_async_copy(ffn_in_ref, ffn_in_hbm, leaving.at[3 * tiles])]
    results[0].start()
    middle_ref[...] = middle_all[pl.ds(pl.multiple_of(y * block, block), block), :]

    def hidden_tile(first, size):
        def column(k):
            return pl.ds(pl.multiple_of(k * ff + first, 128), size)

        gate = dot_nn(ffn_in_ref[...], weights[:, column(0)])
        up = dot_nn(ffn_in_ref[...], weights[:, column(1)])
        grad_hidden = dot_nn(cot_ref[...], weights[:, column(2)])
        sig = jax.nn.sigmoid(gate)
        silu = gate * sig
        acts_ref[:, column(0)] = (
            grad_hidden * up * sig * (1.0 + gate * (1.0 - sig))
        ).astype(bf16)
        acts_ref[:, column(1)] = (grad_hidden * silu).astype(bf16)
        acts_ref[:, column(2)] = (silu * up).astype(bf16)

    for i in range(tiles):
        for copy in tile_parts(i):
            copy.wait()
        size = tile if i < whole_tiles else rest
        hidden_tile(i * tile, size)
        for k in range(3):
            columns = pl.ds(k * ff + i * tile, size)
            copy = pltpu.make_async_copy(
                acts_ref.at[:, columns], acts_hbm.at[:, columns], leaving.at[3 * i + k]
            )
            copy.start()
            results.append(copy)

    def back_tile(n, carry):
        rows = pl.ds(pl.multiple_of(n * tile, tile), tile)
        back = dot_nt(acts_ref[:, : 2 * ff], weights[rows, : 2 * ff]).astype(bf16)
        for i in range(FOUR):
            back_all[mod4(i - y), :, rows] = back[i * block : (i + 1) * block, :]
        out = dot_nt(acts_ref[:, 2 * ff :], weights[rows, 2 * ff : 3 * ff]).astype(bf16)
        for i in range(FOUR):
            out_ref[mod4(i - y), :, rows] = out[i * block : (i + 1) * block, :]
        return carry

    lax.fori_loop(0, width // tile, back_tile, 0)
    for j, ref in enumerate((back0, back1, back2, back3)):
        ref[...] = back_all[j]
    for copy in results:
        copy.wait()


def out_ffn(mixed_parts, tokens_all, weights, gain, cot):
    length, width = tokens_all.shape
    ff = (weights.shape[1] - width) // 3
    vmem = pl.BlockSpec(memory_space=pltpu.VMEM)
    return pl.pallas_call(
        out_ffn_kernel,
        out_shape=(
            shape((length // FOUR, width), f32),
            shape((length, width), bf16),
            shape((length, 3 * ff), bf16),
        )
        + (shape((length // FOUR, width), bf16),) * 4
        + (shape((FOUR, length // FOUR, width), bf16),),
        in_specs=[pl.BlockSpec(memory_space=pltpu.SMEM)] + [vmem] * 5 + [pl.BlockSpec(memory_space=pl.ANY)] + [vmem] * 2,
        out_specs=(vmem,) + (pl.BlockSpec(memory_space=pl.ANY),) * 2 + (vmem,) * 5,
        scratch_shapes=[
            pltpu.VMEM(weights.shape, bf16),
            pltpu.VMEM((length, width), bf16),
            pltpu.VMEM((length, width), f32),
            pltpu.VMEM((FOUR, length // FOUR, width), bf16),
            pltpu.VMEM((length, width), bf16),
            pltpu.VMEM((length, 3 * ff), bf16),
            pltpu.SemaphoreType.DMA((3 * (-(-ff // 256)) + 1,)),
            pltpu.SemaphoreType.DMA((3 * (-(-ff // 256)) + 1,)),
        ],
        compiler_params=pltpu.CompilerParams(vmem_limit_bytes=60 * 1024 * 1024),
        cost_estimate=pl.CostEstimate(
            flops=2 * length * width * (6 * ff + width),
            bytes_accessed=2 * weights.size + 14 * length * width,
            transcendentals=length * ff,
        ),
        name="out_ffn",
    )(lax.axis_index("y").astype(jnp.int32).reshape(1), *mixed_parts, tokens_all, weights, gain.reshape(1, -1), cot)


def ffn_grads_kernel(ffn_in_ref, cot_ref, acts_ref, grads_ref, in_t, cot_t):
    rows = ffn_in_ref.shape[1]
    ff = acts_ref.shape[1] // 3
    step = 32
    for source, target in ((ffn_in_ref, in_t), (cot_ref, cot_t)):
        turned = source[...].T
        for x in range(rows // (8 * step)):
            for z in range(FOUR):
                for core in range(2):
                    old = ((x * FOUR + z) * 2 + core) * step
                    new = ((x * 2 + core) * FOUR + z) * step
                    target[new : new + step, :] = turned[old : old + step, :]
    tile = 256
    for first in range(0, 3 * ff, tile):
        size = min(tile, 3 * ff - first)
        left = in_t if first < 2 * ff else cot_t
        grads_ref[:, first : first + size] = dot_nn(
            left[...], acts_ref[:, first : first + size]
        ).astype(bf16)


def ffn_grads(ffn_in, cot, acts):
    length, width = ffn_in.shape
    columns = acts.shape[1]
    half = width // 4
    return pl.pallas_call(
        ffn_grads_kernel,
        grid=(4,),
        out_shape=jax.ShapeDtypeStruct((width, columns), bf16),
        in_specs=[
            pl.BlockSpec((length, half), lambda i: (0, i)),
            pl.BlockSpec((length, half), lambda i: (0, i)),
            pl.BlockSpec((length, columns), lambda i: (0, 0)),
        ],
        out_specs=pl.BlockSpec((half, columns), lambda i: (i, 0)),
        scratch_shapes=[pltpu.VMEM((half, length), bf16), pltpu.VMEM((half, length), bf16)],
        compiler_params=pltpu.CompilerParams(vmem_limit_bytes=60 * 1024 * 1024),
        cost_estimate=pl.CostEstimate(
            flops=2 * length * width * columns,
            bytes_accessed=2 * (2 * length * width + length * columns + width * columns),
            transcendentals=0,
        ),
        name="ffn_grads",
    )(ffn_in, cot, acts)


def local(
    tokens,
    segments,
    query_weight,
    key_weight,
    value_weight,
    out_weight,
    gate_weight,
    up_weight,
    down_weight,
    attn_gain,
    ffn_gain,
    query_gain,
    key_gain,
    cotangent,
):
    dp = ("x", "z", "c")
    length = segments.shape[0]
    block = length // FOUR
    query_cols = query_weight.shape[1]
    kv_cols = key_weight.shape[1]
    ff_cols = gate_weight.shape[1]
    qkv_cols = query_cols + 2 * kv_cols
    place = jnp.stack([lax.axis_index(axis) for axis in ("x", "z", "c", "y")]).astype(jnp.int32)

    own, other = gather_dp_blocks(pack_columns([query_weight, key_weight, value_weight]))
    large_shard = pack_columns([gate_weight, up_weight, down_weight.T] + gather_y(out_weight.T))
    large_full = lax.all_gather(large_shard, dp, axis=0, tiled=True)
    full_out_t = large_full[:, 3 * ff_cols : 3 * ff_cols + query_cols]

    token_parts = gather_y(jnp.concatenate([tokens, cotangent], axis=0))
    grad_out_all = order_rows(token_parts, block)
    cosine, sine = rope_tables(doc_positions(segments))
    repeats = (query_cols + kv_cols) // HD
    cosine, sine = jnp.tile(cosine, (1, repeats)), jnp.tile(sine, (1, repeats))
    head_gain = jnp.concatenate(
        [query_gain] * (query_cols // HD) + [key_gain] * (kv_cols // HD)
    ).reshape(1, -1)
    tokens_all, full_qkv, normed_t, proj, rot, value, probs, mixed = attention(
        place, block, token_parts, own, other, cosine, sine, segments, attn_gain.reshape(1, -1), head_gain
    )
    middle, ffn_all, acts, *ffn_back, ffn_out = out_ffn(
        gather_y(mixed), tokens_all, large_full, ffn_gain, grad_out_all
    )
    arrived = [ffn_back[0]] + [shift(ffn_back[j], "y", j) for j in (1, 2, 3)]
    ffn_sums, arrived = lax.optimization_barrier((ffn_grads(ffn_all, grad_out_all, acts), arrived))
    grad_ffn_in = sum(part.astype(f32) for part in arrived)
    ffn_part = lax.psum_scatter(ffn_sums, ("x", "c"), scatter_dimension=0, tiled=True)
    ffn_inv = inverse_rms(middle)
    grad_through = norm_back_value(middle, ffn_inv, ffn_gain, grad_ffn_in)
    ffn_gain_part = jnp.sum(grad_ffn_in * middle * ffn_inv, axis=0)
    grad_middle = cotangent.astype(f32) + grad_through
    gm_parts = gather_y(grad_middle.astype(bf16))
    width = tokens.shape[1]
    theirs, mine, *messages, gains = attention_back(
        place, gm_parts, full_out_t, full_qkv, tokens_all, proj, rot, value, probs, cosine, sine,
        head_gain, ffn_gain_part.reshape(1, -1), ffn_out, normed_t, mixed,
    )
    arrived = shift(theirs, "c", 1, 2)
    back_parts = [messages[0]] + [shift(messages[j], "y", j) for j in (1, 2, 3)]
    own_rows, gains, *outgoing = after_core(place, mine, arrived, gains)
    arrived = [shift(part, "z", j + 1) for j, part in enumerate(outgoing)]
    ffn_own, *ffn_pieces = split_z(place, ffn_part)
    ffn_pieces, own_rows = lax.optimization_barrier((ffn_pieces, own_rows))
    ffn_arrived = [shift(part, "z", j + 1) for j, part in enumerate(ffn_pieces)]
    own_rows, gains, *outgoing = after_z(place, own_rows, gains, arrived)
    arrived = [shift(part, "x", j + 1) for j, part in enumerate(outgoing)]
    back_parts, ffn_arrived, arrived = lax.optimization_barrier((back_parts, ffn_arrived, arrived))
    *weight_grads, gains = after_x(
        own_rows, gains, arrived, ffn_own, ffn_arrived,
        (query_cols, kv_cols, kv_cols, query_cols), (ff_cols,) * 3,
    )
    grad_query_weight, grad_key_weight, grad_value_weight, grad_out_t = weight_grads[:4]
    grad_gate_weight, grad_up_weight, grad_down_t = weight_grads[4:]
    grad_out_weight = grad_out_t.T
    grad_down_weight = grad_down_t.T
    gain_grads = last_gains(gather_y(gains), width)

    sums = sum(part.astype(f32) for part in back_parts)
    result = (middle + sums[block:]).astype(bf16)
    own_tokens = tokens.astype(f32)
    grad_input = norm_back_value(own_tokens, inverse_rms(own_tokens), attn_gain, sums[:block])
    grad_tokens = (grad_middle + grad_input).astype(bf16)
    return (
        result,
        grad_tokens,
        grad_query_weight,
        grad_key_weight,
        grad_value_weight,
        grad_out_weight,
        grad_gate_weight,
        grad_up_weight,
        grad_down_weight,
        *[gain.reshape(-1) for gain in gain_grads],
    )


def solution(mesh):
    axes = Mesh(mesh.devices.reshape(4, 4, 2, 4), ("x", "z", "c", "y"))
    dp = ("x", "z", "c")
    rows = P(("x", "z", "c", "y"), None)
    placed = (
        rows,
        P(dp),
        P(dp, "y"),
        P(dp, "y"),
        P(dp, "y"),
        P("y", dp),
        P(dp, "y"),
        P(dp, "y"),
        P("y", dp),
        P(),
        P(),
        P(),
        P(),
        rows,
    )
    return jax.shard_map(
        local,
        mesh=axes,
        in_specs=placed,
        out_specs=(
            rows,
            rows,
            P(dp, "y"),
            P(dp, "y"),
            P(dp, "y"),
            P("y", dp),
            P(dp, "y"),
            P(dp, "y"),
            P("y", dp),
            P(),
            P(),
            P(),
            P(),
        ),
        check_vma=False,
    )
```

```python
import math

import jax
import jax.numpy as jnp
from jax import lax
from jax.experimental import pallas as pl
from jax.experimental.pallas import tpu as pltpu
from jax.sharding import Mesh, PartitionSpec as P

HD = 64
FOUR = 4

epsilon = 1e-05
rope_base = 1000000.0
masked_score = -1e30

bf16 = jnp.bfloat16
f32 = jnp.float32


def dot_nn(left, right):
    return lax.dot_general(left, right, (((1,), (0,)), ((), ())), preferred_element_type=f32)


def dot_nt(left, right):
    return lax.dot_general(left, right, (((1,), (1,)), ((), ())), preferred_element_type=f32)


def dot_tn(left, right):
    return lax.dot_general(left, right, (((0,), (0,)), ((), ())), preferred_element_type=f32)


def inverse_rms(value):
    return lax.rsqrt(jnp.mean(value * value, axis=-1, keepdims=True) + epsilon)


def norm_back_value(value, inverse, norm_gain, incoming):
    scaled = incoming * norm_gain
    average = jnp.mean(value * scaled, axis=-1, keepdims=True)
    return inverse * scaled - value * (inverse * inverse * inverse) * average


def doc_positions(segment_ids):
    length = segment_ids.shape[0]
    indices = jnp.arange(length, dtype=jnp.int32)
    begins = jnp.concatenate([jnp.ones((1,), dtype=jnp.bool_), segment_ids[1:] != segment_ids[:-1]])
    starts = lax.cummax(jnp.where(begins, indices, jnp.zeros_like(indices)), axis=0)
    return indices - starts


def rope_tables(positions):
    half_dim = HD // 2
    exponents = jnp.arange(half_dim, dtype=f32) * (2.0 / HD)
    frequency = jnp.exp(-math.log(rope_base) * exponents)
    angles = positions.astype(f32)[:, None] * frequency[None, :]
    cosine, sine = jnp.cos(angles), jnp.sin(angles)
    return (
        jnp.concatenate([cosine, cosine], axis=1),
        jnp.concatenate([-sine, sine], axis=1),
    )


def shift(value, axis, distance, size=FOUR):
    return lax.ppermute(value, axis, [(i, (i + distance) % size) for i in range(size)])


def gather_y(block):
    return [block] + [shift(block, "y", -j) for j in (1, 2, 3)]


def scatter_sum_y(blocks):
    total = blocks[0].astype(f32)
    for arrived in [shift(blocks[j].astype(bf16), "y", j) for j in (1, 2, 3)]:
        total = total + arrived.astype(f32)
    return total


def mod4(value):
    return lax.rem(value + FOUR, FOUR)


def gather_dp_blocks(shard):
    along_x = jnp.stack([shard] + [shift(shard, "x", -j) for j in (1, 2, 3)])
    along_z = jnp.stack([along_x] + [shift(along_x, "z", -j) for j in (1, 2, 3)])
    return along_z, shift(along_z, "c", 1, 2)


def pack_kernel(*refs):
    out_ref = refs[-1]
    first = 0
    for ref in refs[:-1]:
        out_ref[:, first : first + ref.shape[1]] = ref[...]
        first += ref.shape[1]


def pack_columns(parts):
    vmem = pl.BlockSpec(memory_space=pltpu.VMEM)
    return pl.pallas_call(
        pack_kernel,
        out_shape=jax.ShapeDtypeStruct(
            (parts[0].shape[0], sum(part.shape[1] for part in parts)), parts[0].dtype
        ),
        in_specs=[vmem] * len(parts),
        out_specs=vmem,
        name="pack_columns",
    )(*parts)


def order_rows_kernel(y_ref, part0, part1, part2, part3, out_ref):
    for j, part in enumerate((part0, part1, part2, part3)):
        out_ref[mod4(y_ref[0] + j)] = part[part.shape[0] - out_ref.shape[1] :, :]


def order_rows(parts, rows):
    columns = parts[0].shape[1]
    y = lax.axis_index("y").astype(jnp.int32).reshape(1)
    vmem = pl.BlockSpec(memory_space=pltpu.VMEM)
    return pl.pallas_call(
        order_rows_kernel,
        out_shape=jax.ShapeDtypeStruct((FOUR, rows, columns), parts[0].dtype),
        in_specs=[pl.BlockSpec(memory_space=pltpu.SMEM)] + [vmem] * 4,
        out_specs=vmem,
        compiler_params=pltpu.CompilerParams(vmem_limit_bytes=60 * 1024 * 1024),
        name="order_rows",
    )(y, *parts).reshape(FOUR * rows, columns)


VMEM = pl.BlockSpec(memory_space=pltpu.VMEM)
ANY = pl.BlockSpec(memory_space=pl.ANY)
SMEM = pl.BlockSpec(memory_space=pltpu.SMEM)
shape = jax.ShapeDtypeStruct


def head_mean(value):
    width = value.shape[1]
    row = lax.broadcasted_iota(jnp.int32, (width, width), 0) // HD
    column = lax.broadcasted_iota(jnp.int32, (width, width), 1) // HD
    ones = jnp.where(row == column, 1.0 / HD, 0.0)
    return lax.dot_general(
        value,
        ones,
        (((1,), (0,)), ((), ())),
        precision=lax.Precision.HIGHEST,
        preferred_element_type=f32,
    )


def swap_halves(value):
    width = value.shape[1]
    lane = lax.broadcasted_iota(jnp.int32, value.shape, 1)
    ahead = pltpu.roll(value, width - HD // 2, 1)
    behind = pltpu.roll(value, HD // 2, 1)
    return jnp.where(lane % HD < HD // 2, ahead, behind)


def by_core(turned, target):
    step = 32
    for i in range(turned.shape[0] // step):
        first = (i // 2) * step
        target[i % 2, first : first + step, :] = turned[i * step : (i + 1) * step, :]


def attention_kernel(
    place_ref, tok0, tok1, tok2, tok3, own_ref, other_ref, cos_ref, sin_ref, id_col, id_row,
    gain_ref, head_gain_ref,
    tokens_ref, weights_ref, normed_t_ref, proj_ref, rot_ref, value_ref, probs_ref, mixed_ref,
    normed_ref,
):
    x, z, core, y = place_ref[0], place_ref[1], place_ref[2], place_ref[3]
    length, width = tokens_ref.shape
    block = length // FOUR
    for j, part in enumerate((tok0, tok1, tok2, tok3)):
        rows = pl.ds(pl.multiple_of(mod4(y + j) * block, block), block)
        tokens_ref[rows, :] = part[:block, :]
    for i in range(FOUR):
        for k in range(FOUR):
            from_x, from_z = mod4(i - x), mod4(k - z)
            weights_ref[i, k, core] = own_ref[from_z, from_x]
            weights_ref[i, k, 1 - core] = other_ref[from_z, from_x]
    tokens = tokens_ref[...].astype(f32)
    normed_ref[...] = (tokens * inverse_rms(tokens) * gain_ref[...]).astype(bf16)
    by_core(normed_ref[...].T, normed_t_ref)
    columns = weights_ref.shape[-1]
    projected = dot_nn(normed_ref[...], weights_ref[...].reshape(width, columns))
    heads = proj_ref.shape[1]
    both = projected[:, :heads]
    proj_ref[...] = both
    value_ref[...] = projected[:, heads:].astype(bf16)
    normal = both * lax.rsqrt(head_mean(both * both) + epsilon) * head_gain_ref[...]
    rot_ref[...] = (normal * cos_ref[...] + swap_halves(normal) * sin_ref[...]).astype(bf16)
    query_cols = mixed_ref.shape[1]
    groups = value_ref.shape[1] // HD
    per_group = query_cols // HD // groups
    index = lax.broadcasted_iota(jnp.int32, (length, length), 0)
    other = lax.broadcasted_iota(jnp.int32, (length, length), 1)
    allowed = (index >= other) & (id_col[...] == id_row[...])
    for g in range(groups):
        key = rot_ref[:, query_cols + g * HD : query_cols + (g + 1) * HD]
        value = value_ref[:, g * HD : (g + 1) * HD]
        for h in range(g * per_group, (g + 1) * per_group):
            scores = dot_nt(rot_ref[:, h * HD : (h + 1) * HD], key) * (1.0 / math.sqrt(HD))
            scores = jnp.where(allowed, scores, masked_score)
            exponent = jnp.exp(scores - jnp.max(scores, axis=-1, keepdims=True))
            probs = (exponent * (1.0 / jnp.sum(exponent, axis=-1, keepdims=True))).astype(bf16)
            probs_ref[h] = probs
            mixed_ref[:, h * HD : (h + 1) * HD] = dot_nn(probs, value).astype(bf16)


def attention(place, rows, token_parts, own, other, cos, sin, ids, gain, head_gain):
    width = token_parts[0].shape[1]
    length = FOUR * rows
    heads = head_gain.shape[1]
    columns = own.shape[-1]
    values = columns - heads
    queries = heads - values
    return pl.pallas_call(
        attention_kernel,
        out_shape=(
            shape((length, width), bf16),
            shape((FOUR, FOUR, 2, own.shape[2], columns), bf16),
            shape((2, width // 2, length), bf16),
            shape((length, heads), f32),
            shape((length, heads), bf16),
            shape((length, values), bf16),
            shape((queries // HD, length, length), bf16),
            shape((length, queries), bf16),
        ),
        in_specs=[SMEM] + [VMEM] * 12,
        out_specs=(VMEM,) * 8,
        scratch_shapes=[pltpu.VMEM((length, width), bf16)],
        compiler_params=pltpu.CompilerParams(vmem_limit_bytes=60 * 1024 * 1024),
        cost_estimate=pl.CostEstimate(
            flops=2 * length * (width * columns + 2 * length * queries),
            bytes_accessed=8 * 1024 * 1024,
            transcendentals=length * length * queries // HD,
        ),
        name="attention",
    )(place, *token_parts, own, other, cos, sin, ids.reshape(-1, 1), ids.reshape(1, -1), gain, head_gain)


def attention_back_kernel(
    place_ref, gm0, gm1, gm2, gm3, out_t_ref, weights_hbm, tokens_hbm, proj_ref, rot_ref, value_ref,
    probs_ref, cos_ref, sin_ref, head_gain_ref, ffn_gain_ref, ffn_out_hbm, normed_t_hbm, mixed_ref,
    theirs_ref, mine_ref, message0, message1, message2, message3, gains_ref,
    turned_key, turned_value, grad_rot, gm_ref, grad_ref, gm_t, back_all,
    weights_ref, tokens_ref, ffn_out_ref, normed_t_ref, sems,
):
    late = [
        pltpu.make_async_copy(source, target, sems.at[i])
        for i, (source, target) in enumerate(
            (
                (weights_hbm, weights_ref),
                (tokens_hbm, tokens_ref),
                (ffn_out_hbm, ffn_out_ref),
                (normed_t_hbm, normed_t_ref),
            )
        )
    ]
    for copy in late:
        copy.start()
    y = place_ref[3]
    length, width = tokens_ref.shape
    block = length // FOUR
    heads = proj_ref.shape[1]
    for j, part in enumerate((gm0, gm1, gm2, gm3)):
        rows = pl.ds(pl.multiple_of(mod4(y + j) * block, block), block)
        gm_ref[rows, :] = part[...]
    scale = 1.0 / math.sqrt(HD)
    query_cols = out_t_ref.shape[1]
    groups = value_ref.shape[1] // HD
    per_group = query_cols // HD // groups
    grad_mixed = dot_nn(gm_ref[...], out_t_ref[...]).astype(bf16)
    grad_mixed_t = grad_mixed.T
    query_t = rot_ref[:, :query_cols].T
    for g in range(groups):
        key = rot_ref[:, query_cols + g * HD : query_cols + (g + 1) * HD]
        value = value_ref[:, g * HD : (g + 1) * HD]
        key_sum = jnp.zeros((HD, length), f32)
        value_sum = jnp.zeros((HD, length), f32)
        for h in range(g * per_group, (g + 1) * per_group):
            columns = slice(h * HD, (h + 1) * HD)
            probs = probs_ref[h]
            wide = probs.astype(f32)
            grad_probs = dot_nt(grad_mixed[:, columns], value)
            delta = jnp.sum(wide * grad_probs, axis=-1, keepdims=True)
            grad_scores = (wide * (grad_probs - delta)).astype(bf16)
            grad_rot[:, columns] = dot_nn(grad_scores, key) * scale
            key_sum = key_sum + dot_nn(query_t[columns, :], grad_scores)
            value_sum = value_sum + dot_nn(grad_mixed_t[columns, :], probs)
        turned_key[g * HD : (g + 1) * HD, :] = key_sum * scale
        turned_value[g * HD : (g + 1) * HD, :] = value_sum
    grad_rot[:, query_cols:] = turned_key[...].T
    grad_ref[:, heads:] = turned_value[...].T.astype(bf16)
    incoming = grad_rot[...]
    normal = incoming * cos_ref[...] - swap_halves(incoming) * sin_ref[...]
    both = proj_ref[...]
    inverse = lax.rsqrt(head_mean(both * both) + epsilon)
    scaled = normal * head_gain_ref[...]
    grad = inverse * scaled - both * (inverse * inverse * inverse) * head_mean(both * scaled)
    grad_ref[:, :heads] = grad.astype(bf16)
    head_part = jnp.sum(normal * both * inverse, axis=0, keepdims=True)

    for copy in late:
        copy.wait()
    tokens = tokens_ref[...].astype(f32)
    token_inverse = inverse_rms(tokens)
    weights = weights_ref[...].reshape(width, -1)
    tile = 256
    part = []
    for n in range(width // tile):
        columns = slice(n * tile, (n + 1) * tile)
        back = dot_nt(grad_ref[...], weights[columns, :])
        part.append(jnp.sum(back * (tokens[:, columns] * token_inverse), axis=0, keepdims=True))
        back = back.astype(bf16)
        for i in range(FOUR):
            back_all[mod4(i - y), :, columns] = back[i * block : (i + 1) * block, :]
    for j, ref in enumerate((message0, message1, message2, message3)):
        ref[:block, :] = back_all[j]
        ref[block:, :] = ffn_out_ref[j]
    flat = jnp.concatenate(part + [ffn_gain_ref[...], head_part], axis=1)
    gains_ref[...] = jnp.zeros_like(gains_ref)
    line = gains_ref.shape[1]
    for row in range(-(-flat.shape[1] // line)):
        size = min(line, flat.shape[1] - row * line)
        gains_ref[row : row + 1, :size] = flat[:, row * line : row * line + size]

    core = place_ref[2]
    by_core(gm_ref[...].T, gm_t)
    columns = grad_ref.shape[1]
    for which, ref in ((1 - core, theirs_ref), (core, mine_ref)):
        rows = mine_ref.shape[0]
        ref[:rows, :columns] = dot_nn(normed_t_ref[which], grad_ref[...]).astype(bf16)
        ref[:rows, columns:] = dot_nn(gm_t[which], mixed_ref[...]).astype(bf16)
    theirs_ref[mine_ref.shape[0] :, :] = coded(gains_ref[...])


def attention_back(
    place, gm_parts, out_t, weights, tokens, proj, rot, value, probs, cos, sin, head_gain, ffn_gain_part,
    ffn_out, normed_t, mixed,
):
    length, width = tokens.shape
    heads = proj.shape[1]
    values = value.shape[1]
    line = heads + values + mixed.shape[1]
    return pl.pallas_call(
        attention_back_kernel,
        out_shape=(
            shape((width // 2 + 16, line), bf16),
            shape((width // 2, line), bf16),
        )
        + (shape((length // 2, width), bf16),) * 4
        + (shape((8, line), f32),),
        in_specs=[SMEM] + [VMEM] * 5 + [ANY] * 2 + [VMEM] * 8 + [ANY] * 2 + [VMEM],
        out_specs=(VMEM,) * 7,
        scratch_shapes=[
            pltpu.VMEM((values, length), f32),
            pltpu.VMEM((values, length), f32),
            pltpu.VMEM((length, heads), f32),
            pltpu.VMEM((length, width), bf16),
            pltpu.VMEM((length, heads + values), bf16),
            pltpu.VMEM((2, width // 2, length), bf16),
            pltpu.VMEM((FOUR, length // FOUR, width), bf16),
            pltpu.VMEM(weights.shape, bf16),
            pltpu.VMEM((length, width), bf16),
            pltpu.VMEM(ffn_out.shape, bf16),
            pltpu.VMEM(normed_t.shape, bf16),
            pltpu.SemaphoreType.DMA((4,)),
        ],
        compiler_params=pltpu.CompilerParams(vmem_limit_bytes=60 * 1024 * 1024),
        cost_estimate=pl.CostEstimate(
            flops=10**11,
            bytes_accessed=16 * 1024 * 1024,
            transcendentals=0,
        ),
        name="attention_back",
    )(
        place, *gm_parts, out_t, weights, tokens, proj, rot, value, probs, cos, sin, head_gain,
        ffn_gain_part, ffn_out, normed_t, mixed,
    )


def coded(value):
    high = value.astype(bf16).astype(f32)
    return jnp.concatenate([high, value - high], axis=0).astype(bf16)


def decoded(rows):
    wide = rows.astype(f32)
    return wide[:8] + wide[8:]


def after_core_kernel(
    place_ref, mine_ref, arrived_ref, gains_in,
    own_ref, gains_ref, out1, out2, out3,
):
    z = place_ref[1]
    rows = own_ref.shape[0]
    few = rows // FOUR

    def piece(j):
        parts = []
        for x in range(FOUR):
            at = pl.ds(pl.multiple_of(x * rows + mod4(z + j) * few, few), few)
            parts.append(mine_ref[at, :].astype(f32) + arrived_ref[at, :].astype(f32))
        return jnp.concatenate(parts, axis=0)

    gains = gains_in[...] + decoded(arrived_ref[FOUR * rows :, :])
    gains_ref[...] = gains
    own_ref[...] = piece(0)
    for j, ref in ((1, out1), (2, out2), (3, out3)):
        ref[:rows, :] = piece(j).astype(bf16)
        ref[rows:, :] = coded(gains)


def after_core(place, mine, arrived, gains):
    rows, columns = mine.shape
    rows = rows // FOUR
    return pl.pallas_call(
        after_core_kernel,
        out_shape=(shape((rows, columns), f32), shape((8, columns), f32))
        + (shape((rows + 16, columns), bf16),) * 3,
        in_specs=[SMEM] + [VMEM] * 3,
        out_specs=(VMEM,) * 5,
        compiler_params=pltpu.CompilerParams(vmem_limit_bytes=60 * 1024 * 1024),
        name="after_core",
    )(place, mine, arrived, gains)


def after_z_kernel(
    place_ref, own_in, gains_in, in1, in2, in3, own_ref, gains_ref, out1, out2, out3, total
):
    x = place_ref[0]
    rows = own_in.shape[0]
    value = own_in[...]
    gains = gains_in[...]
    for ref in (in1, in2, in3):
        value = value + ref[:rows, :].astype(f32)
        gains = gains + decoded(ref[rows:, :])
    total[...] = value
    gains_ref[...] = gains
    few = own_ref.shape[0]

    def piece(j):
        return total[pl.ds(pl.multiple_of(mod4(x + j) * few, few), few), :]

    own_ref[...] = piece(0)
    extra = coded(gains)
    for j, ref in ((1, out1), (2, out2), (3, out3)):
        ref[:few, :] = piece(j).astype(bf16)
        ref[few:, :] = extra


def after_z(place, own, gains, arrived):
    rows, columns = own.shape
    few = rows // FOUR
    return pl.pallas_call(
        after_z_kernel,
        out_shape=(shape((few, columns), f32), shape((8, columns), f32))
        + (shape((few + 16, columns), bf16),) * 3,
        in_specs=[SMEM] + [VMEM] * 5,
        out_specs=(VMEM,) * 5,
        scratch_shapes=[pltpu.VMEM((rows, columns), f32)],
        compiler_params=pltpu.CompilerParams(vmem_limit_bytes=60 * 1024 * 1024),
        name="after_z",
    )(place, own, gains, *arrived)


def split_z_kernel(place_ref, part_ref, *refs):
    rows = refs[0].shape[0]
    for j, ref in enumerate(refs):
        at = pl.multiple_of(mod4(place_ref[1] + j) * rows, rows)
        ref[...] = part_ref[pl.ds(at, rows), :]


def split_z(place, part):
    rows, columns = part.shape
    return pl.pallas_call(
        split_z_kernel,
        out_shape=(shape((rows // FOUR, columns), part.dtype),) * 4,
        in_specs=[SMEM, VMEM],
        out_specs=(VMEM,) * 4,
        compiler_params=pltpu.CompilerParams(vmem_limit_bytes=60 * 1024 * 1024),
        name="split_z",
    )(place, part)


def after_x_kernel(own_in, gains_in, in1, in2, in3, ffn_in, ffn1, ffn2, ffn3, *refs):
    rows = own_in.shape[0]
    count = 4
    value = own_in[...]
    gains = gains_in[...]
    for ref in (in1, in2, in3):
        value = value + ref[:rows, :].astype(f32)
        gains = gains + decoded(ref[rows:, :])
    refs[-1][...] = gains
    first = 0
    for ref in refs[:count]:
        ref[...] = value[:, first : first + ref.shape[1]]
        first += ref.shape[1]
    first = 0
    for ref in refs[count:-1]:
        at = slice(first, first + ref.shape[1])
        total = ffn_in[:, at].astype(f32)
        for part in (ffn1, ffn2, ffn3):
            total = total + part[:, at].astype(f32)
        ref[...] = total
        first += ref.shape[1]


def after_x(own, gains, arrived, ffn_own, ffn_arrived, sizes, ffn_sizes):
    rows, columns = own.shape
    return pl.pallas_call(
        after_x_kernel,
        out_shape=tuple(shape((rows, size), f32) for size in sizes + ffn_sizes)
        + (shape(gains.shape, f32),),
        in_specs=[VMEM] * 9,
        out_specs=(VMEM,) * (len(sizes + ffn_sizes) + 1),
        compiler_params=pltpu.CompilerParams(vmem_limit_bytes=60 * 1024 * 1024),
        name="after_x",
    )(own, gains, *arrived, ffn_own, *ffn_arrived)


def last_gains_kernel(part0, part1, part2, part3, attn_ref, ffn_ref, query_ref, key_ref):
    total = part0[...] + part1[...] + part2[...] + part3[...]
    flat = jnp.concatenate([total[row : row + 1, :] for row in range(4)], axis=1)
    width = attn_ref.shape[1]
    attn_ref[...] = flat[:, :width]
    ffn_ref[...] = flat[:, width : 2 * width]
    first = 2 * width
    for ref, heads in ((query_ref, 4), (key_ref, 2)):
        ref[...] = sum(flat[:, first + h * HD : first + (h + 1) * HD] for h in range(heads))
        first += heads * HD


def last_gains(parts, width):
    return pl.pallas_call(
        last_gains_kernel,
        out_shape=(shape((1, width), f32),) * 2 + (shape((1, HD), f32),) * 2,
        in_specs=[VMEM] * 4,
        out_specs=(VMEM,) * 4,
        compiler_params=pltpu.CompilerParams(vmem_limit_bytes=60 * 1024 * 1024),
        name="last_gains",
    )(*parts)


def out_ffn_kernel(
    y_ref, mixed0, mixed1, mixed2, mixed3, tokens_ref, weights_hbm, gain_ref, cot_ref,
    middle_ref, ffn_in_hbm, acts_hbm, back0, back1, back2, back3, out_ref,
    weights, mixed_all, middle_all, back_all, ffn_in_ref, acts_ref, sems, leaving,
):
    length, width = tokens_ref.shape
    ff = acts_ref.shape[1] // 3
    block = length // FOUR
    tile = 256
    whole_tiles = ff // tile
    rest = ff - whole_tiles * tile

    def part(first, size, sem):
        columns = pl.ds(first, size)
        return pltpu.make_async_copy(
            weights_hbm.at[:, columns], weights.at[:, columns], sems.at[sem]
        )

    def tile_parts(i):
        size = tile if i < whole_tiles else rest
        return [part(k * ff + i * tile, size, 3 * i + k) for k in range(3)]

    tiles = whole_tiles + (1 if rest else 0)
    out_part = part(3 * ff, width, 3 * tiles)
    out_part.start()
    for i in range(tiles):
        for copy in tile_parts(i):
            copy.start()

    for j, ref in enumerate((mixed0, mixed1, mixed2, mixed3)):
        cols = ref.shape[1]
        mixed_all[:, j * cols : (j + 1) * cols] = ref[...]
    out_part.wait()

    def out_tile(n, carry):
        columns = pl.ds(pl.multiple_of(n * tile, tile), tile)
        w = weights[columns, 3 * ff : 3 * ff + width]
        middle_all[:, columns] = tokens_ref[:, columns].astype(f32) + dot_nt(mixed_all[...], w)
        return carry

    lax.fori_loop(0, width // tile, out_tile, 0)
    middle = middle_all[...]
    inverse = lax.rsqrt(jnp.mean(middle * middle, axis=-1, keepdims=True) + epsilon)
    ffn_in_ref[...] = (middle * inverse * gain_ref[...]).astype(bf16)
    y = y_ref[0]
    results = [pltpu.make_async_copy(ffn_in_ref, ffn_in_hbm, leaving.at[3 * tiles])]
    results[0].start()
    middle_ref[...] = middle_all[pl.ds(pl.multiple_of(y * block, block), block), :]

    def hidden_tile(first, size):
        def column(k):
            return pl.ds(pl.multiple_of(k * ff + first, 128), size)

        gate = dot_nn(ffn_in_ref[...], weights[:, column(0)])
        up = dot_nn(ffn_in_ref[...], weights[:, column(1)])
        grad_hidden = dot_nn(cot_ref[...], weights[:, column(2)])
        sig = jax.nn.sigmoid(gate)
        silu = gate * sig
        acts_ref[:, column(0)] = (
            grad_hidden * up * sig * (1.0 + gate * (1.0 - sig))
        ).astype(bf16)
        acts_ref[:, column(1)] = (grad_hidden * silu).astype(bf16)
        acts_ref[:, column(2)] = (silu * up).astype(bf16)

    for i in range(tiles):
        for copy in tile_parts(i):
            copy.wait()
        size = tile if i < whole_tiles else rest
        hidden_tile(i * tile, size)
        for k in range(3):
            columns = pl.ds(k * ff + i * tile, size)
            copy = pltpu.make_async_copy(
                acts_ref.at[:, columns], acts_hbm.at[:, columns], leaving.at[3 * i + k]
            )
            copy.start()
            results.append(copy)

    def back_tile(n, carry):
        rows = pl.ds(pl.multiple_of(n * tile, tile), tile)
        back = dot_nt(acts_ref[:, : 2 * ff], weights[rows, : 2 * ff]).astype(bf16)
        for i in range(FOUR):
            back_all[mod4(i - y), :, rows] = back[i * block : (i + 1) * block, :]
        out = dot_nt(acts_ref[:, 2 * ff :], weights[rows, 2 * ff : 3 * ff]).astype(bf16)
        for i in range(FOUR):
            out_ref[mod4(i - y), :, rows] = out[i * block : (i + 1) * block, :]
        return carry

    lax.fori_loop(0, width // tile, back_tile, 0)
    for j, ref in enumerate((back0, back1, back2, back3)):
        ref[...] = back_all[j]
    for copy in results:
        copy.wait()


def out_ffn(mixed_parts, tokens_all, weights, gain, cot):
    length, width = tokens_all.shape
    ff = (weights.shape[1] - width) // 3
    vmem = pl.BlockSpec(memory_space=pltpu.VMEM)
    return pl.pallas_call(
        out_ffn_kernel,
        out_shape=(
            shape((length // FOUR, width), f32),
            shape((length, width), bf16),
            shape((length, 3 * ff), bf16),
        )
        + (shape((length // FOUR, width), bf16),) * 4
        + (shape((FOUR, length // FOUR, width), bf16),),
        in_specs=[pl.BlockSpec(memory_space=pltpu.SMEM)] + [vmem] * 5 + [pl.BlockSpec(memory_space=pl.ANY)] + [vmem] * 2,
        out_specs=(vmem,) + (pl.BlockSpec(memory_space=pl.ANY),) * 2 + (vmem,) * 5,
        scratch_shapes=[
            pltpu.VMEM(weights.shape, bf16),
            pltpu.VMEM((length, width), bf16),
            pltpu.VMEM((length, width), f32),
            pltpu.VMEM((FOUR, length // FOUR, width), bf16),
            pltpu.VMEM((length, width), bf16),
            pltpu.VMEM((length, 3 * ff), bf16),
            pltpu.SemaphoreType.DMA((3 * (-(-ff // 256)) + 1,)),
            pltpu.SemaphoreType.DMA((3 * (-(-ff // 256)) + 1,)),
        ],
        compiler_params=pltpu.CompilerParams(vmem_limit_bytes=60 * 1024 * 1024),
        cost_estimate=pl.CostEstimate(
            flops=2 * length * width * (6 * ff + width),
            bytes_accessed=2 * weights.size + 14 * length * width,
            transcendentals=length * ff,
        ),
        name="out_ffn",
    )(lax.axis_index("y").astype(jnp.int32).reshape(1), *mixed_parts, tokens_all, weights, gain.reshape(1, -1), cot)


def ffn_grads_kernel(ffn_in_ref, cot_ref, acts_ref, grads_ref, in_t, cot_t):
    rows = ffn_in_ref.shape[1]
    ff = acts_ref.shape[1] // 3
    step = 32
    for source, target in ((ffn_in_ref, in_t), (cot_ref, cot_t)):
        turned = source[...].T
        for x in range(rows // (8 * step)):
            for z in range(FOUR):
                for core in range(2):
                    old = ((x * FOUR + z) * 2 + core) * step
                    new = ((x * 2 + core) * FOUR + z) * step
                    target[new : new + step, :] = turned[old : old + step, :]
    tile = 256
    for first in range(0, 3 * ff, tile):
        size = min(tile, 3 * ff - first)
        left = in_t if first < 2 * ff else cot_t
        grads_ref[:, first : first + size] = dot_nn(
            left[...], acts_ref[:, first : first + size]
        ).astype(bf16)


def ffn_grads(ffn_in, cot, acts):
    length, width = ffn_in.shape
    columns = acts.shape[1]
    half = width // 4
    return pl.pallas_call(
        ffn_grads_kernel,
        grid=(4,),
        out_shape=jax.ShapeDtypeStruct((width, columns), bf16),
        in_specs=[
            pl.BlockSpec((length, half), lambda i: (0, i)),
            pl.BlockSpec((length, half), lambda i: (0, i)),
            pl.BlockSpec((length, columns), lambda i: (0, 0)),
        ],
        out_specs=pl.BlockSpec((half, columns), lambda i: (i, 0)),
        scratch_shapes=[pltpu.VMEM((half, length), bf16), pltpu.VMEM((half, length), bf16)],
        compiler_params=pltpu.CompilerParams(vmem_limit_bytes=60 * 1024 * 1024),
        cost_estimate=pl.CostEstimate(
            flops=2 * length * width * columns,
            bytes_accessed=2 * (2 * length * width + length * columns + width * columns),
            transcendentals=0,
        ),
        name="ffn_grads",
    )(ffn_in, cot, acts)


def local(
    tokens,
    segments,
    query_weight,
    key_weight,
    value_weight,
    out_weight,
    gate_weight,
    up_weight,
    down_weight,
    attn_gain,
    ffn_gain,
    query_gain,
    key_gain,
    cotangent,
):
    dp = ("x", "z", "c")
    length = segments.shape[0]
    block = length // FOUR
    query_cols = query_weight.shape[1]
    kv_cols = key_weight.shape[1]
    ff_cols = gate_weight.shape[1]
    qkv_cols = query_cols + 2 * kv_cols
    place = jnp.stack([lax.axis_index(axis) for axis in ("x", "z", "c", "y")]).astype(jnp.int32)

    own, other = gather_dp_blocks(pack_columns([query_weight, key_weight, value_weight]))
    large_shard = pack_columns([gate_weight, up_weight, down_weight.T] + gather_y(out_weight.T))
    large_full = lax.all_gather(large_shard, dp, axis=0, tiled=True)
    full_out_t = large_full[:, 3 * ff_cols : 3 * ff_cols + query_cols]

    token_parts = gather_y(jnp.concatenate([tokens, cotangent], axis=0))
    grad_out_all = order_rows(token_parts, block)
    cosine, sine = rope_tables(doc_positions(segments))
    repeats = (query_cols + kv_cols) // HD
    cosine, sine = jnp.tile(cosine, (1, repeats)), jnp.tile(sine, (1, repeats))
    head_gain = jnp.concatenate(
        [query_gain] * (query_cols // HD) + [key_gain] * (kv_cols // HD)
    ).reshape(1, -1)
    tokens_all, full_qkv, normed_t, proj, rot, value, probs, mixed = attention(
        place, block, token_parts, own, other, cosine, sine, segments, attn_gain.reshape(1, -1), head_gain
    )
    middle, ffn_all, acts, *ffn_back, ffn_out = out_ffn(
        gather_y(mixed), tokens_all, large_full, ffn_gain, grad_out_all
    )
    arrived = [ffn_back[0]] + [shift(ffn_back[j], "y", j) for j in (1, 2, 3)]
    ffn_sums, arrived = lax.optimization_barrier((ffn_grads(ffn_all, grad_out_all, acts), arrived))
    grad_ffn_in = sum(part.astype(f32) for part in arrived)
    ffn_part = lax.psum_scatter(ffn_sums, ("x", "c"), scatter_dimension=0, tiled=True)
    ffn_inv = inverse_rms(middle)
    grad_through = norm_back_value(middle, ffn_inv, ffn_gain, grad_ffn_in)
    ffn_gain_part = jnp.sum(grad_ffn_in * middle * ffn_inv, axis=0)
    grad_middle = cotangent.astype(f32) + grad_through
    gm_parts = gather_y(grad_middle.astype(bf16))
    width = tokens.shape[1]
    theirs, mine, *messages, gains = attention_back(
        place, gm_parts, full_out_t, full_qkv, tokens_all, proj, rot, value, probs, cosine, sine,
        head_gain, ffn_gain_part.reshape(1, -1), ffn_out, normed_t, mixed,
    )
    arrived = shift(theirs, "c", 1, 2)
    back_parts = [messages[0]] + [shift(messages[j], "y", j) for j in (1, 2, 3)]
    own_rows, gains, *outgoing = after_core(place, mine, arrived, gains)
    arrived = [shift(part, "z", j + 1) for j, part in enumerate(outgoing)]
    ffn_own, *ffn_pieces = split_z(place, ffn_part)
    ffn_pieces, own_rows = lax.optimization_barrier((ffn_pieces, own_rows))
    ffn_arrived = [shift(part, "z", j + 1) for j, part in enumerate(ffn_pieces)]
    own_rows, gains, *outgoing = after_z(place, own_rows, gains, arrived)
    arrived = [shift(part, "x", j + 1) for j, part in enumerate(outgoing)]
    back_parts, ffn_arrived, arrived = lax.optimization_barrier((back_parts, ffn_arrived, arrived))
    *weight_grads, gains = after_x(
        own_rows, gains, arrived, ffn_own, ffn_arrived,
        (query_cols, kv_cols, kv_cols, query_cols), (ff_cols,) * 3,
    )
    grad_query_weight, grad_key_weight, grad_value_weight, grad_out_t = weight_grads[:4]
    grad_gate_weight, grad_up_weight, grad_down_t = weight_grads[4:]
    grad_out_weight = grad_out_t.T
    grad_down_weight = grad_down_t.T
    gain_grads = last_gains(gather_y(gains), width)

    sums = sum(part.astype(f32) for part in back_parts)
    result = (middle + sums[block:]).astype(bf16)
    own_tokens = tokens.astype(f32)
    grad_input = norm_back_value(own_tokens, inverse_rms(own_tokens), attn_gain, sums[:block])
    grad_tokens = (grad_middle + grad_input).astype(bf16)
    return (
        result,
        grad_tokens,
        grad_query_weight,
        grad_key_weight,
        grad_value_weight,
        grad_out_weight,
        grad_gate_weight,
        grad_up_weight,
        grad_down_weight,
        *[gain.reshape(-1) for gain in gain_grads],
    )


def solution(mesh):
    axes = Mesh(mesh.devices.reshape(4, 4, 2, 4), ("x", "z", "c", "y"))
    dp = ("x", "z", "c")
    rows = P(("x", "z", "c", "y"), None)
    placed = (
        rows,
        P(dp),
        P(dp, "y"),
        P(dp, "y"),
        P(dp, "y"),
        P("y", dp),
        P(dp, "y"),
        P(dp, "y"),
        P("y", dp),
        P(),
        P(),
        P(),
        P(),
        rows,
    )
    return jax.shard_map(
        local,
        mesh=axes,
        in_specs=placed,
        out_specs=(
            rows,
            rows,
            P(dp, "y"),
            P(dp, "y"),
            P(dp, "y"),
            P("y", dp),
            P(dp, "y"),
            P(dp, "y"),
            P("y", dp),
            P(),
            P(),
            P(),
            P(),
        ),
        check_vma=False,
    )
```
